32 devices in a mesh: dp: 4 (over z), blk: 2 (over x), uly: 4 (over y, core).
Axes of the slice: x: 2, y: 2, z: 4, core: 2. Of those that a mesh axis runs over, the one named last changes fastest.
Arguments:
- tokens: bfloat16 [8, 1024, 768], P('dp', ('blk', 'uly')), may hold values from -6 to 6
- cotangent: bfloat16 [8, 1024, 768], P('dp', ('blk', 'uly')), may hold values from -6 to 6
- segments: int32 [8, 1024], P('dp', ('blk', 'uly')), may hold values from 0 to 1, as said below
- noised: int32 [8, 1024], P('dp', ('blk', 'uly')), may hold values 0 or 1
- levels: int32 [8], P('dp'), may hold values from 0 to 127
- ada_weight: bfloat16 [2, 4608, 128], P(None, 'dp'), may hold values from -0.5 to 0.5
- ada_bias: bfloat16 [2, 4608], P(None, 'dp'), may hold values from -1.75 to 1.75
- first_gain: bfloat16 [2, 768], P(None, 'dp'), may hold values from 0.5 to 1.5
- qkv_weight: bfloat16 [2, 768, 2304], P(None, 'dp'), may hold values from -0.21875 to 0.21875
- out_weight: bfloat16 [2, 768, 768], P(None, 'dp'), may hold values from -4 to 4
- second_gain: bfloat16 [2, 768], P(None, 'dp'), may hold values from 0.5 to 1.5
- hidden_weight: bfloat16 [2, 768, 3072], P(None, 'dp'), may hold values from -0.21875 to 0.21875
- hidden_bias: bfloat16 [2, 3072], P(None, 'dp'), may hold values from -1.75 to 1.75
- down_weight: bfloat16 [2, 3072, 768], P(None, 'dp'), may hold values from -0.109375 to 0.109375
- down_bias: bfloat16 [2, 768], P(None, 'dp'), may hold values from -1.75 to 1.75
Outputs:
- output: bfloat16 [8, 1024, 768], P('dp', ('blk', 'uly'))
- tokens_grad: bfloat16 [8, 1024, 768], P('dp', ('blk', 'uly'))
- ada_weight_grad: float32 [2, 4608, 128], P(None, 'dp')
- ada_bias_grad: float32 [2, 4608], P(None, 'dp')
- first_gain_grad: float32 [2, 768], P(None, 'dp')
- qkv_weight_grad: float32 [2, 768, 2304], P(None, 'dp')
- out_weight_grad: float32 [2, 768, 768], P(None, 'dp')
- second_gain_grad: float32 [2, 768], P(None, 'dp')
- hidden_weight_grad: float32 [2, 768, 3072], P(None, 'dp')
- hidden_bias_grad: float32 [2, 3072], P(None, 'dp')
- down_weight_grad: float32 [2, 3072, 768], P(None, 'dp')
- down_bias_grad: float32 [2, 768], P(None, 'dp')
The draws below stay inside these ranges and needn't reach their ends.
Inputs may be any that keep to these rules, and one draw needn't show every extreme that they name: `segments`: in each group of 2 consecutive rows exactly one row, drawn from the seed, is a single document (ids all 0); every other row is packed: its id at position t is (t + off) // 1024 for an offset off of 1 to 1023 drawn for the row.
All inputs are finite; a program needn't handle non-finite values. No bound on the sum of `noised` on one device may be relied on, other than what follows from the above.
Results may differ from the reference program's by a relative error of at most 0.019.
Values may be sent and summed in bfloat16 or wider, within the bound.
No kernel may reach another device: no remote copies, remote signals or barrier semaphores. Data moves between devices by JAX's collectives and lax.ppermute only.
A program may use at most 256 MiB of HBM per device.

```python
import math
import jax
import jax.numpy as jnp
from jax import lax

D = 768
HEADS = 12
FF = 3072
COND = 128
LAYERS = 2
MB = 2
DOC_LEN = 1024
LEVELS = 128
ROW = 1024
ROWS = 8


def draw_segments(key, part):
    key = jax.random.fold_in(key, 11)
    first_key, second_key = jax.random.split(key)
    groups = ROWS // MB
    single = jax.random.randint(first_key, (groups,), 0, MB)
    offsets = jax.random.randint(second_key, (ROWS, 1), 1, DOC_LEN)
    positions = jnp.arange(ROW, dtype=jnp.int32)[None, :]
    packed = (positions + offsets) // DOC_LEN
    is_single = jnp.arange(ROWS, dtype=jnp.int32) % MB == jnp.repeat(single, MB)
    return jnp.where(is_single[:, None], 0, packed).astype(jnp.int32)


def place_ends(array, stream_key, smallest, top_value):
    shape = array.shape
    index_at = [jax.random.randint(jax.random.fold_in(stream_key, axis), (), 0, shape[axis]) for axis in range(len(shape))]
    array = array.at[tuple(index_at)].set(smallest)
    longest = shape.index(max(shape))
    index_at[longest] = (index_at[longest] + 1) % shape[longest]
    return array.at[tuple(index_at)].set(top_value)


def level_of(own_key, extent, cuts, smallest, top_value):
    gain, own = 1.0, jax.random.fold_in(own_key, 6)
    for axis_at, blocks in cuts:
        heights = jnp.exp(jax.random.uniform(jax.random.fold_in(own, axis_at), (blocks,), jnp.float32, smallest / len(cuts), top_value / len(cuts)))
        gain = gain * jnp.repeat(heights, extent[axis_at] // blocks).reshape([-1 if axis == axis_at else 1 for axis in range(len(extent))])
    return gain


def scatter_about(rng, dims, deviation, most, cuts=(), kind=jnp.bfloat16):
    drawn = deviation * jax.random.normal(rng, dims, jnp.float32)
    if cuts:
        drawn = drawn * level_of(rng, dims, cuts, -0.22, 0.18)
    return jnp.clip(drawn, -most, most).astype(kind)


def setup_inputs(seed: int = 0) -> dict:
    key_list = jax.random.split(jax.random.key(seed), 16)
    tokens = scatter_about(key_list[0], (ROWS, ROW, D), 1.0, 6.0, ((0, 4), (1, 8)))
    cotangent = scatter_about(key_list[1], (ROWS, ROW, D), 1.0, 6.0, ((0, 4), (1, 8)))
    segments = draw_segments(jax.random.fold_in(key_list[15], 71), 0)
    noised = place_ends((jax.random.randint(key_list[3], (ROWS, ROW), 0, 2) < 1).astype(jnp.int32), jax.random.fold_in(key_list[3], 1), 0, 1)
    levels = place_ends(jax.random.randint(key_list[4], (ROWS,), 0, LEVELS), jax.random.fold_in(key_list[4], 1), 0, LEVELS - 1).astype(jnp.int32)
    ada_weight = scatter_about(key_list[5], (LAYERS, 6 * D, COND), COND ** -0.5, 0.5, ((1, 4),))
    ada_bias = scatter_about(key_list[6], (LAYERS, 6 * D), 0.3, 1.75, ((1, 4),))
    first_gain = jnp.clip(1.0 + 0.1 * jax.random.normal(key_list[7], (LAYERS, D), jnp.float32), 0.5, 1.5).astype(jnp.bfloat16)
    qkv_weight = scatter_about(key_list[8], (LAYERS, D, 3 * D), D ** -0.5, 0.21875, ((1, 4),))
    out_weight = scatter_about(key_list[9], (LAYERS, D, D), (max(1, 3 * D // DOC_LEN)) ** -0.5, 4.0, ((1, 4),))
    second_gain = jnp.clip(1.0 + 0.1 * jax.random.normal(key_list[10], (LAYERS, D), jnp.float32), 0.5, 1.5).astype(jnp.bfloat16)
    hidden_weight = scatter_about(key_list[11], (LAYERS, D, FF), D ** -0.5, 0.21875, ((1, 4),))
    hidden_bias = scatter_about(key_list[12], (LAYERS, FF), 0.3, 1.75, ((1, 4),))
    down_weight = scatter_about(key_list[13], (LAYERS, FF, D), FF ** -0.5, 0.109375, ((1, 4),))
    down_bias = scatter_about(key_list[14], (LAYERS, D), 0.3, 1.75, ((1, 4),))
    return dict(tokens=tokens, cotangent=cotangent, segments=segments, noised=noised, levels=levels, ada_weight=ada_weight, ada_bias=ada_bias, first_gain=first_gain, qkv_weight=qkv_weight, out_weight=out_weight, second_gain=second_gain, hidden_weight=hidden_weight, hidden_bias=hidden_bias, down_weight=down_weight, down_bias=down_bias)


epsilon = 1e-05
neg_big = -1e+30
highest = lax.Precision.HIGHEST

@jax.custom_vjp
def low(v):
    return lax.optimization_barrier(v.astype(jnp.bfloat16)).astype(jnp.float32)

@jax.custom_vjp
def low_back(v):
    return v

def low_keep(v):
    return (low(v), None)

def low_pass(kept, grad):
    return (grad,)

def back_keep(v):
    return (v, None)

def back_low(kept, grad):
    return (low(grad),)
low.defvjp(low_keep, low_pass)
low_back.defvjp(back_keep, back_low)

def cond_vector(levels, width):
    half_width = width // 2
    freqs = jnp.exp(-math.log(10000.0) * jnp.arange(half_width, dtype=jnp.float32) / half_width)
    angles = levels.astype(jnp.float32)[:, None] * freqs[None, :]
    return jax.nn.silu(jnp.concatenate([jnp.cos(angles), jnp.sin(angles)], axis=-1))

def norm_mod(values, gain_vec, shift_vec, scale_vec):
    average = lax.optimization_barrier(jnp.mean(values, axis=-1, keepdims=True))
    centered = values - average
    variance = lax.optimization_barrier(jnp.mean(centered * centered, axis=-1, keepdims=True))
    return centered * lax.rsqrt(variance + epsilon) * gain_vec * (1.0 + scale_vec) + shift_vec

def attend_row(queries, keys, values, seg_row):
    allowed = seg_row[:, None] == seg_row[None, :]
    factor = queries.shape[-1] ** (-0.5)

    def one_head(triple):
        head_q, head_k, head_v = triple
        scores = low_back(factor * jnp.dot(head_q, head_k.T, precision=highest))
        probs = jax.nn.softmax(jnp.where(allowed, scores, neg_big), axis=-1)
        return jnp.dot(low(probs), head_v, precision=highest)
    result = lax.map(jax.checkpoint(one_head), (queries.transpose(1, 0, 2), keys.transpose(1, 0, 2), values.transpose(1, 0, 2)))
    return result.transpose(1, 0, 2).reshape(queries.shape[0], -1)

def block_layer(state, seg_row, cond_row, params):
    ada_weight, ada_bias, first_gain, qkv_weight, out_weight, second_gain, hidden_weight, hidden_bias, down_weight, down_bias = params
    modulation = jnp.dot(ada_weight, cond_row, precision=highest) + ada_bias
    shift_one, scale_one, gate_one, shift_two, scale_two, gate_two = jnp.split(modulation, 6)
    normed = low(norm_mod(state, first_gain, shift_one, scale_one))
    qkv = low(low_back(jnp.dot(normed, qkv_weight, precision=highest)))
    tokens_row = state.shape[0]
    pieces = qkv.reshape(tokens_row, 3, HEADS, D // HEADS)
    attended = low(low_back(attend_row(pieces[:, 0], pieces[:, 1], pieces[:, 2], seg_row)))
    branch_one = low_back(jnp.dot(attended, out_weight, precision=highest))
    middle = state + gate_one * branch_one
    normed_two = low(norm_mod(middle, second_gain, shift_two, scale_two))
    hidden_pre = low_back(jnp.dot(normed_two, hidden_weight, precision=highest) + hidden_bias)
    activated = low(jax.nn.gelu(hidden_pre, approximate=True))
    branch_two = low_back(jnp.dot(activated, down_weight, precision=highest) + down_bias)
    return middle + gate_two * branch_two

def forward(inputs, params, segments, conds):

    def row_fn(state, seg_row, cond_row):
        for layer_index in range(LAYERS):
            state = block_layer(state, seg_row, cond_row, tuple((weight[layer_index] for weight in params)))
        return state
    checked = jax.checkpoint(row_fn)

    def scan_step(carry, items):
        return (carry, checked(items[0], items[1], items[2]))
    return lax.scan(scan_step, None, (inputs, segments, conds))[1]

def reference(tokens, cotangent, segments, noised, levels, ada_weight, ada_bias, first_gain, qkv_weight, out_weight, second_gain, hidden_weight, hidden_bias, down_weight, down_bias):
    params = tuple((weight.astype(jnp.float32) for weight in (ada_weight, ada_bias, first_gain, qkv_weight, out_weight, second_gain, hidden_weight, hidden_bias, down_weight, down_bias)))
    conds = low(cond_vector(levels, ada_weight.shape[2]))

    def wrapped(inputs, weights):
        return forward(inputs, weights, segments, conds)
    result, pullback = jax.vjp(wrapped, tokens.astype(jnp.float32), params)
    seed_grad = cotangent.astype(jnp.float32) * noised.astype(jnp.float32)[..., None]
    input_grad, grads = pullback(seed_grad)
    return (result.astype(jnp.bfloat16), input_grad.astype(jnp.bfloat16), grads[0], grads[1], grads[2], grads[3], grads[4], grads[5], grads[6], grads[7], grads[8], grads[9])
```

```python
import math

import jax
import jax.numpy as jnp
from jax import lax
from jax.experimental import pallas as pl
from jax.experimental.pallas import tpu as pltpu
from jax.sharding import PartitionSpec as P

HEADS = 12


epsilon = 1e-05
neg_big = -1e30


def cond_vector(levels, width):
    half_width = width // 2
    freqs = jnp.exp(-math.log(10000.0) * jnp.arange(half_width, dtype=jnp.float32) / half_width)
    angles = levels.astype(jnp.float32)[:, None] * freqs[None, :]
    return jax.nn.silu(jnp.concatenate([jnp.cos(angles), jnp.sin(angles)], axis=-1))


def norm_mod(values, gain_vec, shift_vec, scale_vec):
    average = jnp.mean(values, axis=-1, keepdims=True)
    centered = values - average
    variance = jnp.mean(centered * centered, axis=-1, keepdims=True)
    return centered * lax.rsqrt(variance + epsilon) * gain_vec * (1.0 + scale_vec) + shift_vec


def gelu_tanh(values):
    return jax.nn.gelu(values, approximate=True)


def left_product(first, second):
    return lax.dot_general(
        first, second, (((0,), (0,)), ((), ())), preferred_element_type=jnp.float32
    )


def right_product(first, second):
    return lax.dot_general(
        first, second, (((1,), (1,)), ((), ())), preferred_element_type=jnp.float32
    )


def fetch(params, layer_index):
    p_ada, p_bias, p_gain, p_qkv, p_out, p_gain_two, p_hidden, p_hbias, p_down, p_dbias = params
    return (
        lax.all_gather(p_ada[layer_index], "dp", axis=0, tiled=True),
        lax.all_gather(p_bias[layer_index], "dp", axis=0, tiled=True),
        lax.all_gather(p_gain[layer_index], "dp", axis=0, tiled=True),
        lax.all_gather(p_qkv[layer_index], "dp", axis=0, tiled=True),
        lax.all_gather(p_out[layer_index], "dp", axis=0, tiled=True),
        lax.all_gather(p_gain_two[layer_index], "dp", axis=0, tiled=True),
        lax.all_gather(p_hidden[layer_index], "dp", axis=0, tiled=True),
        lax.all_gather(p_hbias[layer_index], "dp", axis=0, tiled=True),
        lax.all_gather(p_down[layer_index], "dp", axis=0, tiled=True),
        lax.all_gather(p_dbias[layer_index], "dp", axis=0, tiled=True),
    )


def reduce_grads(grads):
    shards = (
        lax.psum_scatter(
            grads[0].astype(jnp.bfloat16), "dp", scatter_dimension=0, tiled=True
        ).astype(jnp.float32),
        lax.psum_scatter(
            grads[1].astype(jnp.bfloat16), "dp", scatter_dimension=0, tiled=True
        ).astype(jnp.float32),
        lax.psum_scatter(
            grads[2].astype(jnp.bfloat16), "dp", scatter_dimension=0, tiled=True
        ).astype(jnp.float32),
        lax.psum_scatter(
            grads[3].astype(jnp.bfloat16), "dp", scatter_dimension=0, tiled=True
        ).astype(jnp.float32),
        lax.psum_scatter(
            grads[4].astype(jnp.bfloat16), "dp", scatter_dimension=0, tiled=True
        ).astype(jnp.float32),
        lax.psum_scatter(
            grads[5].astype(jnp.bfloat16), "dp", scatter_dimension=0, tiled=True
        ).astype(jnp.float32),
        lax.psum_scatter(
            grads[6].astype(jnp.bfloat16), "dp", scatter_dimension=0, tiled=True
        ).astype(jnp.float32),
        lax.psum_scatter(
            grads[7].astype(jnp.bfloat16), "dp", scatter_dimension=0, tiled=True
        ).astype(jnp.float32),
        lax.psum_scatter(
            grads[8].astype(jnp.bfloat16), "dp", scatter_dimension=0, tiled=True
        ).astype(jnp.float32),
        lax.psum_scatter(
            grads[9].astype(jnp.bfloat16), "dp", scatter_dimension=0, tiled=True
        ).astype(jnp.float32),
    )
    return (
        lax.psum(shards[0].astype(jnp.bfloat16), ("blk", "uly")).astype(jnp.float32),
        lax.psum(shards[1].astype(jnp.bfloat16), ("blk", "uly")).astype(jnp.float32),
        lax.psum(shards[2].astype(jnp.bfloat16), ("blk", "uly")).astype(jnp.float32),
        lax.psum(shards[3].astype(jnp.bfloat16), ("blk", "uly")).astype(jnp.float32),
        lax.psum(shards[4].astype(jnp.bfloat16), ("blk", "uly")).astype(jnp.float32),
        lax.psum(shards[5].astype(jnp.bfloat16), ("blk", "uly")).astype(jnp.float32),
        lax.psum(shards[6].astype(jnp.bfloat16), ("blk", "uly")).astype(jnp.float32),
        lax.psum(shards[7].astype(jnp.bfloat16), ("blk", "uly")).astype(jnp.float32),
        lax.psum(shards[8].astype(jnp.bfloat16), ("blk", "uly")).astype(jnp.float32),
        lax.psum(shards[9].astype(jnp.bfloat16), ("blk", "uly")).astype(jnp.float32),
    )


def over_blocks(block_fn, carry, key_piece, value_piece, seg_piece):
    count = key_piece.shape[2]
    size = 512

    def block_step(inner, position):
        offset = position * size
        key_blk = lax.dynamic_slice_in_dim(key_piece, offset, size, 2)
        value_blk = lax.dynamic_slice_in_dim(value_piece, offset, size, 2)
        seg_blk = lax.dynamic_slice_in_dim(seg_piece, offset, size, 0)
        return (block_fn(inner, key_blk, value_blk, seg_blk, offset), None)

    return lax.scan(block_step, carry, jnp.arange(count // size, dtype=jnp.int32))[0]


def split_heads(qkv_b):
    tokens_dev = qkv_b.shape[0]
    width = qkv_b.shape[1] // 3
    heads_all = lax.all_to_all(
        qkv_b.reshape(tokens_dev, 3, width), "uly", split_axis=2, concat_axis=0, tiled=True
    )
    span = heads_all.shape[0]
    head_dim = width // HEADS
    local_heads = heads_all.shape[2] // head_dim
    layout = heads_all.reshape(span, 3, local_heads, head_dim).transpose(1, 2, 3, 0)
    return (layout[0], layout[1], layout[2])


def layer_forward(state, weights_now, cond_b, seg_row):
    (
        ada_weight,
        ada_bias,
        first_gain,
        qkv_weight,
        out_weight,
        second_gain,
        hidden_weight,
        hidden_bias,
        down_weight,
        down_bias,
    ) = weights_now
    modulation = jnp.dot(ada_weight, cond_b, preferred_element_type=jnp.float32) + ada_bias.astype(
        jnp.float32
    )
    shift_one, scale_one, gate_one, shift_two, scale_two, gate_two = jnp.split(modulation, 6)
    normed_b = norm_mod(state, first_gain.astype(jnp.float32), shift_one, scale_one).astype(
        jnp.bfloat16
    )
    qkv_b = jnp.dot(normed_b, qkv_weight, preferred_element_type=jnp.float32).astype(jnp.bfloat16)
    query_t, key_t, value_t = split_heads(qkv_b)
    local_heads, head_dim, span = query_t.shape
    factor = head_dim ** (-0.5)
    query_seg = lax.dynamic_slice_in_dim(seg_row, lax.axis_index("blk") * span, span, 0)

    def forward_block(carry, key_blk, value_blk, seg_blk, start):
        running_max, running_total, weighted = carry
        scores = (
            jnp.einsum("hdq,hdk->hqk", query_t, key_blk, preferred_element_type=jnp.float32)
            * factor
        )
        allowed = (query_seg[:, None] == seg_blk[None, :])[None]
        masked = jnp.where(allowed, scores, neg_big)
        new_max = jnp.maximum(running_max, jnp.max(masked, axis=-1))
        probabilities = jnp.where(allowed, jnp.exp(masked - new_max[..., None]), 0.0)
        rescale = jnp.exp(running_max - new_max)
        running_total = running_total * rescale + jnp.sum(probabilities, axis=-1)
        update = jnp.einsum(
            "hqk,hdk->hdq",
            probabilities.astype(jnp.bfloat16),
            value_blk,
            preferred_element_type=jnp.float32,
        )
        weighted = weighted * rescale[:, None, :] + update
        return (new_max, running_total, weighted)

    initial = (
        jnp.full((local_heads, span), neg_big, jnp.float32),
        jnp.zeros((local_heads, span), jnp.float32),
        jnp.zeros((local_heads, head_dim, span), jnp.float32),
    )
    running_max, running_total, weighted = over_blocks(
        forward_block,
        initial,
        lax.all_gather(key_t, "blk", axis=2, tiled=True),
        lax.all_gather(value_t, "blk", axis=2, tiled=True),
        seg_row,
    )
    attended_heads = weighted / running_total[:, None, :]
    log_total = running_max + jnp.log(running_total)
    sendable = (
        attended_heads.astype(jnp.bfloat16).transpose(2, 0, 1).reshape(span, local_heads * head_dim)
    )
    attended_b = lax.all_to_all(sendable, "uly", split_axis=0, concat_axis=1, tiled=True)
    branch_one = jnp.dot(attended_b, out_weight, preferred_element_type=jnp.float32)
    middle = state + gate_one * branch_one
    normed_two = norm_mod(middle, second_gain.astype(jnp.float32), shift_two, scale_two).astype(
        jnp.bfloat16
    )
    hidden_pre = jnp.dot(
        normed_two, hidden_weight, preferred_element_type=jnp.float32
    ) + hidden_bias.astype(jnp.float32)
    activated = gelu_tanh(hidden_pre).astype(jnp.bfloat16)
    branch_two = jnp.dot(
        activated, down_weight, preferred_element_type=jnp.float32
    ) + down_bias.astype(jnp.float32)
    result = middle + gate_two * branch_two
    kept = (
        state,
        modulation,
        normed_b,
        query_t,
        key_t,
        value_t,
        attended_heads,
        log_total,
        attended_b,
        branch_one,
        middle,
        normed_two,
        hidden_pre,
        activated,
        branch_two,
    )
    return (result, kept)


def layer_backward(grad, weights_now, kept, cond_b, seg_row):
    (
        ada_weight,
        ada_bias,
        first_gain,
        qkv_weight,
        out_weight,
        second_gain,
        hidden_weight,
        hidden_bias,
        down_weight,
        down_bias,
    ) = weights_now
    (
        state,
        modulation,
        normed_b,
        query_t,
        key_t,
        value_t,
        attended_heads,
        log_total,
        attended_b,
        branch_one,
        middle,
        normed_two,
        hidden_pre,
        activated,
        branch_two,
    ) = kept
    shift_one, scale_one, gate_one, shift_two, scale_two, gate_two = jnp.split(modulation, 6)
    gain_one = first_gain.astype(jnp.float32)
    gain_two = second_gain.astype(jnp.float32)
    d_gate_two = jnp.sum(grad * branch_two, axis=0)
    d_branch_two = (gate_two * grad).astype(jnp.bfloat16)
    d_down_weight = left_product(activated, d_branch_two)
    d_down_bias = jnp.sum(d_branch_two.astype(jnp.float32), axis=0)
    d_activated = right_product(d_branch_two, down_weight)
    gelu_back = jax.vjp(gelu_tanh, hidden_pre)[1]
    d_pre = gelu_back(d_activated)[0].astype(jnp.bfloat16)
    d_hidden_weight = left_product(normed_two, d_pre)
    d_hidden_bias = jnp.sum(d_pre.astype(jnp.float32), axis=0)
    d_normed_two = right_product(d_pre, hidden_weight)
    norm_back_two = jax.vjp(norm_mod, middle, gain_two, shift_two, scale_two)[1]
    d_middle_part, d_gain_two, d_shift_two, d_scale_two = norm_back_two(d_normed_two)
    d_middle = grad + d_middle_part
    d_gate_one = jnp.sum(d_middle * branch_one, axis=0)
    d_branch_one = (gate_one * d_middle).astype(jnp.bfloat16)
    d_out_weight = left_product(attended_b, d_branch_one)
    d_attended_b = right_product(d_branch_one, out_weight).astype(jnp.bfloat16)
    local_heads, head_dim, span = query_t.shape
    factor = head_dim ** (-0.5)
    d_heads_t = (
        lax.all_to_all(d_attended_b, "uly", split_axis=1, concat_axis=0, tiled=True)
        .reshape(span, local_heads, head_dim)
        .transpose(1, 2, 0)
    )
    row_delta = jnp.sum(d_heads_t.astype(jnp.float32) * attended_heads, axis=1)
    query_seg = lax.dynamic_slice_in_dim(seg_row, lax.axis_index("blk") * span, span, 0)

    def backward_block(carry, key_blk, value_blk, seg_blk, start):
        d_query, d_key_all, d_value_all = carry
        scores = (
            jnp.einsum("hdq,hdk->hqk", query_t, key_blk, preferred_element_type=jnp.float32)
            * factor
        )
        allowed = (query_seg[:, None] == seg_blk[None, :])[None]
        probabilities = jnp.where(allowed, jnp.exp(scores - log_total[..., None]), 0.0)
        d_probs = jnp.einsum(
            "hdq,hdk->hqk", d_heads_t, value_blk, preferred_element_type=jnp.float32
        )
        d_scores = (probabilities * (d_probs - row_delta[..., None])).astype(jnp.bfloat16)
        d_query = (
            d_query
            + jnp.einsum("hqk,hdk->hdq", d_scores, key_blk, preferred_element_type=jnp.float32)
            * factor
        )
        d_key_new = (
            jnp.einsum("hqk,hdq->hdk", d_scores, query_t, preferred_element_type=jnp.float32)
            * factor
        )
        d_value_new = jnp.einsum(
            "hqk,hdq->hdk",
            probabilities.astype(jnp.bfloat16),
            d_heads_t,
            preferred_element_type=jnp.float32,
        )
        size = key_blk.shape[2]
        d_key_all = lax.dynamic_update_slice_in_dim(
            d_key_all, lax.dynamic_slice_in_dim(d_key_all, start, size, 2) + d_key_new, start, 2
        )
        d_value_all = lax.dynamic_update_slice_in_dim(
            d_value_all,
            lax.dynamic_slice_in_dim(d_value_all, start, size, 2) + d_value_new,
            start,
            2,
        )
        return (d_query, d_key_all, d_value_all)

    row_len = seg_row.shape[0]
    initial = (
        jnp.zeros((local_heads, head_dim, span), jnp.float32),
        jnp.zeros((local_heads, head_dim, row_len), jnp.float32),
        jnp.zeros((local_heads, head_dim, row_len), jnp.float32),
    )
    d_query, d_key_all, d_value_all = over_blocks(
        backward_block,
        initial,
        lax.all_gather(key_t, "blk", axis=2, tiled=True),
        lax.all_gather(value_t, "blk", axis=2, tiled=True),
        seg_row,
    )
    d_key, d_value = (
        lax.psum_scatter(
            d_key_all.astype(jnp.bfloat16), "blk", scatter_dimension=2, tiled=True
        ).astype(jnp.float32),
        lax.psum_scatter(
            d_value_all.astype(jnp.bfloat16), "blk", scatter_dimension=2, tiled=True
        ).astype(jnp.float32),
    )
    joined = jnp.stack([d_query, d_key, d_value], axis=0).astype(jnp.bfloat16)
    stacked = joined.transpose(3, 0, 1, 2).reshape(span, 3, local_heads * head_dim)
    returned = lax.all_to_all(stacked, "uly", split_axis=0, concat_axis=2, tiled=True)
    tokens_dev = state.shape[0]
    d_qkv_b = returned.reshape(tokens_dev, returned.shape[1] * returned.shape[2])
    d_qkv_weight = left_product(normed_b, d_qkv_b)
    d_normed = right_product(d_qkv_b, qkv_weight)
    norm_back_one = jax.vjp(norm_mod, state, gain_one, shift_one, scale_one)[1]
    d_state_part, d_gain_one, d_shift_one, d_scale_one = norm_back_one(d_normed)
    d_state = d_middle + d_state_part
    d_modulation = jnp.concatenate(
        [d_shift_one, d_scale_one, d_gate_one, d_shift_two, d_scale_two, d_gate_two]
    )
    d_ada_weight = d_modulation[:, None] * cond_b.astype(jnp.float32)[None, :]
    grads = (
        d_ada_weight,
        d_modulation,
        d_gain_one,
        d_qkv_weight,
        d_out_weight,
        d_gain_two,
        d_hidden_weight,
        d_hidden_bias,
        d_down_weight,
        d_down_bias,
    )
    return (d_state, grads)


def add_tuples(first, second):
    if first is None:
        return second
    return tuple((left_item + right_item for left_item, right_item in zip(first, second)))


def local(
    tokens,
    cotangent,
    segments,
    noised,
    levels,
    ada_weight,
    ada_bias,
    first_gain,
    qkv_weight,
    out_weight,
    second_gain,
    hidden_weight,
    hidden_bias,
    down_weight,
    down_bias,
):
    params = (
        ada_weight,
        ada_bias,
        first_gain,
        qkv_weight,
        out_weight,
        second_gain,
        hidden_weight,
        hidden_bias,
        down_weight,
        down_bias,
    )
    layers = ada_weight.shape[0]
    batches = tokens.shape[0]
    row_segs = lax.all_gather(segments, ("blk", "uly"), axis=1, tiled=True)
    conds = cond_vector(levels, ada_weight.shape[2]).astype(jnp.bfloat16)
    stored = [fetch(params, layer_index) for layer_index in range(layers)]
    sums = [None] * layers
    outputs = []
    input_grads = []
    for batch_index in range(batches):
        state = tokens[batch_index].astype(jnp.float32)
        cond_b = conds[batch_index]
        seg_row = row_segs[batch_index]
        kept_all = []
        for layer_index in range(layers):
            weights_now = stored[layer_index]
            state, kept = layer_forward(state, weights_now, cond_b, seg_row)
            kept_all.append(kept)
        outputs.append(state.astype(jnp.bfloat16))
        grad = (
            cotangent[batch_index].astype(jnp.float32)
            * noised[batch_index].astype(jnp.float32)[:, None]
        )
        for layer_index in reversed(range(layers)):
            weights_now = stored[layer_index]
            grad, grads = layer_backward(grad, weights_now, kept_all[layer_index], cond_b, seg_row)
            sums[layer_index] = add_tuples(sums[layer_index], reduce_grads(grads))
        input_grads.append(grad.astype(jnp.bfloat16))
    stacked = [
        jnp.stack([sums[layer_index][member] for layer_index in range(layers)])
        for member in range(10)
    ]
    return (
        jnp.stack(outputs),
        jnp.stack(input_grads),
        stacked[0],
        stacked[1],
        stacked[2],
        stacked[3],
        stacked[4],
        stacked[5],
        stacked[6],
        stacked[7],
        stacked[8],
        stacked[9],
    )


SWAP = [(0, 1), (1, 0)]
PAIR = [(0, 1), (1, 0), (2, 3), (3, 2)]
ACROSS = [(0, 2), (2, 0), (1, 3), (3, 1)]


def swap_blk(value):
    return lax.ppermute(value, "blk", SWAP)


def swap_half(value):
    return lax.ppermute(value, "uly", ACROSS)


def swap_core(value):
    return lax.ppermute(value, "uly", PAIR)


def plain_product(first, second):
    return jnp.dot(first, second, preferred_element_type=jnp.float32)


def normalise(values):
    average = jnp.mean(values, axis=-1, keepdims=True)
    centered = values - average
    variance = jnp.mean(centered * centered, axis=-1, keepdims=True)
    inverse = lax.rsqrt(variance + epsilon)
    return centered * inverse, inverse


def pick(array, index, axis):
    return lax.dynamic_index_in_dim(array, index, axis, keepdims=False)


def spread(piece, turn):
    near = swap_half(piece)
    far = swap_blk(piece)
    last = swap_blk(near) if turn else swap_half(far)
    return (piece, near, far, last)


def join_rows(pieces, quarter):
    shards, rows, columns = pieces[0].shape
    whole = jnp.zeros((shards, 4, rows, columns), pieces[0].dtype)
    for relative, piece in enumerate(pieces):
        whole = lax.dynamic_update_slice(whole, piece[:, None], (0, quarter ^ relative, 0, 0))
    return whole.reshape(shards * 4 * rows, columns)


def heads_of(array):
    return array.reshape(array.shape[0], -1, 64)


def attend(query, key, value, query_seg, key_seg):
    scores = jnp.einsum(
        "qhd,khd->hqk", heads_of(query), heads_of(key), preferred_element_type=jnp.float32
    ) * (64**-0.5)
    allowed = (query_seg[:, None] == key_seg[None, :])[None]
    masked = jnp.where(allowed, scores, neg_big)
    top = jnp.max(masked, axis=-1)
    weights = jnp.where(allowed, jnp.exp(masked - top[..., None]), 0.0)
    total = jnp.sum(weights, axis=-1)
    summed = jnp.einsum(
        "hqk,khd->hqd", weights.astype(jnp.bfloat16), heads_of(value), preferred_element_type=jnp.float32
    )
    attended = (summed / total[..., None]).transpose(1, 0, 2).reshape(query.shape)
    return attended, top + jnp.log(total)


def attend_back(query, key, value, query_seg, key_seg, log_total, d_out, delta):
    q_h, k_h, v_h, d_h = heads_of(query), heads_of(key), heads_of(value), heads_of(d_out)
    scores = jnp.einsum("qhd,khd->hqk", q_h, k_h, preferred_element_type=jnp.float32) * (64**-0.5)
    allowed = (query_seg[:, None] == key_seg[None, :])[None]
    probs = jnp.where(allowed, jnp.exp(scores - log_total[..., None]), 0.0)
    d_probs = jnp.einsum("qhd,khd->hqk", d_h, v_h, preferred_element_type=jnp.float32)
    d_scores = (probs * (d_probs - delta[..., None])).astype(jnp.bfloat16)
    d_query = jnp.einsum("hqk,khd->qhd", d_scores, k_h, preferred_element_type=jnp.float32) * (64**-0.5)
    d_key = jnp.einsum("hqk,qhd->khd", d_scores, q_h, preferred_element_type=jnp.float32) * (64**-0.5)
    d_value = jnp.einsum(
        "hqk,qhd->khd", probs.astype(jnp.bfloat16), d_h, preferred_element_type=jnp.float32
    )
    return d_query.reshape(query.shape), d_key.reshape(key.shape), d_value.reshape(value.shape)


def low(value):
    return value.astype(jnp.bfloat16)


def wide(value):
    return value.astype(jnp.float32)


def reduce_pieces(far_pair, near_pair):
    arrived = [swap_blk(term) for term in far_pair]
    kept = [wide(a) + wide(b) for a, b in zip(near_pair, arrived)]
    across = swap_half(low(kept[1]))
    return low(kept[0] + wide(across))


def scatter_shards(array):
    return lax.psum_scatter(array, "dp", scatter_dimension=0, tiled=True)


def local_paired(
    tokens,
    cotangent,
    segments,
    noised,
    levels,
    ada_weight,
    ada_bias,
    first_gain,
    qkv_weight,
    out_weight,
    second_gain,
    hidden_weight,
    hidden_bias,
    down_weight,
    down_bias,
):
    layers, ada_part, cond_width = ada_weight.shape
    part = first_gain.shape[1]
    hidden_part = hidden_bias.shape[1]
    width = tokens.shape[2]
    shards = width // part
    hidden = hidden_part * shards
    half = width // 2
    block = hidden_part // 8
    blk = lax.axis_index("blk")
    place = lax.axis_index("uly")
    core = place % 2
    quarter = blk * 2 + place // 2
    unit = core * 4 + quarter
    shard = lax.axis_index("dp")
    row = shard * 2 + blk

    def exchange(two_rows):
        mine = pick(two_rows, blk, 0)
        arrived = swap_blk(pick(two_rows, 1 - blk, 0))
        return mine, arrived

    start = jnp.concatenate(exchange(tokens), axis=0)
    segs_two = jnp.concatenate(exchange(segments), axis=0)

    def attention_piece(index):
        rows = lax.dynamic_slice(
            qkv_weight[index], (quarter * (part // 4), 0), (part // 4, 3 * width)
        )
        cut = [
            lax.dynamic_slice(rows, (0, kind * width + core * half), (part // 4, half))
            for kind in range(3)
        ]
        cut.append(
            lax.dynamic_slice(
                out_weight[index], (quarter * (part // 4), core * half), (part // 4, half)
            )
        )
        return jnp.concatenate(cut, axis=1)

    def hidden_piece(index):
        cut = hidden_weight[index].reshape(part, shards, 8, block)
        return pick(cut, unit, 2).reshape(part, shards * block)

    def down_piece(index):
        return lax.dynamic_slice(down_weight[index], (unit * block, 0), (block, width))

    gathered = []
    turn = 0
    for index in range(layers):
        attention = lax.all_gather(attention_piece(index), "dp", axis=0, tiled=False)
        hiddens = lax.all_gather(hidden_piece(index), "dp", axis=0, tiled=True)
        downs = lax.all_gather(down_piece(index), "dp", axis=0, tiled=True)
        gathered.append((spread(attention, 0), spread(hiddens, 1), spread(downs, 0)))

    all_levels = lax.all_gather(levels, "dp", axis=0, tiled=True)
    conds = low(cond_vector(all_levels, cond_width))
    rows_all = conds.shape[0]
    shared = []
    for index in range(layers):
        part_mod = right_product(conds, ada_weight[index]) + wide(ada_bias[index])
        shared.append(
            jnp.concatenate(
                [
                    part_mod.reshape(-1),
                    wide(first_gain[index]),
                    wide(second_gain[index]),
                    wide(down_bias[index]),
                    wide(hidden_bias[index]),
                ]
            )
        )
    shared = lax.all_gather(jnp.stack(shared), "dp", axis=0, tiled=False)
    vectors = []
    for index in range(layers):
        table = shared[:, index]
        mods = table[:, : rows_all * ada_part].reshape(shards, rows_all, ada_part)
        modulation = pick(mods, row, 1).reshape(6, width)
        at = rows_all * ada_part
        gain_one = table[:, at : at + part].reshape(-1)
        gain_two = table[:, at + part : at + 2 * part].reshape(-1)
        bias_down = table[:, at + 2 * part : at + 3 * part].reshape(-1)
        bias_hidden = table[:, at + 3 * part :].reshape(shards, 2, 4, block)
        bias_core = pick(bias_hidden, core, 1).transpose(1, 0, 2).reshape(4, shards * block)
        bias_units = [pick(bias_core, quarter ^ relative, 0) for relative in range(4)]
        vectors.append((modulation, gain_one, gain_two, bias_down, bias_units))

    seg_chip = jnp.concatenate([segs_two, swap_core(segs_two)])
    seg_all = jnp.concatenate([seg_chip, swap_half(seg_chip)])

    def both(mine):
        return jnp.concatenate([mine, swap_core(mine)], axis=0)

    def fold(partial):
        count = partial.shape[0] // 2
        return partial[:count] + wide(swap_core(low(partial[count:])))

    def in_order(mine, other, axis):
        return jnp.where(
            core == 0,
            jnp.concatenate([mine, other], axis=axis),
            jnp.concatenate([other, mine], axis=axis),
        )

    state = wide(start)
    kept = []
    for index in range(layers):
        modulation, gain_one, gain_two, bias_down, bias_units = vectors[index]
        shift_one, scale_one, gate_one, shift_two, scale_two, gate_two = modulation
        attention, hiddens, downs = gathered[index]
        joined = join_rows(attention, quarter)
        qkv_core, out_core = joined[:, : 3 * half], joined[:, 3 * half :]
        out_full = in_order(out_core, swap_core(out_core), 1)
        normed = both(
            low(normalise(state)[0] * gain_one * (1.0 + scale_one) + shift_one)
        )
        key_value = low(plain_product(normed, qkv_core[:, half:]))
        key_value_far = swap_half(key_value)
        query = low(plain_product(normed, qkv_core[:, :half]))
        key = jnp.concatenate([key_value[:, :half], key_value_far[:, :half]], axis=0)
        value = jnp.concatenate([key_value[:, half:], key_value_far[:, half:]], axis=0)
        heads_out, log_total = attend(query, key, value, seg_chip, seg_all)
        sendable = low(heads_out)
        count = state.shape[0]
        attended = in_order(sendable[:count], swap_core(sendable[count:]), 1)
        branch_one = plain_product(attended, out_full)
        middle = state + gate_one * branch_one
        normed_two = both(
            low(normalise(middle)[0] * gain_two * (1.0 + scale_two) + shift_two)
        )
        pres, acts = [], []
        partial = 0.0
        for relative in range(4):
            pre = plain_product(normed_two, hiddens[relative]) + bias_units[relative]
            act = low(gelu_tanh(pre))
            partial = partial + plain_product(act, downs[relative])
            pres.append(pre)
            acts.append(act)
        branch_two = fold(partial) + bias_down
        result = middle + gate_two * branch_two
        kept.append(
            (
                state,
                normed,
                qkv_core,
                out_full,
                query,
                key,
                value,
                heads_out,
                log_total,
                attended,
                branch_one,
                middle,
                normed_two,
                pres,
                acts,
                branch_two,
            )
        )
        state = result

    def give_back(rows):
        mine, other = rows[: rows.shape[0] // 2], rows[rows.shape[0] // 2 :]
        arrived = swap_blk(other)
        return jnp.where(blk == 0, jnp.stack([mine, arrived]), jnp.stack([arrived, mine]))

    output = give_back(low(state))

    masked = cotangent * low(noised)[..., None]
    grad = wide(jnp.concatenate(exchange(masked), axis=0))
    small = [None] * layers
    shards_out = [None] * layers
    for index in reversed(range(layers)):
        modulation, gain_one, gain_two, bias_down, bias_units = vectors[index]
        shift_one, scale_one, gate_one, shift_two, scale_two, gate_two = modulation
        attention, hiddens, downs = gathered[index]
        (
            state_in,
            normed,
            qkv_core,
            out_full,
            query,
            key,
            value,
            heads_out,
            log_total,
            attended,
            branch_one,
            middle,
            normed_two,
            pres,
            acts,
            branch_two,
        ) = kept[index]
        count = grad.shape[0]
        d_gate_two = jnp.sum(grad * branch_two, axis=0)
        d_branch_two = low(gate_two * grad)
        d_bias_down = jnp.sum(wide(d_branch_two), axis=0)
        d_branch_chip = both(d_branch_two)
        d_downs, d_hiddens, d_bias_units = [None] * 4, [None] * 4, [None] * 4
        d_normed_two = 0.0
        for relative in (2, 3, 1, 0):
            d_act = right_product(d_branch_chip, downs[relative])
            d_pre = low(jax.vjp(gelu_tanh, pres[relative])[1](d_act)[0])
            d_downs[relative] = low(left_product(acts[relative], d_branch_chip))
            d_hiddens[relative] = low(left_product(normed_two, d_pre))
            d_bias_units[relative] = jnp.sum(wide(d_pre), axis=0)
            d_normed_two = d_normed_two + right_product(d_pre, hiddens[relative])
        d_down_shard = scatter_shards(reduce_pieces(d_downs[2:], d_downs[:2]))
        d_hidden_shard = scatter_shards(reduce_pieces(d_hiddens[2:], d_hiddens[:2]))
        d_normed_two = fold(d_normed_two)

        def norm_back(d_normed, values, gain, scale):
            unit_values, inverse = normalise(values)
            first = jnp.sum(d_normed, axis=0)
            second = jnp.sum(d_normed * unit_values, axis=0)
            scaled = d_normed * ((1.0 + scale) * gain)
            inner = jnp.mean(scaled * unit_values, axis=-1, keepdims=True)
            d_values = (
                scaled - jnp.mean(scaled, axis=-1, keepdims=True) - unit_values * inner
            ) * inverse
            return d_values, first, second

        d_values, sum_two, dot_two = norm_back(d_normed_two, middle, gain_two, scale_two)
        d_middle = grad + d_values
        d_gate_one = jnp.sum(d_middle * branch_one, axis=0)
        d_branch_one = low(gate_one * d_middle)
        d_attended = low(right_product(d_branch_one, out_full))
        d_att_mine = lax.dynamic_slice_in_dim(d_attended, core * half, half, 1)
        d_att_other = lax.dynamic_slice_in_dim(d_attended, (1 - core) * half, half, 1)
        d_heads = jnp.concatenate([d_att_mine, swap_core(d_att_other)], axis=0)
        d_out_other = low(
            left_product(
                attended, lax.dynamic_slice_in_dim(d_branch_one, (1 - core) * half, half, 1)
            )
        )
        d_out_mine = left_product(
            attended, lax.dynamic_slice_in_dim(d_branch_one, core * half, half, 1)
        )
        d_out_core = low(d_out_mine + wide(swap_core(d_out_other)))
        delta = jnp.sum(heads_of(wide(d_heads) * heads_out), axis=-1).T
        local_keys = 2 * count
        _, d_key_far, d_value_far = attend_back(
            query, key[local_keys:], value[local_keys:], seg_chip, seg_all[local_keys:], log_total,
            d_heads, delta,
        )
        d_far = swap_half(low(jnp.concatenate([d_key_far, d_value_far], axis=1)))
        d_query_far = _
        d_query, d_key, d_value = attend_back(
            query, key[:local_keys], value[:local_keys], seg_chip, seg_all[:local_keys], log_total,
            d_heads, delta,
        )
        d_qkv = low(
            jnp.concatenate(
                [
                    d_query + d_query_far,
                    d_key + wide(d_far[:, :half]),
                    d_value + wide(d_far[:, half:]),
                ],
                axis=1,
            )
        )
        d_qkv_core = low(left_product(normed, d_qkv))
        d_attn = jnp.concatenate([d_qkv_core, d_out_core], axis=1).reshape(
            shards, 4, part // 4, 4 * half
        )

        def quarter_of(relative):
            return pick(d_attn, quarter ^ relative, 1)

        d_attn_shard = scatter_shards(
            reduce_pieces(
                [quarter_of(2), quarter_of(3)], [quarter_of(0), quarter_of(1)]
            ).reshape(shards * (part // 4), 4 * half)
        )
        d_normed = fold(right_product(d_qkv, qkv_core))
        d_values, sum_one, dot_one = norm_back(d_normed, state_in, gain_one, scale_one)
        grad = d_middle + d_values
        d_modulation = jnp.concatenate(
            [sum_one, gain_one * dot_one, d_gate_one, sum_two, gain_two * dot_two, d_gate_two]
        )
        d_units = jnp.stack(d_bias_units).reshape(4, shards, block)
        d_units = jnp.stack([pick(d_units, quarter ^ number, 0) for number in range(4)], axis=1)
        d_units = jnp.stack([d_units, jnp.zeros_like(d_units)], axis=1)
        d_units = jnp.where(core == 0, d_units, d_units[:, ::-1])
        small[index] = jnp.concatenate(
            [
                d_modulation.reshape(shards, -1),
                ((1.0 + scale_one) * dot_one).reshape(shards, -1),
                ((1.0 + scale_two) * dot_two).reshape(shards, -1),
                d_bias_down.reshape(shards, -1),
                d_units.reshape(shards, -1),
            ],
            axis=1,
        )
        shards_out[index] = (d_attn_shard, d_hidden_shard, d_down_shard)

    tokens_grad = give_back(low(grad))

    vector = jnp.stack(small)
    vector = vector + swap_core(vector)
    vector = vector + swap_half(vector)
    every = lax.all_gather(vector, ("dp", "blk"), axis=0, tiled=False)
    mine = pick(every, shard, 2)
    totals = jnp.sum(mine, axis=0)
    d_mods = mine[:, :, :ada_part]
    at = ada_part
    grad_gain_one = totals[:, at : at + part]
    grad_gain_two = totals[:, at + part : at + 2 * part]
    grad_bias_down = totals[:, at + 2 * part : at + 3 * part]
    grad_bias_hidden = totals[:, at + 3 * part :]
    grad_ada = jnp.einsum(
        "rlm,rc->lmc", d_mods, wide(conds), precision=lax.Precision.HIGHEST
    )
    grad_ada_bias = totals[:, :ada_part]

    order = [(place_ % 2) * 4 + blk_ * 2 + place_ // 2 for blk_ in range(2) for place_ in range(4)]
    back = [order.index(number) for number in range(8)]
    finals = [[], [], [], []]
    for index in range(layers):
        whole = [
            wide(lax.all_gather(piece, ("blk", "uly"), axis=0, tiled=False))[jnp.array(back)]
            for piece in shards_out[index]
        ]
        attn = whole[0].reshape(2, 4, part // 4, 4, half)
        attn = attn.transpose(1, 2, 3, 0, 4).reshape(part, 4, width)
        finals[0].append(attn[:, :3].reshape(part, 3 * width))
        finals[1].append(attn[:, 3])
        finals[2].append(
            whole[1].reshape(8, part, shards, block).transpose(1, 2, 0, 3).reshape(part, hidden)
        )
        finals[3].append(whole[2].reshape(8 * block, width))
    grad_qkv, grad_out, grad_hidden, grad_down = (jnp.stack(item) for item in finals)
    return (
        output,
        tokens_grad,
        grad_ada,
        grad_ada_bias,
        grad_gain_one,
        grad_qkv,
        grad_out,
        grad_gain_two,
        grad_hidden,
        grad_bias_hidden,
        grad_down,
        grad_bias_down,
    )


def pick_plan(mesh):
    def run(*arrays):
        tokens, ada_weight, first_gain, hidden_bias = (
            arrays[0],
            arrays[5],
            arrays[7],
            arrays[12],
        )
        fits = (
            mesh.shape["blk"] == 2
            and mesh.shape["uly"] == 4
            and tokens.shape[0] == 2
            and tokens.shape[2] // HEADS == 64
            and first_gain.shape[1] % 64 == 0
            and hidden_bias.shape[1] % 128 == 0
        )
        return (local_paired if fits else local)(*arrays)

    return run


def solution(mesh):
    in_specs = (
        P("dp", ("blk", "uly"), None),
        P("dp", ("blk", "uly"), None),
        P("dp", ("blk", "uly")),
        P("dp", ("blk", "uly")),
        P("dp"),
        P(None, "dp", None),
        P(None, "dp"),
        P(None, "dp"),
        P(None, "dp", None),
        P(None, "dp", None),
        P(None, "dp"),
        P(None, "dp", None),
        P(None, "dp"),
        P(None, "dp", None),
        P(None, "dp"),
    )
    out_specs = (
        P("dp", ("blk", "uly"), None),
        P("dp", ("blk", "uly"), None),
        P(None, "dp", None),
        P(None, "dp"),
        P(None, "dp"),
        P(None, "dp", None),
        P(None, "dp", None),
        P(None, "dp"),
        P(None, "dp", None),
        P(None, "dp"),
        P(None, "dp", None),
        P(None, "dp"),
    )
    return jax.shard_map(pick_plan(mesh), mesh=mesh, in_specs=in_specs, out_specs=out_specs, check_vma=False)
```

```python
import math

import jax
import jax.numpy as jnp
from jax import lax
from jax.experimental import pallas as pl
from jax.experimental.pallas import tpu as pltpu
from jax.sharding import PartitionSpec as P

HEADS = 12


epsilon = 1e-05
neg_big = -1e30


def cond_vector(levels, width):
    half_width = width // 2
    freqs = jnp.exp(-math.log(10000.0) * jnp.arange(half_width, dtype=jnp.float32) / half_width)
    angles = levels.astype(jnp.float32)[:, None] * freqs[None, :]
    return jax.nn.silu(jnp.concatenate([jnp.cos(angles), jnp.sin(angles)], axis=-1))


def norm_mod(values, gain_vec, shift_vec, scale_vec):
    average = jnp.mean(values, axis=-1, keepdims=True)
    centered = values - average
    variance = jnp.mean(centered * centered, axis=-1, keepdims=True)
    return centered * lax.rsqrt(variance + epsilon) * gain_vec * (1.0 + scale_vec) + shift_vec


def gelu_tanh(values):
    return jax.nn.gelu(values, approximate=True)


def left_product(first, second):
    return lax.dot_general(
        first, second, (((0,), (0,)), ((), ())), preferred_element_type=jnp.float32
    )


def right_product(first, second):
    return lax.dot_general(
        first, second, (((1,), (1,)), ((), ())), preferred_element_type=jnp.float32
    )


def fetch(params, layer_index):
    p_ada, p_bias, p_gain, p_qkv, p_out, p_gain_two, p_hidden, p_hbias, p_down, p_dbias = params
    return (
        lax.all_gather(p_ada[layer_index], "dp", axis=0, tiled=True),
        lax.all_gather(p_bias[layer_index], "dp", axis=0, tiled=True),
        lax.all_gather(p_gain[layer_index], "dp", axis=0, tiled=True),
        lax.all_gather(p_qkv[layer_index], "dp", axis=0, tiled=True),
        lax.all_gather(p_out[layer_index], "dp", axis=0, tiled=True),
        lax.all_gather(p_gain_two[layer_index], "dp", axis=0, tiled=True),
        lax.all_gather(p_hidden[layer_index], "dp", axis=0, tiled=True),
        lax.all_gather(p_hbias[layer_index], "dp", axis=0, tiled=True),
        lax.all_gather(p_down[layer_index], "dp", axis=0, tiled=True),
        lax.all_gather(p_dbias[layer_index], "dp", axis=0, tiled=True),
    )


def reduce_grads(grads):
    shards = (
        lax.psum_scatter(
            grads[0].astype(jnp.bfloat16), "dp", scatter_dimension=0, tiled=True
        ).astype(jnp.float32),
        lax.psum_scatter(
            grads[1].astype(jnp.bfloat16), "dp", scatter_dimension=0, tiled=True
        ).astype(jnp.float32),
        lax.psum_scatter(
            grads[2].astype(jnp.bfloat16), "dp", scatter_dimension=0, tiled=True
        ).astype(jnp.float32),
        lax.psum_scatter(
            grads[3].astype(jnp.bfloat16), "dp", scatter_dimension=0, tiled=True
        ).astype(jnp.float32),
        lax.psum_scatter(
            grads[4].astype(jnp.bfloat16), "dp", scatter_dimension=0, tiled=True
        ).astype(jnp.float32),
        lax.psum_scatter(
            grads[5].astype(jnp.bfloat16), "dp", scatter_dimension=0, tiled=True
        ).astype(jnp.float32),
        lax.psum_scatter(
            grads[6].astype(jnp.bfloat16), "dp", scatter_dimension=0, tiled=True
        ).astype(jnp.float32),
        lax.psum_scatter(
            grads[7].astype(jnp.bfloat16), "dp", scatter_dimension=0, tiled=True
        ).astype(jnp.float32),
        lax.psum_scatter(
            grads[8].astype(jnp.bfloat16), "dp", scatter_dimension=0, tiled=True
        ).astype(jnp.float32),
        lax.psum_scatter(
            grads[9].astype(jnp.bfloat16), "dp", scatter_dimension=0, tiled=True
        ).astype(jnp.float32),
    )
    return (
        lax.psum(shards[0].astype(jnp.bfloat16), ("blk", "uly")).astype(jnp.float32),
        lax.psum(shards[1].astype(jnp.bfloat16), ("blk", "uly")).astype(jnp.float32),
        lax.psum(shards[2].astype(jnp.bfloat16), ("blk", "uly")).astype(jnp.float32),
        lax.psum(shards[3].astype(jnp.bfloat16), ("blk", "uly")).astype(jnp.float32),
        lax.psum(shards[4].astype(jnp.bfloat16), ("blk", "uly")).astype(jnp.float32),
        lax.psum(shards[5].astype(jnp.bfloat16), ("blk", "uly")).astype(jnp.float32),
        lax.psum(shards[6].astype(jnp.bfloat16), ("blk", "uly")).astype(jnp.float32),
        lax.psum(shards[7].astype(jnp.bfloat16), ("blk", "uly")).astype(jnp.float32),
        lax.psum(shards[8].astype(jnp.bfloat16), ("blk", "uly")).astype(jnp.float32),
        lax.psum(shards[9].astype(jnp.bfloat16), ("blk", "uly")).astype(jnp.float32),
    )


def over_blocks(block_fn, carry, key_piece, value_piece, seg_piece):
    count = key_piece.shape[2]
    size = 512

    def block_step(inner, position):
        offset = position * size
        key_blk = lax.dynamic_slice_in_dim(key_piece, offset, size, 2)
        value_blk = lax.dynamic_slice_in_dim(value_piece, offset, size, 2)
        seg_blk = lax.dynamic_slice_in_dim(seg_piece, offset, size, 0)
        return (block_fn(inner, key_blk, value_blk, seg_blk, offset), None)

    return lax.scan(block_step, carry, jnp.arange(count // size, dtype=jnp.int32))[0]


def split_heads(qkv_b):
    tokens_dev = qkv_b.shape[0]
    width = qkv_b.shape[1] // 3
    heads_all = lax.all_to_all(
        qkv_b.reshape(tokens_dev, 3, width), "uly", split_axis=2, concat_axis=0, tiled=True
    )
    span = heads_all.shape[0]
    head_dim = width // HEADS
    local_heads = heads_all.shape[2] // head_dim
    layout = heads_all.reshape(span, 3, local_heads, head_dim).transpose(1, 2, 3, 0)
    return (layout[0], layout[1], layout[2])


def layer_forward(state, weights_now, cond_b, seg_row):
    (
        ada_weight,
        ada_bias,
        first_gain,
        qkv_weight,
        out_weight,
        second_gain,
        hidden_weight,
        hidden_bias,
        down_weight,
        down_bias,
    ) = weights_now
    modulation = jnp.dot(ada_weight, cond_b, preferred_element_type=jnp.float32) + ada_bias.astype(
        jnp.float32
    )
    shift_one, scale_one, gate_one, shift_two, scale_two, gate_two = jnp.split(modulation, 6)
    normed_b = norm_mod(state, first_gain.astype(jnp.float32), shift_one, scale_one).astype(
        jnp.bfloat16
    )
    qkv_b = jnp.dot(normed_b, qkv_weight, preferred_element_type=jnp.float32).astype(jnp.bfloat16)
    query_t, key_t, value_t = split_heads(qkv_b)
    local_heads, head_dim, span = query_t.shape
    factor = head_dim ** (-0.5)
    query_seg = lax.dynamic_slice_in_dim(seg_row, lax.axis_index("blk") * span, span, 0)

    def forward_block(carry, key_blk, value_blk, seg_blk, start):
        running_max, running_total, weighted = carry
        scores = (
            jnp.einsum("hdq,hdk->hqk", query_t, key_blk, preferred_element_type=jnp.float32)
            * factor
        )
        allowed = (query_seg[:, None] == seg_blk[None, :])[None]
        masked = jnp.where(allowed, scores, neg_big)
        new_max = jnp.maximum(running_max, jnp.max(masked, axis=-1))
        probabilities = jnp.where(allowed, jnp.exp(masked - new_max[..., None]), 0.0)
        rescale = jnp.exp(running_max - new_max)
        running_total = running_total * rescale + jnp.sum(probabilities, axis=-1)
        update = jnp.einsum(
            "hqk,hdk->hdq",
            probabilities.astype(jnp.bfloat16),
            value_blk,
            preferred_element_type=jnp.float32,
        )
        weighted = weighted * rescale[:, None, :] + update
        return (new_max, running_total, weighted)

    initial = (
        jnp.full((local_heads, span), neg_big, jnp.float32),
        jnp.zeros((local_heads, span), jnp.float32),
        jnp.zeros((local_heads, head_dim, span), jnp.float32),
    )
    running_max, running_total, weighted = over_blocks(
        forward_block,
        initial,
        lax.all_gather(key_t, "blk", axis=2, tiled=True),
        lax.all_gather(value_t, "blk", axis=2, tiled=True),
        seg_row,
    )
    attended_heads = weighted / running_total[:, None, :]
    log_total = running_max + jnp.log(running_total)
    sendable = (
        attended_heads.astype(jnp.bfloat16).transpose(2, 0, 1).reshape(span, local_heads * head_dim)
    )
    attended_b = lax.all_to_all(sendable, "uly", split_axis=0, concat_axis=1, tiled=True)
    branch_one = jnp.dot(attended_b, out_weight, preferred_element_type=jnp.float32)
    middle = state + gate_one * branch_one
    normed_two = norm_mod(middle, second_gain.astype(jnp.float32), shift_two, scale_two).astype(
        jnp.bfloat16
    )
    hidden_pre = jnp.dot(
        normed_two, hidden_weight, preferred_element_type=jnp.float32
    ) + hidden_bias.astype(jnp.float32)
    activated = gelu_tanh(hidden_pre).astype(jnp.bfloat16)
    branch_two = jnp.dot(
        activated, down_weight, preferred_element_type=jnp.float32
    ) + down_bias.astype(jnp.float32)
    result = middle + gate_two * branch_two
    kept = (
        state,
        modulation,
        normed_b,
        query_t,
        key_t,
        value_t,
        attended_heads,
        log_total,
        attended_b,
        branch_one,
        middle,
        normed_two,
        hidden_pre,
        activated,
        branch_two,
    )
    return (result, kept)


def layer_backward(grad, weights_now, kept, cond_b, seg_row):
    (
        ada_weight,
        ada_bias,
        first_gain,
        qkv_weight,
        out_weight,
        second_gain,
        hidden_weight,
        hidden_bias,
        down_weight,
        down_bias,
    ) = weights_now
    (
        state,
        modulation,
        normed_b,
        query_t,
        key_t,
        value_t,
        attended_heads,
        log_total,
        attended_b,
        branch_one,
        middle,
        normed_two,
        hidden_pre,
        activated,
        branch_two,
    ) = kept
    shift_one, scale_one, gate_one, shift_two, scale_two, gate_two = jnp.split(modulation, 6)
    gain_one = first_gain.astype(jnp.float32)
    gain_two = second_gain.astype(jnp.float32)
    d_gate_two = jnp.sum(grad * branch_two, axis=0)
    d_branch_two = (gate_two * grad).astype(jnp.bfloat16)
    d_down_weight = left_product(activated, d_branch_two)
    d_down_bias = jnp.sum(d_branch_two.astype(jnp.float32), axis=0)
    d_activated = right_product(d_branch_two, down_weight)
    gelu_back = jax.vjp(gelu_tanh, hidden_pre)[1]
    d_pre = gelu_back(d_activated)[0].astype(jnp.bfloat16)
    d_hidden_weight = left_product(normed_two, d_pre)
    d_hidden_bias = jnp.sum(d_pre.astype(jnp.float32), axis=0)
    d_normed_two = right_product(d_pre, hidden_weight)
    norm_back_two = jax.vjp(norm_mod, middle, gain_two, shift_two, scale_two)[1]
    d_middle_part, d_gain_two, d_shift_two, d_scale_two = norm_back_two(d_normed_two)
    d_middle = grad + d_middle_part
    d_gate_one = jnp.sum(d_middle * branch_one, axis=0)
    d_branch_one = (gate_one * d_middle).astype(jnp.bfloat16)
    d_out_weight = left_product(attended_b, d_branch_one)
    d_attended_b = right_product(d_branch_one, out_weight).astype(jnp.bfloat16)
    local_heads, head_dim, span = query_t.shape
    factor = head_dim ** (-0.5)
    d_heads_t = (
        lax.all_to_all(d_attended_b, "uly", split_axis=1, concat_axis=0, tiled=True)
        .reshape(span, local_heads, head_dim)
        .transpose(1, 2, 0)
    )
    row_delta = jnp.sum(d_heads_t.astype(jnp.float32) * attended_heads, axis=1)
    query_seg = lax.dynamic_slice_in_dim(seg_row, lax.axis_index("blk") * span, span, 0)

    def backward_block(carry, key_blk, value_blk, seg_blk, start):
        d_query, d_key_all, d_value_all = carry
        scores = (
            jnp.einsum("hdq,hdk->hqk", query_t, key_blk, preferred_element_type=jnp.float32)
            * factor
        )
        allowed = (query_seg[:, None] == seg_blk[None, :])[None]
        probabilities = jnp.where(allowed, jnp.exp(scores - log_total[..., None]), 0.0)
        d_probs = jnp.einsum(
            "hdq,hdk->hqk", d_heads_t, value_blk, preferred_element_type=jnp.float32
        )
        d_scores = (probabilities * (d_probs - row_delta[..., None])).astype(jnp.bfloat16)
        d_query = (
            d_query
            + jnp.einsum("hqk,hdk->hdq", d_scores, key_blk, preferred_element_type=jnp.float32)
            * factor
        )
        d_key_new = (
            jnp.einsum("hqk,hdq->hdk", d_scores, query_t, preferred_element_type=jnp.float32)
            * factor
        )
        d_value_new = jnp.einsum(
            "hqk,hdq->hdk",
            probabilities.astype(jnp.bfloat16),
            d_heads_t,
            preferred_element_type=jnp.float32,
        )
        size = key_blk.shape[2]
        d_key_all = lax.dynamic_update_slice_in_dim(
            d_key_all, lax.dynamic_slice_in_dim(d_key_all, start, size, 2) + d_key_new, start, 2
        )
        d_value_all = lax.dynamic_update_slice_in_dim(
            d_value_all,
            lax.dynamic_slice_in_dim(d_value_all, start, size, 2) + d_value_new,
            start,
            2,
        )
        return (d_query, d_key_all, d_value_all)

    row_len = seg_row.shape[0]
    initial = (
        jnp.zeros((local_heads, head_dim, span), jnp.float32),
        jnp.zeros((local_heads, head_dim, row_len), jnp.float32),
        jnp.zeros((local_heads, head_dim, row_len), jnp.float32),
    )
    d_query, d_key_all, d_value_all = over_blocks(
        backward_block,
        initial,
        lax.all_gather(key_t, "blk", axis=2, tiled=True),
        lax.all_gather(value_t, "blk", axis=2, tiled=True),
        seg_row,
    )
    d_key, d_value = (
        lax.psum_scatter(
            d_key_all.astype(jnp.bfloat16), "blk", scatter_dimension=2, tiled=True
        ).astype(jnp.float32),
        lax.psum_scatter(
            d_value_all.astype(jnp.bfloat16), "blk", scatter_dimension=2, tiled=True
        ).astype(jnp.float32),
    )
    joined = jnp.stack([d_query, d_key, d_value], axis=0).astype(jnp.bfloat16)
    stacked = joined.transpose(3, 0, 1, 2).reshape(span, 3, local_heads * head_dim)
    returned = lax.all_to_all(stacked, "uly", split_axis=0, concat_axis=2, tiled=True)
    tokens_dev = state.shape[0]
    d_qkv_b = returned.reshape(tokens_dev, returned.shape[1] * returned.shape[2])
    d_qkv_weight = left_product(normed_b, d_qkv_b)
    d_normed = right_product(d_qkv_b, qkv_weight)
    norm_back_one = jax.vjp(norm_mod, state, gain_one, shift_one, scale_one)[1]
    d_state_part, d_gain_one, d_shift_one, d_scale_one = norm_back_one(d_normed)
    d_state = d_middle + d_state_part
    d_modulation = jnp.concatenate(
        [d_shift_one, d_scale_one, d_gate_one, d_shift_two, d_scale_two, d_gate_two]
    )
    d_ada_weight = d_modulation[:, None] * cond_b.astype(jnp.float32)[None, :]
    grads = (
        d_ada_weight,
        d_modulation,
        d_gain_one,
        d_qkv_weight,
        d_out_weight,
        d_gain_two,
        d_hidden_weight,
        d_hidden_bias,
        d_down_weight,
        d_down_bias,
    )
    return (d_state, grads)


def add_tuples(first, second):
    if first is None:
        return second
    return tuple((left_item + right_item for left_item, right_item in zip(first, second)))


def local(
    tokens,
    cotangent,
    segments,
    noised,
    levels,
    ada_weight,
    ada_bias,
    first_gain,
    qkv_weight,
    out_weight,
    second_gain,
    hidden_weight,
    hidden_bias,
    down_weight,
    down_bias,
):
    params = (
        ada_weight,
        ada_bias,
        first_gain,
        qkv_weight,
        out_weight,
        second_gain,
        hidden_weight,
        hidden_bias,
        down_weight,
        down_bias,
    )
    layers = ada_weight.shape[0]
    batches = tokens.shape[0]
    row_segs = lax.all_gather(segments, ("blk", "uly"), axis=1, tiled=True)
    conds = cond_vector(levels, ada_weight.shape[2]).astype(jnp.bfloat16)
    stored = [fetch(params, layer_index) for layer_index in range(layers)]
    sums = [None] * layers
    outputs = []
    input_grads = []
    for batch_index in range(batches):
        state = tokens[batch_index].astype(jnp.float32)
        cond_b = conds[batch_index]
        seg_row = row_segs[batch_index]
        kept_all = []
        for layer_index in range(layers):
            weights_now = stored[layer_index]
            state, kept = layer_forward(state, weights_now, cond_b, seg_row)
            kept_all.append(kept)
        outputs.append(state.astype(jnp.bfloat16))
        grad = (
            cotangent[batch_index].astype(jnp.float32)
            * noised[batch_index].astype(jnp.float32)[:, None]
        )
        for layer_index in reversed(range(layers)):
            weights_now = stored[layer_index]
            grad, grads = layer_backward(grad, weights_now, kept_all[layer_index], cond_b, seg_row)
            sums[layer_index] = add_tuples(sums[layer_index], reduce_grads(grads))
        input_grads.append(grad.astype(jnp.bfloat16))
    stacked = [
        jnp.stack([sums[layer_index][member] for layer_index in range(layers)])
        for member in range(10)
    ]
    return (
        jnp.stack(outputs),
        jnp.stack(input_grads),
        stacked[0],
        stacked[1],
        stacked[2],
        stacked[3],
        stacked[4],
        stacked[5],
        stacked[6],
        stacked[7],
        stacked[8],
        stacked[9],
    )


SWAP = [(0, 1), (1, 0)]
PAIR = [(0, 1), (1, 0), (2, 3), (3, 2)]
ACROSS = [(0, 2), (2, 0), (1, 3), (3, 1)]
VMEM_BYTES = 48 * 1024 * 1024
FREE = pl.CostEstimate(flops=0, bytes_accessed=0, transcendentals=0)


def swap_blk(value):
    return lax.ppermute(value, "blk", SWAP)


def swap_half(value):
    return lax.ppermute(value, "uly", ACROSS)


def swap_core(value):
    return lax.ppermute(value, "uly", PAIR)


def from_shard(value, back, shards):
    return lax.ppermute(value, "dp", [(at, (at + back) % shards) for at in range(shards)])


def plain_product(first, second):
    return jnp.dot(first, second, preferred_element_type=jnp.float32)


def normalise(values):
    average = jnp.mean(values, axis=-1, keepdims=True)
    centered = values - average
    variance = jnp.mean(centered * centered, axis=-1, keepdims=True)
    inverse = lax.rsqrt(variance + epsilon)
    return centered * inverse, inverse


def pick(array, index, axis):
    return lax.dynamic_index_in_dim(array, index, axis, keepdims=False)


def low(value):
    return value.astype(jnp.bfloat16)


def wide(value):
    return value.astype(jnp.float32)


def run_copies(pairs, sems):
    copies = [
        pltpu.make_async_copy(source, target, sems.at[number])
        for number, (source, target) in enumerate(pairs)
    ]
    for copy in copies:
        copy.start()
    for copy in copies:
        copy.wait()


def cut_kernel(sizes, place_ref, qkv_ref, out_ref, hidden_ref, down_ref, first_ref, second_ref, third_ref, sems):
    rows_in, rows_down, half, hidden_cut, shards = sizes
    quarter, core = place_ref[0], place_ref[1]
    rows = pl.ds(pl.multiple_of(quarter * rows_in, 16), rows_in)
    width = 2 * half
    pairs = []
    for layer in range(qkv_ref.shape[0]):
        attn_ref = first_ref if layer == 0 else third_ref.at[layer - 1, pl.ds(0, rows_in)]
        mlp_ref = second_ref if layer == 0 else third_ref.at[layer - 1, pl.ds(rows_in, 2 * rows_in)]
        lanes = pl.multiple_of(core * half, 128)
        for kind in range(3):
            pairs.append(
                (
                    qkv_ref.at[layer, rows, pl.ds(kind * width + lanes, half)],
                    attn_ref.at[:, pl.ds(kind * half, half)],
                )
            )
        pairs.append((out_ref.at[layer, rows, pl.ds(lanes, half)], attn_ref.at[:, pl.ds(3 * half, half)]))
        lanes = pl.multiple_of(core * hidden_cut, 128)
        for at in range(shards):
            pairs.append(
                (
                    hidden_ref.at[layer, rows, pl.ds(at * 2 * hidden_cut + lanes, hidden_cut)],
                    mlp_ref.at[pl.ds(0, rows_in), pl.ds(at * hidden_cut, hidden_cut)],
                )
            )
        first = pl.multiple_of(core * hidden_cut + quarter * rows_down, 16)
        for side in range(2):
            pairs.append(
                (
                    down_ref.at[layer, pl.ds(first + side * rows_in, rows_in)],
                    mlp_ref.at[pl.ds(rows_in, rows_in), pl.ds(side * width, width)],
                )
            )
    run_copies(pairs, sems)


def cut_pieces(place, sizes, qkv_weight, out_weight, hidden_weight, down_weight):
    rows_in, rows_down, half, hidden_cut, shards = sizes
    layers = qkv_weight.shape[0]
    kind = qkv_weight.dtype
    return pl.pallas_call(
        lambda *refs: cut_kernel(sizes, *refs),
        out_shape=(
            jax.ShapeDtypeStruct((rows_in, 4 * half), kind),
            jax.ShapeDtypeStruct((2 * rows_in, 4 * half), kind),
            jax.ShapeDtypeStruct((layers - 1, 3 * rows_in, 4 * half), kind),
        ),
        in_specs=[pl.BlockSpec(memory_space=pltpu.SMEM)] + [pl.BlockSpec(memory_space=pl.ANY)] * 4,
        out_specs=(pl.BlockSpec(memory_space=pltpu.VMEM),) * 3,
        scratch_shapes=[pltpu.SemaphoreType.DMA((layers * (6 + shards),))],
        compiler_params=pltpu.CompilerParams(vmem_limit_bytes=VMEM_BYTES),
        cost_estimate=FREE,
        name="cut_pieces",
    )(place, qkv_weight, out_weight, hidden_weight, down_weight)


def join_attn_kernel(place_ref, own_ref, near_ref, far_ref, last_ref, *refs):
    whole_ref, sems = refs[-2:]
    quarter = place_ref[0]
    run_copies(
        [
            (piece_ref.at[at], whole_ref.at[at, quarter ^ relative])
            for relative, piece_ref in enumerate((own_ref, near_ref, far_ref, last_ref))
            for at in range(own_ref.shape[0])
        ],
        sems,
    )


def join_mlp_kernel(place_ref, own_ref, near_ref, far_ref, last_h_ref, last_d_ref, *refs):
    hidden_ref, down_ref, sems = refs[-3:]
    quarter = place_ref[0]
    rows = hidden_ref.shape[2]
    width = down_ref.shape[3]
    pairs = []
    for relative, piece_ref in enumerate((own_ref, near_ref, far_ref, None)):
        for at in range(own_ref.shape[0]):
            top = last_h_ref.at[at] if piece_ref is None else piece_ref.at[at, pl.ds(0, rows)]
            pairs.append((top, hidden_ref.at[at, quarter ^ relative]))
            for side in range(2):
                lanes = pl.ds(side * width, width)
                low_part = (
                    last_d_ref.at[at, :, lanes]
                    if piece_ref is None
                    else piece_ref.at[at, pl.ds(rows, rows), lanes]
                )
                pairs.append((low_part, down_ref.at[at, quarter ^ relative, pl.ds(side * rows, rows)]))
    run_copies(pairs, sems)


def join_call(kernel, place, pieces, shapes, after, count, name):
    return pl.pallas_call(
        kernel,
        out_shape=tuple(jax.ShapeDtypeStruct(shape, pieces[0].dtype) for shape in shapes),
        in_specs=[pl.BlockSpec(memory_space=pltpu.SMEM)]
        + [pl.BlockSpec(memory_space=pl.ANY)] * (len(pieces) + len(after)),
        out_specs=(pl.BlockSpec(memory_space=pltpu.VMEM),) * len(shapes),
        scratch_shapes=[pltpu.SemaphoreType.DMA((count,))],
        compiler_params=pltpu.CompilerParams(vmem_limit_bytes=VMEM_BYTES),
        cost_estimate=FREE,
        name=name,
    )(place, *pieces, *after)


def join_attn(place, pieces, after=()):
    shards, rows, columns = pieces[0].shape
    (whole,) = join_call(
        join_attn_kernel, place, pieces, [(shards, 4, rows, columns)], after, 4 * shards, "join_attn"
    )
    return whole.reshape(shards * 4 * rows, columns)


def join_mlp(place, pieces, width, after=()):
    shards, rows, columns = pieces[0].shape
    shapes = [(shards, 4, rows // 2, columns), (shards, 4, rows, width)]
    hiddens, downs = join_call(
        join_mlp_kernel, place, pieces, shapes, after, 12 * shards, "join_mlp"
    )
    return hiddens.reshape(shards * 2 * rows, columns), downs.reshape(shards * 4 * rows, width)


def finish_kernel(half, attn_ref, mlp_ref, *refs):
    qkv_ref, out_ref, hidden_ref, down_ref = refs[-4:]
    rows = attn_ref.shape[2]
    shards = attn_ref.shape[3] // half
    width = 2 * half
    hidden_cut = mlp_ref.shape[3] // shards
    for core in range(2):
        for kind in range(3):
            qkv_ref[0, :, kind * width + core * half : kind * width + (core + 1) * half] = wide(
                attn_ref[0, core, :, kind * half : (kind + 1) * half]
            )
        out_ref[0, :, core * half : (core + 1) * half] = wide(attn_ref[0, core, :, 3 * half :])
        for at in range(shards):
            start = at * 2 * hidden_cut + core * hidden_cut
            hidden_ref[0, :, start : start + hidden_cut] = wide(
                mlp_ref[0, core, :rows, at * hidden_cut : (at + 1) * hidden_cut]
            )
        for side in range(2):
            down_ref[0, core, 0, side * rows : (side + 1) * rows] = wide(
                mlp_ref[0, core, rows:, side * width : (side + 1) * width]
            )


def finish(layer, layers, attn, mlp, half, hidden, before=None):
    _, _, rows, columns = attn.shape
    width = 2 * half
    shapes = (
        (layers, 4 * rows, 3 * width),
        (layers, 4 * rows, width),
        (layers, 4 * rows, hidden),
        (layers, 2, 4, 2 * rows, width),
    )
    operands, specs, aliases = [attn, mlp], [], {}
    specs.append(pl.BlockSpec((1, 2, rows, columns), lambda at: (at, 0, 0, 0)))
    specs.append(pl.BlockSpec((1, 2, 2 * rows, columns), lambda at: (at, 0, 0, 0)))
    if before is not None:
        operands += list(before)
        specs += [pl.BlockSpec(memory_space=pl.ANY)] * 4
        aliases = {2 + number: number for number in range(4)}
    return pl.pallas_call(
        lambda *refs: finish_kernel(half, *refs),
        grid=(4,),
        out_shape=tuple(jax.ShapeDtypeStruct(shape, jnp.float32) for shape in shapes),
        in_specs=specs,
        out_specs=(
            pl.BlockSpec((1, rows, 3 * width), lambda at: (layer, at, 0)),
            pl.BlockSpec((1, rows, width), lambda at: (layer, at, 0)),
            pl.BlockSpec((1, rows, hidden), lambda at: (layer, at, 0)),
            pl.BlockSpec((1, 2, 1, 2 * rows, width), lambda at: (layer, 0, at, 0, 0)),
        ),
        input_output_aliases=aliases,
        compiler_params=pltpu.CompilerParams(vmem_limit_bytes=VMEM_BYTES),
        cost_estimate=FREE,
        name="finish",
    )(*operands)


TILE = 256


def attend_kernel(seg_q_ref, seg_k_ref, q_ref, kl_ref, vl_ref, kf_ref, vf_ref, o_ref, of_ref, lse_ref):
    count = kl_ref.shape[0]
    low_half = lax.broadcasted_iota(jnp.int32, (count, 128), 1) < 64
    for start in range(0, q_ref.shape[0], TILE):
        rows = pl.ds(start, TILE)
        seg_q = seg_q_ref[rows, :]
        allow_l = seg_q == seg_k_ref[:, :count]
        allow_f = seg_q == seg_k_ref[:, count:]
        query = q_ref[rows, :]
        query = query * jnp.asarray(0.125, query.dtype)
        outs, lses = [], []
        for head in range(2):
            half = low_half if head == 0 else jnp.logical_not(low_half)
            q_h = jnp.where(half[:TILE], query, jnp.zeros_like(query))
            s_l = jnp.where(allow_l, right_product(q_h, kl_ref[...]), neg_big)
            s_f = jnp.where(allow_f, right_product(q_h, kf_ref[...]), neg_big)
            top = jnp.maximum(
                jnp.max(s_l, axis=1, keepdims=True), jnp.max(s_f, axis=1, keepdims=True)
            )
            p_l = jnp.exp(s_l - top).astype(jnp.bfloat16)
            p_f = jnp.exp(s_f - top).astype(jnp.bfloat16)
            one = jnp.ones((count, 128), jnp.bfloat16)
            summed = plain_product(p_l, jnp.where(half, vl_ref[...], one)) + plain_product(
                p_f, jnp.where(half, vf_ref[...], one)
            )
            total = pltpu.roll(summed, 64, 1)
            outs.append(summed / total)
            lses.append(top + jnp.log(total))
        result = jnp.where(low_half[:TILE], outs[0], outs[1])
        of_ref[rows, :] = result
        o_ref[rows, :] = result.astype(jnp.bfloat16)
        lse_ref[rows, :] = jnp.where(low_half[:TILE], lses[0], lses[1])


def attend(query, near, far, seg_q, seg_k):
    count, half = query.shape
    pairs = half // 128
    block = lambda off: pl.BlockSpec((count, 128), lambda j: (0, off + j))
    return pl.pallas_call(
        attend_kernel,
        grid=(pairs,),
        out_shape=(
            jax.ShapeDtypeStruct((count, half), jnp.bfloat16),
            jax.ShapeDtypeStruct((count, half), jnp.float32),
            jax.ShapeDtypeStruct((count, half), jnp.float32),
        ),
        in_specs=[
            pl.BlockSpec((count, 1), lambda j: (0, 0)),
            pl.BlockSpec((1, 2 * count), lambda j: (0, 0)),
            block(0),
            block(0),
            block(pairs),
            block(0),
            block(pairs),
        ],
        out_specs=(block(0), block(0), block(0)),
        compiler_params=pltpu.CompilerParams(vmem_limit_bytes=VMEM_BYTES),
        cost_estimate=FREE,
        name="attend",
    )(seg_q, seg_k, query, near, near, far, far)


def back_kernel(has_more, seg_q_ref, seg_k_ref, q_ref, k_ref, v_ref, do_ref, o_ref, lse_ref, *refs):
    count = k_ref.shape[0]
    low_half = lax.broadcasted_iota(jnp.int32, (TILE, 128), 1) < 64
    q_turned = (q_ref[...].astype(jnp.float32) * 0.125).T.astype(jnp.bfloat16)
    do_turned = do_ref[...].astype(jnp.float32).T.astype(jnp.bfloat16)
    d_keys, d_values, d_queries = [0.0, 0.0], [0.0, 0.0], []
    for start in range(0, q_ref.shape[0], TILE):
        rows = pl.ds(start, TILE)
        allow = seg_q_ref[rows, :] == seg_k_ref[...]
        query = q_ref[rows, :]
        query = query * jnp.asarray(0.125, query.dtype)
        d_out = do_ref[rows, :]
        product = d_out.astype(jnp.float32) * o_ref[rows, :]
        d_query = []
        for head in range(2):
            half = low_half if head == 0 else jnp.logical_not(low_half)
            lanes = slice(64 * head, 64 * head + 64)
            q_h = jnp.where(half, query, jnp.zeros_like(query))
            do_h = jnp.where(half, d_out, jnp.zeros_like(d_out))
            scores = jnp.where(allow, right_product(q_h, k_ref[...]), neg_big)
            probs = jnp.exp(scores - lse_ref[rows, 64 * head : 64 * head + 1])
            d_probs = right_product(do_h, v_ref[...])
            delta = jnp.sum(jnp.where(half, product, 0.0), axis=1, keepdims=True)
            d_scores = (probs * (d_probs - delta)).astype(jnp.bfloat16)
            d_values[head] += plain_product(
                do_turned[lanes, start : start + TILE], probs.astype(jnp.bfloat16)
            )
            d_keys[head] += plain_product(q_turned[lanes, start : start + TILE], d_scores)
            d_query.append(plain_product(d_scores, k_ref[...]))
        d_queries.append(jnp.where(low_half, d_query[0], d_query[1]) * 0.125)
    d_key = jnp.concatenate(d_keys, axis=0).T
    d_value = jnp.concatenate(d_values, axis=0).T
    d_query = jnp.concatenate(d_queries, axis=0)
    if has_more:
        dq_more_ref, dk_more_ref, dv_more_ref, out_ref = refs
        half = out_ref.shape[1] // 3
        at = pl.multiple_of(pl.program_id(0) * 128, 128)
        out_ref[:, pl.ds(at, 128)] = (d_query + dq_more_ref[...]).astype(jnp.bfloat16)
        out_ref[:, pl.ds(half + at, 128)] = (d_key + dk_more_ref[...].astype(jnp.float32)).astype(
            jnp.bfloat16
        )
        out_ref[:, pl.ds(2 * half + at, 128)] = (
            d_value + dv_more_ref[...].astype(jnp.float32)
        ).astype(jnp.bfloat16)
    else:
        dq_ref, out_ref = refs
        half = out_ref.shape[1] // 2
        at = pl.multiple_of(pl.program_id(0) * 128, 128)
        dq_ref[...] = d_query
        out_ref[:, pl.ds(at, 128)] = d_key.astype(jnp.bfloat16)
        out_ref[:, pl.ds(half + at, 128)] = d_value.astype(jnp.bfloat16)


def attend_back(query, keys, seg_q, seg_k, d_out, out, lse, more=None):
    count, half = query.shape
    pairs = half // 128
    block = lambda off: pl.BlockSpec((count, 128), lambda j: (0, off + j))
    whole = lambda width: pl.BlockSpec((count, width), lambda j: (0, 0))
    operands = [seg_q, seg_k, query, keys, keys, d_out, out, lse]
    specs = [
        pl.BlockSpec((count, 1), lambda j: (0, 0)),
        pl.BlockSpec((1, count), lambda j: (0, 0)),
        block(0),
        block(0),
        block(pairs),
        block(0),
        block(0),
        block(0),
    ]
    if more is None:
        out_shape = (
            jax.ShapeDtypeStruct((count, half), jnp.float32),
            jax.ShapeDtypeStruct((count, 2 * half), jnp.bfloat16),
        )
        out_specs = (block(0), whole(2 * half))
    else:
        operands += [more[0], more[1], more[1]]
        specs += [block(0), block(0), block(pairs)]
        out_shape = jax.ShapeDtypeStruct((count, 3 * half), jnp.bfloat16)
        out_specs = whole(3 * half)
    return pl.pallas_call(
        lambda *refs: back_kernel(more is not None, *refs),
        grid=(pairs,),
        out_shape=out_shape,
        in_specs=specs,
        out_specs=out_specs,
        compiler_params=pltpu.CompilerParams(vmem_limit_bytes=VMEM_BYTES),
        cost_estimate=FREE,
        name="attend_back",
    )(*operands)


def local_paired(
    tokens,
    cotangent,
    segments,
    noised,
    levels,
    ada_weight,
    ada_bias,
    first_gain,
    qkv_weight,
    out_weight,
    second_gain,
    hidden_weight,
    hidden_bias,
    down_weight,
    down_bias,
):
    layers, ada_part, cond_width = ada_weight.shape
    part = first_gain.shape[1]
    hidden_part = hidden_bias.shape[1]
    width = tokens.shape[2]
    shards = width // part
    hidden = hidden_part * shards
    half = width // 2
    rows_in = part // 4
    rows_down = hidden_part // 8
    hidden_cut = hidden_part // 2
    blk = lax.axis_index("blk")
    uly = lax.axis_index("uly")
    core = uly % 2
    quarter = blk * 2 + uly // 2
    shard = lax.axis_index("dp")
    row = shard * 2 + blk
    place = quarter.reshape(1).astype(jnp.int32)

    def exchange(two_rows):
        return jnp.concatenate(
            [pick(two_rows, blk, 0), swap_blk(pick(two_rows, 1 - blk, 0))], axis=0
        )

    sizes = (rows_in, rows_down, half, hidden_cut, shards)
    attn_first, mlp_first, rest = cut_pieces(
        jnp.stack([quarter, core]).astype(jnp.int32), sizes, qkv_weight, out_weight, hidden_weight, down_weight
    )

    def every_shard_of(piece):
        return lax.all_gather(piece, "dp", axis=0, tiled=False)

    def spread_attn(own):
        near, far = swap_half(own), swap_blk(own)
        return (own, near, far, swap_blk(near))

    def spread_mlp(own):
        near, far = swap_half(own), swap_blk(own)
        return (own, near, far, swap_blk(near[:, :rows_in]), swap_half(far[:, rows_in:]))

    spreads = [(spread_attn(every_shard_of(attn_first)), spread_mlp(every_shard_of(mlp_first)))]
    for index in range(1, layers):
        own = every_shard_of(rest[index - 1])
        spreads.append((spread_attn(own[:, :rows_in]), spread_mlp(own[:, rows_in:])))

    start = exchange(tokens)
    segs_two = exchange(segments)

    def every_shard(vector):
        arrived = [vector] + [from_shard(vector, back, shards) for back in range(1, shards)]
        table = jnp.stack(arrived)
        return jnp.stack([pick(table, (shard + shards - at) % shards, 0) for at in range(shards)])

    all_levels = every_shard(levels).reshape(-1)
    conds = low(cond_vector(all_levels, cond_width))
    rows_all = conds.shape[0]
    shared = []
    for index in range(layers):
        part_mod = right_product(conds, ada_weight[index]) + wide(ada_bias[index])
        shared.append(
            jnp.concatenate(
                [
                    part_mod.reshape(-1),
                    wide(first_gain[index]),
                    wide(second_gain[index]),
                    wide(down_bias[index]),
                    wide(hidden_bias[index]),
                ]
            )
        )
    shared = every_shard(jnp.stack(shared))
    vectors = []
    for index in range(layers):
        table = shared[:, index]
        mods = table[:, : rows_all * ada_part].reshape(shards, rows_all, ada_part)
        modulation = pick(mods, row, 1).reshape(6, width)
        at = rows_all * ada_part
        gain_one = table[:, at : at + part].reshape(-1)
        gain_two = table[:, at + part : at + 2 * part].reshape(-1)
        bias_down = table[:, at + 2 * part : at + 3 * part].reshape(-1)
        bias_hidden = table[:, at + 3 * part :].reshape(shards, 2, hidden_cut)
        bias_core = pick(bias_hidden, core, 1).reshape(-1)
        vectors.append((modulation, gain_one, gain_two, bias_down, bias_core))

    seg_chip = jnp.concatenate([segs_two, swap_core(segs_two)])
    seg_far = swap_half(seg_chip)
    seg_q = seg_chip[:, None]
    seg_near_k, seg_far_k = seg_chip[None, :], seg_far[None, :]
    seg_k = jnp.concatenate([seg_near_k, seg_far_k], axis=1)

    gathered = []
    for index in range(layers):
        attn, mlp = spreads[index]
        gathered.append((join_attn(place, attn), *join_mlp(place, mlp, width)))

    def both(mine):
        return jnp.concatenate([mine, swap_core(mine)], axis=0)

    def fold(partial):
        count = partial.shape[0] // 2
        return partial[:count] + wide(swap_core(low(partial[count:])))

    def in_order(mine, other, axis):
        return jnp.where(
            core == 0,
            jnp.concatenate([mine, other], axis=axis),
            jnp.concatenate([other, mine], axis=axis),
        )

    state = wide(start)
    kept = []
    for index in range(layers):
        modulation, gain_one, gain_two, bias_down, bias_core = vectors[index]
        shift_one, scale_one, gate_one, shift_two, scale_two, gate_two = modulation
        joined, hiddens, downs = gathered[index]
        qkv_core, out_core = joined[:, : 3 * half], joined[:, 3 * half :]
        out_full = in_order(out_core, swap_core(out_core), 1)
        normed = both(
            low(normalise(state)[0] * gain_one * (1.0 + scale_one) + shift_one)
        )
        near = low(plain_product(normed, qkv_core[:, half:]))
        far = swap_half(near)
        query = low(plain_product(normed, qkv_core[:, :half]))
        sendable, heads_out, lse = attend(query, near, far, seg_q, seg_k)
        count = state.shape[0]
        attended = in_order(sendable[:count], swap_core(sendable[count:]), 1)
        branch_one = plain_product(attended, out_full)
        middle = state + gate_one * branch_one
        normed_two = both(
            low(normalise(middle)[0] * gain_two * (1.0 + scale_two) + shift_two)
        )
        pre = plain_product(normed_two, hiddens) + bias_core
        act = low(gelu_tanh(pre))
        branch_two = fold(plain_product(act, downs)) + bias_down
        result = middle + gate_two * branch_two
        kept.append(
            (
                state,
                normed,
                qkv_core,
                out_full,
                query,
                near,
                far,
                heads_out,
                lse,
                attended,
                branch_one,
                middle,
                normed_two,
                pre,
                act,
                branch_two,
            )
        )
        state = result

    def give_back(rows):
        mine, other = rows[: rows.shape[0] // 2], rows[rows.shape[0] // 2 :]
        arrived = swap_blk(other)
        return jnp.where(blk == 0, jnp.stack([mine, arrived]), jnp.stack([arrived, mine]))

    output = give_back(low(state))

    def reduce_plane(array, rows, first_blk):
        terms = array.reshape(shards, 2, 2, rows, array.shape[1])
        if first_blk:
            sent = swap_blk(pick(terms, 1 - blk, 1))
            kept_terms = low(wide(pick(terms, blk, 1)) + wide(sent))
            sent = swap_half(pick(kept_terms, 1 - uly // 2, 1))
            mine = pick(kept_terms, uly // 2, 1)
        else:
            sent = swap_half(pick(terms, 1 - uly // 2, 2))
            kept_terms = low(wide(pick(terms, uly // 2, 2)) + wide(sent))
            sent = swap_blk(pick(kept_terms, 1 - blk, 1))
            mine = pick(kept_terms, blk, 1)
        return low(wide(mine) + wide(sent))

    def scatter_shards(array):
        return lax.psum_scatter(array, "dp", scatter_dimension=0, tiled=False)

    def norm_back(d_normed, values, gain, scale):
        unit_values, inverse = normalise(values)
        first = jnp.sum(d_normed, axis=0)
        second = jnp.sum(d_normed * unit_values, axis=0)
        scaled = d_normed * ((1.0 + scale) * gain)
        inner = jnp.mean(scaled * unit_values, axis=-1, keepdims=True)
        d_values = (
            scaled - jnp.mean(scaled, axis=-1, keepdims=True) - unit_values * inner
        ) * inverse
        return d_values, first, second

    masked = cotangent * low(noised)[..., None]
    grad = wide(exchange(masked))
    small = [None] * layers
    shards_out = [None] * layers
    for index in reversed(range(layers)):
        modulation, gain_one, gain_two, bias_down, bias_core = vectors[index]
        shift_one, scale_one, gate_one, shift_two, scale_two, gate_two = modulation
        joined, hiddens, downs = gathered[index]
        (
            state_in,
            normed,
            qkv_core,
            out_full,
            query,
            near,
            far,
            heads_out,
            lse,
            attended,
            branch_one,
            middle,
            normed_two,
            pre,
            act,
            branch_two,
        ) = kept[index]
        d_gate_two = jnp.sum(grad * branch_two, axis=0)
        d_branch_two = low(gate_two * grad)
        d_bias_down = jnp.sum(wide(d_branch_two), axis=0)
        d_branch_chip = both(d_branch_two)
        d_act = right_product(d_branch_chip, downs)
        d_pre = low(jax.vjp(gelu_tanh, pre)[1](d_act)[0])
        d_down = low(left_product(act, d_branch_chip))
        d_hidden = low(left_product(normed_two, d_pre))
        down_sum = reduce_plane(d_down, rows_down, True)
        hidden_sum = reduce_plane(d_hidden, rows_in, False)
        down_sum = jnp.concatenate([down_sum[:, :rows_in], down_sum[:, rows_in:]], axis=2)
        d_mlp_shard = scatter_shards(jnp.concatenate([hidden_sum, down_sum], axis=1))
        d_bias_core = jnp.sum(wide(d_pre), axis=0)
        d_normed_two = fold(right_product(d_pre, hiddens))
        d_values, sum_two, dot_two = norm_back(d_normed_two, middle, gain_two, scale_two)
        d_middle = grad + d_values
        d_gate_one = jnp.sum(d_middle * branch_one, axis=0)
        d_branch_one = low(gate_one * d_middle)
        d_attended = low(right_product(d_branch_one, out_full))
        d_att_mine = lax.dynamic_slice_in_dim(d_attended, core * half, half, 1)
        d_att_other = lax.dynamic_slice_in_dim(d_attended, (1 - core) * half, half, 1)
        d_heads = jnp.concatenate([d_att_mine, swap_core(d_att_other)], axis=0)
        d_out_other = low(
            left_product(
                attended, lax.dynamic_slice_in_dim(d_branch_one, (1 - core) * half, half, 1)
            )
        )
        d_out_mine = left_product(
            attended, lax.dynamic_slice_in_dim(d_branch_one, core * half, half, 1)
        )
        d_out_core = low(d_out_mine + wide(swap_core(d_out_other)))
        d_query_far, d_far = attend_back(
            query, far, seg_q, seg_far_k, d_heads, heads_out, lse
        )
        d_near = swap_half(d_far)
        d_qkv = attend_back(
            query, near, seg_q, seg_near_k, d_heads, heads_out, lse, (d_query_far, d_near)
        )
        d_qkv_core = low(left_product(normed, d_qkv))
        d_attn = jnp.concatenate([d_qkv_core, d_out_core], axis=1)
        d_attn_shard = scatter_shards(reduce_plane(d_attn, rows_in, True))
        d_normed = fold(right_product(d_qkv, qkv_core))
        d_values, sum_one, dot_one = norm_back(d_normed, state_in, gain_one, scale_one)
        grad = d_middle + d_values
        d_modulation = jnp.concatenate(
            [sum_one, gain_one * dot_one, d_gate_one, sum_two, gain_two * dot_two, d_gate_two]
        )
        d_units = d_bias_core.reshape(shards, 1, hidden_cut)
        d_units = jnp.concatenate(
            [jnp.where(core == 0, d_units, 0.0), jnp.where(core == 1, d_units, 0.0)], axis=1
        )
        small[index] = jnp.concatenate(
            [
                d_modulation.reshape(shards, -1),
                ((1.0 + scale_one) * dot_one).reshape(shards, -1),
                ((1.0 + scale_two) * dot_two).reshape(shards, -1),
                d_bias_down.reshape(shards, -1),
                d_units.reshape(shards, -1),
            ],
            axis=1,
        )
        shards_out[index] = (d_attn_shard, d_mlp_shard)

    tokens_grad = give_back(low(grad))

    def small_sums(vector):
        vector = vector + swap_core(vector)
        vector = vector + swap_half(vector)
        rest = vector[:, ada_part:]
        other = swap_blk(vector)
        two = jnp.concatenate(
            [
                jnp.where(blk == 0, vector[:, :ada_part], other[:, :ada_part]),
                jnp.where(blk == 0, other[:, :ada_part], vector[:, :ada_part]),
                rest + other[:, ada_part:],
            ],
            axis=1,
        )
        arrived = [pick(two, shard, 0)]
        for ahead in range(1, shards):
            arrived.append(from_shard(pick(two, (shard + ahead) % shards, 0), ahead, shards))
        arrived = jnp.stack(arrived)
        totals = jnp.sum(arrived, axis=0)
        by_row = arrived[:, : 2 * ada_part].reshape(shards, 2, ada_part)
        sources = (shard + shards - jnp.arange(shards)) % shards
        cond_rows = wide(conds).reshape(shards, 2, cond_width)[sources]
        grad_ada = jnp.einsum(
            "srm,src->mc", by_row, cond_rows, precision=lax.Precision.HIGHEST
        )
        return (
            grad_ada,
            totals[:ada_part] + totals[ada_part : 2 * ada_part],
            totals[2 * ada_part : 2 * ada_part + part],
            totals[2 * ada_part + part : 2 * ada_part + 2 * part],
            totals[2 * ada_part + 2 * part : 2 * ada_part + 3 * part],
            totals[2 * ada_part + 3 * part :],
        )

    grad_ada, grad_ada_bias, grad_gain_one, grad_gain_two, grad_bias_down, grad_bias_hidden = (
        jnp.stack(item) for item in zip(*[small_sums(small[index]) for index in range(layers)])
    )

    def every_piece(piece):
        whole = lax.all_gather(piece, ("blk", "uly"), axis=0, tiled=False)
        return whole.reshape(4, 2, piece.shape[0], piece.shape[1])

    grads = None
    for index in reversed(range(layers)):
        if index > 0:
            whole = every_piece(jnp.concatenate(shards_out[index], axis=0))
            attn, mlp = whole[:, :, :rows_in], whole[:, :, rows_in:]
        else:
            attn, mlp = every_piece(shards_out[index][0]), every_piece(shards_out[index][1])
        grads = finish(index, layers, attn, mlp, half, hidden, grads)
    grad_qkv, grad_out, grad_hidden, grad_down = grads
    grad_down = grad_down.reshape(layers, hidden_part, width)
    return (
        output,
        tokens_grad,
        grad_ada,
        grad_ada_bias,
        grad_gain_one,
        grad_qkv,
        grad_out,
        grad_gain_two,
        grad_hidden,
        grad_bias_hidden,
        grad_down,
        grad_bias_down,
    )


def pick_plan(mesh):
    def run(*arrays):
        tokens, first_gain, hidden_bias = arrays[0], arrays[7], arrays[12]
        fits = (
            mesh.shape["blk"] == 2
            and mesh.shape["uly"] == 4
            and tokens.shape[0] == 2
            and tokens.shape[1] % 64 == 0
            and tokens.shape[2] == HEADS * 64
            and HEADS % 4 == 0
            and first_gain.shape[1] % 64 == 0
            and hidden_bias.shape[1] % 256 == 0
        )
        return (local_paired if fits else local)(*arrays)

    return run


def solution(mesh):
    in_specs = (
        P("dp", ("blk", "uly"), None),
        P("dp", ("blk", "uly"), None),
        P("dp", ("blk", "uly")),
        P("dp", ("blk", "uly")),
        P("dp"),
        P(None, "dp", None),
        P(None, "dp"),
        P(None, "dp"),
        P(None, "dp", None),
        P(None, "dp", None),
        P(None, "dp"),
        P(None, "dp", None),
        P(None, "dp"),
        P(None, "dp", None),
        P(None, "dp"),
    )
    out_specs = (
        P("dp", ("blk", "uly"), None),
        P("dp", ("blk", "uly"), None),
        P(None, "dp", None),
        P(None, "dp"),
        P(None, "dp"),
        P(None, "dp", None),
        P(None, "dp", None),
        P(None, "dp"),
        P(None, "dp", None),
        P(None, "dp"),
        P(None, "dp", None),
        P(None, "dp"),
    )
    return jax.shard_map(pick_plan(mesh), mesh=mesh, in_specs=in_specs, out_specs=out_specs, check_vma=False)
```

```python
import math

import jax
import jax.numpy as jnp
from jax import lax
from jax.experimental import pallas as pl
from jax.experimental.pallas import tpu as pltpu
from jax.sharding import PartitionSpec as P

HEADS = 12


epsilon = 1e-05
neg_big = -1e30


def cond_vector(levels, width):
    half_width = width // 2
    freqs = jnp.exp(-math.log(10000.0) * jnp.arange(half_width, dtype=jnp.float32) / half_width)
    angles = levels.astype(jnp.float32)[:, None] * freqs[None, :]
    return jax.nn.silu(jnp.concatenate([jnp.cos(angles), jnp.sin(angles)], axis=-1))


def norm_mod(values, gain_vec, shift_vec, scale_vec):
    average = jnp.mean(values, axis=-1, keepdims=True)
    centered = values - average
    variance = jnp.mean(centered * centered, axis=-1, keepdims=True)
    return centered * lax.rsqrt(variance + epsilon) * gain_vec * (1.0 + scale_vec) + shift_vec


def gelu_tanh(values):
    return jax.nn.gelu(values, approximate=True)


def left_product(first, second):
    return lax.dot_general(
        first, second, (((0,), (0,)), ((), ())), preferred_element_type=jnp.float32
    )


def right_product(first, second):
    return lax.dot_general(
        first, second, (((1,), (1,)), ((), ())), preferred_element_type=jnp.float32
    )


def fetch(params, layer_index):
    p_ada, p_bias, p_gain, p_qkv, p_out, p_gain_two, p_hidden, p_hbias, p_down, p_dbias = params
    return (
        lax.all_gather(p_ada[layer_index], "dp", axis=0, tiled=True),
        lax.all_gather(p_bias[layer_index], "dp", axis=0, tiled=True),
        lax.all_gather(p_gain[layer_index], "dp", axis=0, tiled=True),
        lax.all_gather(p_qkv[layer_index], "dp", axis=0, tiled=True),
        lax.all_gather(p_out[layer_index], "dp", axis=0, tiled=True),
        lax.all_gather(p_gain_two[layer_index], "dp", axis=0, tiled=True),
        lax.all_gather(p_hidden[layer_index], "dp", axis=0, tiled=True),
        lax.all_gather(p_hbias[layer_index], "dp", axis=0, tiled=True),
        lax.all_gather(p_down[layer_index], "dp", axis=0, tiled=True),
        lax.all_gather(p_dbias[layer_index], "dp", axis=0, tiled=True),
    )


def reduce_grads(grads):
    shards = (
        lax.psum_scatter(
            grads[0].astype(jnp.bfloat16), "dp", scatter_dimension=0, tiled=True
        ).astype(jnp.float32),
        lax.psum_scatter(
            grads[1].astype(jnp.bfloat16), "dp", scatter_dimension=0, tiled=True
        ).astype(jnp.float32),
        lax.psum_scatter(
            grads[2].astype(jnp.bfloat16), "dp", scatter_dimension=0, tiled=True
        ).astype(jnp.float32),
        lax.psum_scatter(
            grads[3].astype(jnp.bfloat16), "dp", scatter_dimension=0, tiled=True
        ).astype(jnp.float32),
        lax.psum_scatter(
            grads[4].astype(jnp.bfloat16), "dp", scatter_dimension=0, tiled=True
        ).astype(jnp.float32),
        lax.psum_scatter(
            grads[5].astype(jnp.bfloat16), "dp", scatter_dimension=0, tiled=True
        ).astype(jnp.float32),
        lax.psum_scatter(
            grads[6].astype(jnp.bfloat16), "dp", scatter_dimension=0, tiled=True
        ).astype(jnp.float32),
        lax.psum_scatter(
            grads[7].astype(jnp.bfloat16), "dp", scatter_dimension=0, tiled=True
        ).astype(jnp.float32),
        lax.psum_scatter(
            grads[8].astype(jnp.bfloat16), "dp", scatter_dimension=0, tiled=True
        ).astype(jnp.float32),
        lax.psum_scatter(
            grads[9].astype(jnp.bfloat16), "dp", scatter_dimension=0, tiled=True
        ).astype(jnp.float32),
    )
    return (
        lax.psum(shards[0].astype(jnp.bfloat16), ("blk", "uly")).astype(jnp.float32),
        lax.psum(shards[1].astype(jnp.bfloat16), ("blk", "uly")).astype(jnp.float32),
        lax.psum(shards[2].astype(jnp.bfloat16), ("blk", "uly")).astype(jnp.float32),
        lax.psum(shards[3].astype(jnp.bfloat16), ("blk", "uly")).astype(jnp.float32),
        lax.psum(shards[4].astype(jnp.bfloat16), ("blk", "uly")).astype(jnp.float32),
        lax.psum(shards[5].astype(jnp.bfloat16), ("blk", "uly")).astype(jnp.float32),
        lax.psum(shards[6].astype(jnp.bfloat16), ("blk", "uly")).astype(jnp.float32),
        lax.psum(shards[7].astype(jnp.bfloat16), ("blk", "uly")).astype(jnp.float32),
        lax.psum(shards[8].astype(jnp.bfloat16), ("blk", "uly")).astype(jnp.float32),
        lax.psum(shards[9].astype(jnp.bfloat16), ("blk", "uly")).astype(jnp.float32),
    )


def over_blocks(block_fn, carry, key_piece, value_piece, seg_piece):
    count = key_piece.shape[2]
    size = 512

    def block_step(inner, position):
        offset = position * size
        key_blk = lax.dynamic_slice_in_dim(key_piece, offset, size, 2)
        value_blk = lax.dynamic_slice_in_dim(value_piece, offset, size, 2)
        seg_blk = lax.dynamic_slice_in_dim(seg_piece, offset, size, 0)
        return (block_fn(inner, key_blk, value_blk, seg_blk, offset), None)

    return lax.scan(block_step, carry, jnp.arange(count // size, dtype=jnp.int32))[0]


def split_heads(qkv_b):
    tokens_dev = qkv_b.shape[0]
    width = qkv_b.shape[1] // 3
    heads_all = lax.all_to_all(
        qkv_b.reshape(tokens_dev, 3, width), "uly", split_axis=2, concat_axis=0, tiled=True
    )
    span = heads_all.shape[0]
    head_dim = width // HEADS
    local_heads = heads_all.shape[2] // head_dim
    layout = heads_all.reshape(span, 3, local_heads, head_dim).transpose(1, 2, 3, 0)
    return (layout[0], layout[1], layout[2])


def layer_forward(state, weights_now, cond_b, seg_row):
    (
        ada_weight,
        ada_bias,
        first_gain,
        qkv_weight,
        out_weight,
        second_gain,
        hidden_weight,
        hidden_bias,
        down_weight,
        down_bias,
    ) = weights_now
    modulation = jnp.dot(ada_weight, cond_b, preferred_element_type=jnp.float32) + ada_bias.astype(
        jnp.float32
    )
    shift_one, scale_one, gate_one, shift_two, scale_two, gate_two = jnp.split(modulation, 6)
    normed_b = norm_mod(state, first_gain.astype(jnp.float32), shift_one, scale_one).astype(
        jnp.bfloat16
    )
    qkv_b = jnp.dot(normed_b, qkv_weight, preferred_element_type=jnp.float32).astype(jnp.bfloat16)
    query_t, key_t, value_t = split_heads(qkv_b)
    local_heads, head_dim, span = query_t.shape
    factor = head_dim ** (-0.5)
    query_seg = lax.dynamic_slice_in_dim(seg_row, lax.axis_index("blk") * span, span, 0)

    def forward_block(carry, key_blk, value_blk, seg_blk, start):
        running_max, running_total, weighted = carry
        scores = (
            jnp.einsum("hdq,hdk->hqk", query_t, key_blk, preferred_element_type=jnp.float32)
            * factor
        )
        allowed = (query_seg[:, None] == seg_blk[None, :])[None]
        masked = jnp.where(allowed, scores, neg_big)
        new_max = jnp.maximum(running_max, jnp.max(masked, axis=-1))
        probabilities = jnp.where(allowed, jnp.exp(masked - new_max[..., None]), 0.0)
        rescale = jnp.exp(running_max - new_max)
        running_total = running_total * rescale + jnp.sum(probabilities, axis=-1)
        update = jnp.einsum(
            "hqk,hdk->hdq",
            probabilities.astype(jnp.bfloat16),
            value_blk,
            preferred_element_type=jnp.float32,
        )
        weighted = weighted * rescale[:, None, :] + update
        return (new_max, running_total, weighted)

    initial = (
        jnp.full((local_heads, span), neg_big, jnp.float32),
        jnp.zeros((local_heads, span), jnp.float32),
        jnp.zeros((local_heads, head_dim, span), jnp.float32),
    )
    running_max, running_total, weighted = over_blocks(
        forward_block,
        initial,
        lax.all_gather(key_t, "blk", axis=2, tiled=True),
        lax.all_gather(value_t, "blk", axis=2, tiled=True),
        seg_row,
    )
    attended_heads = weighted / running_total[:, None, :]
    log_total = running_max + jnp.log(running_total)
    sendable = (
        attended_heads.astype(jnp.bfloat16).transpose(2, 0, 1).reshape(span, local_heads * head_dim)
    )
    attended_b = lax.all_to_all(sendable, "uly", split_axis=0, concat_axis=1, tiled=True)
    branch_one = jnp.dot(attended_b, out_weight, preferred_element_type=jnp.float32)
    middle = state + gate_one * branch_one
    normed_two = norm_mod(middle, second_gain.astype(jnp.float32), shift_two, scale_two).astype(
        jnp.bfloat16
    )
    hidden_pre = jnp.dot(
        normed_two, hidden_weight, preferred_element_type=jnp.float32
    ) + hidden_bias.astype(jnp.float32)
    activated = gelu_tanh(hidden_pre).astype(jnp.bfloat16)
    branch_two = jnp.dot(
        activated, down_weight, preferred_element_type=jnp.float32
    ) + down_bias.astype(jnp.float32)
    result = middle + gate_two * branch_two
    kept = (
        state,
        modulation,
        normed_b,
        query_t,
        key_t,
        value_t,
        attended_heads,
        log_total,
        attended_b,
        branch_one,
        middle,
        normed_two,
        hidden_pre,
        activated,
        branch_two,
    )
    return (result, kept)


def layer_backward(grad, weights_now, kept, cond_b, seg_row):
    (
        ada_weight,
        ada_bias,
        first_gain,
        qkv_weight,
        out_weight,
        second_gain,
        hidden_weight,
        hidden_bias,
        down_weight,
        down_bias,
    ) = weights_now
    (
        state,
        modulation,
        normed_b,
        query_t,
        key_t,
        value_t,
        attended_heads,
        log_total,
        attended_b,
        branch_one,
        middle,
        normed_two,
        hidden_pre,
        activated,
        branch_two,
    ) = kept
    shift_one, scale_one, gate_one, shift_two, scale_two, gate_two = jnp.split(modulation, 6)
    gain_one = first_gain.astype(jnp.float32)
    gain_two = second_gain.astype(jnp.float32)
    d_gate_two = jnp.sum(grad * branch_two, axis=0)
    d_branch_two = (gate_two * grad).astype(jnp.bfloat16)
    d_down_weight = left_product(activated, d_branch_two)
    d_down_bias = jnp.sum(d_branch_two.astype(jnp.float32), axis=0)
    d_activated = right_product(d_branch_two, down_weight)
    gelu_back = jax.vjp(gelu_tanh, hidden_pre)[1]
    d_pre = gelu_back(d_activated)[0].astype(jnp.bfloat16)
    d_hidden_weight = left_product(normed_two, d_pre)
    d_hidden_bias = jnp.sum(d_pre.astype(jnp.float32), axis=0)
    d_normed_two = right_product(d_pre, hidden_weight)
    norm_back_two = jax.vjp(norm_mod, middle, gain_two, shift_two, scale_two)[1]
    d_middle_part, d_gain_two, d_shift_two, d_scale_two = norm_back_two(d_normed_two)
    d_middle = grad + d_middle_part
    d_gate_one = jnp.sum(d_middle * branch_one, axis=0)
    d_branch_one = (gate_one * d_middle).astype(jnp.bfloat16)
    d_out_weight = left_product(attended_b, d_branch_one)
    d_attended_b = right_product(d_branch_one, out_weight).astype(jnp.bfloat16)
    local_heads, head_dim, span = query_t.shape
    factor = head_dim ** (-0.5)
    d_heads_t = (
        lax.all_to_all(d_attended_b, "uly", split_axis=1, concat_axis=0, tiled=True)
        .reshape(span, local_heads, head_dim)
        .transpose(1, 2, 0)
    )
    row_delta = jnp.sum(d_heads_t.astype(jnp.float32) * attended_heads, axis=1)
    query_seg = lax.dynamic_slice_in_dim(seg_row, lax.axis_index("blk") * span, span, 0)

    def backward_block(carry, key_blk, value_blk, seg_blk, start):
        d_query, d_key_all, d_value_all = carry
        scores = (
            jnp.einsum("hdq,hdk->hqk", query_t, key_blk, preferred_element_type=jnp.float32)
            * factor
        )
        allowed = (query_seg[:, None] == seg_blk[None, :])[None]
        probabilities = jnp.where(allowed, jnp.exp(scores - log_total[..., None]), 0.0)
        d_probs = jnp.einsum(
            "hdq,hdk->hqk", d_heads_t, value_blk, preferred_element_type=jnp.float32
        )
        d_scores = (probabilities * (d_probs - row_delta[..., None])).astype(jnp.bfloat16)
        d_query = (
            d_query
            + jnp.einsum("hqk,hdk->hdq", d_scores, key_blk, preferred_element_type=jnp.float32)
            * factor
        )
        d_key_new = (
            jnp.einsum("hqk,hdq->hdk", d_scores, query_t, preferred_element_type=jnp.float32)
            * factor
        )
        d_value_new = jnp.einsum(
            "hqk,hdq->hdk",
            probabilities.astype(jnp.bfloat16),
            d_heads_t,
            preferred_element_type=jnp.float32,
        )
        size = key_blk.shape[2]
        d_key_all = lax.dynamic_update_slice_in_dim(
            d_key_all, lax.dynamic_slice_in_dim(d_key_all, start, size, 2) + d_key_new, start, 2
        )
        d_value_all = lax.dynamic_update_slice_in_dim(
            d_value_all,
            lax.dynamic_slice_in_dim(d_value_all, start, size, 2) + d_value_new,
            start,
            2,
        )
        return (d_query, d_key_all, d_value_all)

    row_len = seg_row.shape[0]
    initial = (
        jnp.zeros((local_heads, head_dim, span), jnp.float32),
        jnp.zeros((local_heads, head_dim, row_len), jnp.float32),
        jnp.zeros((local_heads, head_dim, row_len), jnp.float32),
    )
    d_query, d_key_all, d_value_all = over_blocks(
        backward_block,
        initial,
        lax.all_gather(key_t, "blk", axis=2, tiled=True),
        lax.all_gather(value_t, "blk", axis=2, tiled=True),
        seg_row,
    )
    d_key, d_value = (
        lax.psum_scatter(
            d_key_all.astype(jnp.bfloat16), "blk", scatter_dimension=2, tiled=True
        ).astype(jnp.float32),
        lax.psum_scatter(
            d_value_all.astype(jnp.bfloat16), "blk", scatter_dimension=2, tiled=True
        ).astype(jnp.float32),
    )
    joined = jnp.stack([d_query, d_key, d_value], axis=0).astype(jnp.bfloat16)
    stacked = joined.transpose(3, 0, 1, 2).reshape(span, 3, local_heads * head_dim)
    returned = lax.all_to_all(stacked, "uly", split_axis=0, concat_axis=2, tiled=True)
    tokens_dev = state.shape[0]
    d_qkv_b = returned.reshape(tokens_dev, returned.shape[1] * returned.shape[2])
    d_qkv_weight = left_product(normed_b, d_qkv_b)
    d_normed = right_product(d_qkv_b, qkv_weight)
    norm_back_one = jax.vjp(norm_mod, state, gain_one, shift_one, scale_one)[1]
    d_state_part, d_gain_one, d_shift_one, d_scale_one = norm_back_one(d_normed)
    d_state = d_middle + d_state_part
    d_modulation = jnp.concatenate(
        [d_shift_one, d_scale_one, d_gate_one, d_shift_two, d_scale_two, d_gate_two]
    )
    d_ada_weight = d_modulation[:, None] * cond_b.astype(jnp.float32)[None, :]
    grads = (
        d_ada_weight,
        d_modulation,
        d_gain_one,
        d_qkv_weight,
        d_out_weight,
        d_gain_two,
        d_hidden_weight,
        d_hidden_bias,
        d_down_weight,
        d_down_bias,
    )
    return (d_state, grads)


def add_tuples(first, second):
    if first is None:
        return second
    return tuple((left_item + right_item for left_item, right_item in zip(first, second)))


def local(
    tokens,
    cotangent,
    segments,
    noised,
    levels,
    ada_weight,
    ada_bias,
    first_gain,
    qkv_weight,
    out_weight,
    second_gain,
    hidden_weight,
    hidden_bias,
    down_weight,
    down_bias,
):
    params = (
        ada_weight,
        ada_bias,
        first_gain,
        qkv_weight,
        out_weight,
        second_gain,
        hidden_weight,
        hidden_bias,
        down_weight,
        down_bias,
    )
    layers = ada_weight.shape[0]
    batches = tokens.shape[0]
    row_segs = lax.all_gather(segments, ("blk", "uly"), axis=1, tiled=True)
    conds = cond_vector(levels, ada_weight.shape[2]).astype(jnp.bfloat16)
    stored = [fetch(params, layer_index) for layer_index in range(layers)]
    sums = [None] * layers
    outputs = []
    input_grads = []
    for batch_index in range(batches):
        state = tokens[batch_index].astype(jnp.float32)
        cond_b = conds[batch_index]
        seg_row = row_segs[batch_index]
        kept_all = []
        for layer_index in range(layers):
            weights_now = stored[layer_index]
            state, kept = layer_forward(state, weights_now, cond_b, seg_row)
            kept_all.append(kept)
        outputs.append(state.astype(jnp.bfloat16))
        grad = (
            cotangent[batch_index].astype(jnp.float32)
            * noised[batch_index].astype(jnp.float32)[:, None]
        )
        for layer_index in reversed(range(layers)):
            weights_now = stored[layer_index]
            grad, grads = layer_backward(grad, weights_now, kept_all[layer_index], cond_b, seg_row)
            sums[layer_index] = add_tuples(sums[layer_index], reduce_grads(grads))
        input_grads.append(grad.astype(jnp.bfloat16))
    stacked = [
        jnp.stack([sums[layer_index][member] for layer_index in range(layers)])
        for member in range(10)
    ]
    return (
        jnp.stack(outputs),
        jnp.stack(input_grads),
        stacked[0],
        stacked[1],
        stacked[2],
        stacked[3],
        stacked[4],
        stacked[5],
        stacked[6],
        stacked[7],
        stacked[8],
        stacked[9],
    )


SWAP = [(0, 1), (1, 0)]
PAIR = [(0, 1), (1, 0), (2, 3), (3, 2)]
ACROSS = [(0, 2), (2, 0), (1, 3), (3, 1)]
VMEM_BYTES = 16 * 1024 * 1024
COPY_BYTES = 8 * 1024 * 1024
FREE = pl.CostEstimate(flops=0, bytes_accessed=0, transcendentals=0)


def swap_blk(value):
    return lax.ppermute(value, "blk", SWAP)


def swap_half(value):
    return lax.ppermute(value, "uly", PAIR)


def swap_core(value):
    return lax.ppermute(value, "uly", ACROSS)


def from_shard(value, back, shards):
    return lax.ppermute(value, "dp", [(at, (at + back) % shards) for at in range(shards)])


def plain_product(first, second):
    return jnp.dot(first, second, preferred_element_type=jnp.float32)


def normalise(values):
    average = jnp.mean(values, axis=-1, keepdims=True)
    centered = values - average
    variance = jnp.mean(centered * centered, axis=-1, keepdims=True)
    inverse = lax.rsqrt(variance + epsilon)
    return centered * inverse, inverse


def pick(array, index, axis):
    return lax.dynamic_index_in_dim(array, index, axis, keepdims=False)


def low(value):
    return value.astype(jnp.bfloat16)


def wide(value):
    return value.astype(jnp.float32)


def token(array):
    while array.ndim > 2:
        array = array[0]
    return array[:16, :128]


def whole_call(kernel, name, shapes, operands, place=None, after=()):
    specs = [] if place is None else [pl.BlockSpec(memory_space=pltpu.SMEM)]
    specs += [pl.BlockSpec(memory_space=pltpu.VMEM)] * len(operands)
    specs += [pl.BlockSpec(memory_space=pl.ANY)] * len(after)
    count = len(operands) + (place is not None)

    def body(*refs):
        kernel(*refs[:count], *refs[count + len(after) :])

    return pl.pallas_call(
        body,
        out_shape=tuple(jax.ShapeDtypeStruct(shape, kind) for shape, kind in shapes),
        in_specs=specs,
        out_specs=(pl.BlockSpec(memory_space=pltpu.VMEM),) * len(shapes),
        compiler_params=pltpu.CompilerParams(vmem_limit_bytes=VMEM_BYTES),
        cost_estimate=FREE,
        name=name,
    )(*([] if place is None else [place]), *operands, *after)


def hold(value, *after):
    return pl.pallas_call(
        lambda *refs: None,
        out_shape=jax.ShapeDtypeStruct(value.shape, value.dtype),
        in_specs=[pl.BlockSpec(memory_space=pl.ANY)] * (1 + len(after)),
        out_specs=pl.BlockSpec(memory_space=pl.ANY),
        input_output_aliases={0: 0},
        cost_estimate=FREE,
        name="hold",
    )(value, *after)


def run_copies(pairs, sems):
    copies = [
        pltpu.make_async_copy(source, target, sems.at[number])
        for number, (source, target) in enumerate(pairs)
    ]
    for copy in copies:
        copy.start()
    for copy in copies:
        copy.wait()


def attn_pairs(sizes, layer, rows, core, qkv_ref, out_ref, target_ref):
    rows_in, rows_down, half, hidden_cut, shards = sizes
    lanes = pl.multiple_of(core * half, 128)
    pairs = [
        (
            qkv_ref.at[layer, rows, pl.ds(kind * 2 * half + lanes, half)],
            target_ref.at[:, pl.ds(kind * half, half)],
        )
        for kind in range(3)
    ]
    pairs.append((out_ref.at[layer, rows], target_ref.at[:, pl.ds(3 * half, 2 * half)]))
    return pairs


def hidden_pairs(sizes, layer, rows, core, hidden_ref, target_ref):
    rows_in, rows_down, half, hidden_cut, shards = sizes
    lanes = pl.multiple_of(core * hidden_cut, 128)
    return [
        (
            hidden_ref.at[layer, rows, pl.ds(at * 2 * hidden_cut + lanes, hidden_cut)],
            target_ref.at[:, pl.ds(at * hidden_cut, hidden_cut)],
        )
        for at in range(shards)
    ]


def down_pairs(sizes, layer, place_ref, down_ref, target_ref):
    rows_in, rows_down, half, hidden_cut, shards = sizes
    first = pl.multiple_of(place_ref[2] * hidden_cut + place_ref[1] * rows_down, 16)
    return [
        (
            down_ref.at[layer, pl.ds(first + side * rows_in, rows_in)],
            target_ref.at[:, pl.ds(side * 2 * half, 2 * half)],
        )
        for side in range(2)
    ]


def mlp_pairs(sizes, layer, place_ref, hidden_ref, down_ref, target_ref):
    rows_in = sizes[0]
    rows = pl.ds(pl.multiple_of(place_ref[1] * rows_in, 16), rows_in)
    pairs = hidden_pairs(sizes, layer, rows, place_ref[2], hidden_ref, target_ref.at[pl.ds(0, rows_in)])
    return pairs + down_pairs(
        sizes, layer, place_ref, down_ref, target_ref.at[pl.ds(rows_in, rows_in)]
    )


def cut_attn_kernel(sizes, layer, place_ref, qkv_ref, out_ref, *refs):
    piece_ref, sems = refs[-2:]
    rows = pl.ds(pl.multiple_of(place_ref[1] * sizes[0], 16), sizes[0])
    run_copies(attn_pairs(sizes, layer, rows, place_ref[2], qkv_ref, out_ref, piece_ref), sems)


def cut_mlp_kernel(sizes, layer, place_ref, hidden_ref, down_ref, *refs):
    piece_ref, sems = refs[-2:]
    run_copies(mlp_pairs(sizes, layer, place_ref, hidden_ref, down_ref, piece_ref), sems)


def others_kernel(count, first, place_ref, all_ref, *refs):
    outs, sems = refs[-1 - count : -1], refs[-1]
    shards = all_ref.shape[0]
    pairs = []
    for out_ref in outs:
        rows = out_ref.shape[1]
        for back in range(1, shards):
            source = all_ref.at[lax.rem(place_ref[0] + shards - back, shards), pl.ds(first, rows)]
            pairs.append((source, out_ref.at[back - 1]))
        first += rows
    run_copies(pairs, sems)


def others(place, whole, first, cuts, after=()):
    shards, _, columns = whole.shape
    return pl.pallas_call(
        lambda *refs: others_kernel(len(cuts), first, *refs),
        out_shape=tuple(jax.ShapeDtypeStruct((shards - 1, rows, columns), whole.dtype) for rows in cuts),
        in_specs=[pl.BlockSpec(memory_space=pltpu.SMEM)]
        + [pl.BlockSpec(memory_space=pl.ANY)] * (1 + len(after)),
        out_specs=(pl.BlockSpec(memory_space=pltpu.VMEM),) * len(cuts),
        scratch_shapes=[pltpu.SemaphoreType.DMA((len(cuts) * (shards - 1),))],
        compiler_params=pltpu.CompilerParams(vmem_limit_bytes=COPY_BYTES),
        cost_estimate=FREE,
        name="others",
    )(place, whole, *after)


def copy_call(kernel, name, place, operands, shapes, count, after=()):
    kind = operands[0].dtype
    return pl.pallas_call(
        kernel,
        out_shape=tuple(jax.ShapeDtypeStruct(shape, kind) for shape in shapes),
        in_specs=[pl.BlockSpec(memory_space=pltpu.SMEM)]
        + [pl.BlockSpec(memory_space=pltpu.HBM)] * len(operands)
        + [pl.BlockSpec(memory_space=pl.ANY)] * len(after),
        out_specs=(pl.BlockSpec(memory_space=pltpu.VMEM),) * len(shapes),
        scratch_shapes=[pltpu.SemaphoreType.DMA((count,))],
        compiler_params=pltpu.CompilerParams(vmem_limit_bytes=COPY_BYTES),
        cost_estimate=FREE,
        name=name,
    )(place, *operands, *after)


def join_attn_kernel(sizes, layer, place_ref, qkv_ref, out_ref, *refs):
    pieces, whole_ref, sems = refs[:4], refs[-2], refs[-1]
    rows_in, shards = sizes[0], sizes[-1]
    shard, quarter, core = place_ref[0], place_ref[1], place_ref[2]
    pairs = attn_pairs(
        sizes, layer, slice(None), core, qkv_ref, out_ref, whole_ref.at[shard]
    )
    for relative, piece_ref in enumerate(pieces):
        rows = pl.ds(pl.multiple_of((quarter ^ relative) * rows_in, 16), rows_in)
        for back in range(1, shards):
            target = whole_ref.at[lax.rem(shard + shards - back, shards), rows]
            pairs.append((piece_ref.at[back - 1], target))
    run_copies(pairs, sems)


def join_mlp_kernel(sizes, layer, place_ref, hidden_ref, down_ref, *refs):
    pieces = refs[:4]
    whole_h_ref, whole_d_ref, sems = refs[-3:]
    rows_in, rows_down, half, hidden_cut, shards = sizes
    shard, quarter, core = place_ref[0], place_ref[1], place_ref[2]
    pairs = hidden_pairs(sizes, layer, slice(None), core, hidden_ref, whole_h_ref.at[shard])
    first = pl.multiple_of(core * hidden_cut, 128)
    pairs.append((down_ref.at[layer, pl.ds(first, hidden_cut)], whole_d_ref.at[shard]))
    for relative in range(4):
        at_h = pl.multiple_of((quarter ^ relative) * rows_in, 16)
        at_d = pl.multiple_of((quarter ^ relative) * rows_down, 16)
        for back in range(1, shards):
            place = lax.rem(shard + shards - back, shards)
            part_h = pieces[relative].at[back - 1, pl.ds(0, rows_in)]
            part_d = pieces[relative].at[back - 1, pl.ds(rows_in, rows_in)]
            pairs.append((part_h, whole_h_ref.at[place, pl.ds(at_h, rows_in)]))
            for side in range(2):
                pairs.append(
                    (
                        part_d.at[:, pl.ds(side * 2 * half, 2 * half)],
                        whole_d_ref.at[place, pl.ds(at_d + side * rows_in, rows_in)],
                    )
                )
    run_copies(pairs, sems)


def finish_attn_part(owner, half, rows, piece, qkv_ref, out_ref):
    width = 2 * half
    lanes = pl.multiple_of(owner * half, 128)
    for kind in range(3):
        qkv_ref[0, :, pl.ds(kind * width + lanes, half)] = wide(
            piece[0, :rows, kind * half : (kind + 1) * half]
        )
    out_ref[0, :, pl.ds(lanes, half)] = wide(piece[0, :rows, 3 * half :])


def finish_mlp_part(owner, half, rows, shards, start, piece, hidden_ref, down_ref):
    width = 2 * half
    hidden_cut = hidden_ref.shape[2] // (2 * shards)
    lanes = pl.multiple_of(owner * hidden_cut, 128)
    for at in range(shards):
        hidden_ref[0, :, pl.ds(at * 2 * hidden_cut + lanes, hidden_cut)] = wide(
            piece[0, start : start + rows, at * hidden_cut : (at + 1) * hidden_cut]
        )
    for side in range(2):
        down_ref[0, owner, 0, side * rows : (side + 1) * rows] = wide(
            piece[0, start + rows :, side * width : (side + 1) * width]
        )


def finish_kernel(parts, half, rows, shards, place_ref, *refs):
    outs = refs[len(refs) - 2 * len(parts) :]
    for relative in range(2):
        owner, at = place_ref[2] ^ relative, 0
        for number, part in enumerate(parts):
            if part == "attn":
                finish_attn_part(owner, half, rows, refs[relative], *outs[2 * number : 2 * number + 2])
                at += rows
            else:
                finish_mlp_part(
                    owner, half, rows, shards, at, refs[relative], *outs[2 * number : 2 * number + 2]
                )


def finish(place, layer, parts, pieces, shapes, half, rows, shards, before=None):
    width = 2 * half
    blocks = {
        "attn": [
            pl.BlockSpec((1, rows, 3 * width), lambda at, place: (layer, place[1] ^ at, 0)),
            pl.BlockSpec((1, rows, width), lambda at, place: (layer, place[1] ^ at, 0)),
        ],
        "mlp": [
            pl.BlockSpec((1, rows, shapes["mlp"][0][2]), lambda at, place: (layer, place[1] ^ at, 0)),
            pl.BlockSpec(
                (1, 2, 1, 2 * rows, width), lambda at, place: (layer, 0, place[1] ^ at, 0, 0)
            ),
        ],
    }
    operands, aliases = list(pieces), {}
    specs = [pl.BlockSpec((1, *piece.shape[1:]), lambda at, place: (at, 0, 0)) for piece in pieces]
    if before is not None:
        operands += list(before)
        specs += [pl.BlockSpec(memory_space=pl.ANY)] * len(before)
        aliases = {3 + number: number for number in range(len(before))}
    return pl.pallas_call(
        lambda *refs: finish_kernel(parts, half, rows, shards, *refs),
        grid_spec=pltpu.PrefetchScalarGridSpec(
            num_scalar_prefetch=1,
            grid=(4,),
            in_specs=specs,
            out_specs=tuple(block for part in parts for block in blocks[part]),
        ),
        out_shape=tuple(
            jax.ShapeDtypeStruct(shape, jnp.float32) for part in parts for shape in shapes[part]
        ),
        input_output_aliases=aliases,
        compiler_params=pltpu.CompilerParams(vmem_limit_bytes=VMEM_BYTES),
        cost_estimate=FREE,
        name="finish",
    )(place, *operands)


TILE = 256
SHIFT_ONE, SCALE_ONE, GATE_ONE, SHIFT_TWO, SCALE_TWO, GATE_TWO, GAIN_ONE, GAIN_TWO, BIAS_DOWN = range(9)


def row_of(ref, number):
    return ref[number : number + 1, :]


def norm_rows(values, vec_ref, gain, scale, shift):
    unit_values, _ = normalise(values)
    return low(
        unit_values * row_of(vec_ref, gain) * (1.0 + row_of(vec_ref, scale)) + row_of(vec_ref, shift)
    )


def enter_kernel(x_ref, vec_ref, n_ref):
    n_ref[...] = norm_rows(wide(x_ref[...]), vec_ref, GAIN_ONE, SCALE_ONE, SHIFT_ONE)


def project_kernel(first, last, own_ref, other_ref, weight_ref, out_ref, *refs):
    count = own_ref.shape[0]
    for chip_ref in refs:
        chip_ref[:count, :] = own_ref[...]
        chip_ref[count:, :] = other_ref[...]
    out_ref[:count, :] = low(plain_product(own_ref[...], weight_ref[:, first:last]))
    out_ref[count:, :] = low(plain_product(other_ref[...], weight_ref[:, first:last]))


def middle_kernel(
    place_ref, att_own_ref, att_other_ref, weight_ref, state_ref, vec_ref, branch_ref, middle_ref, n_ref, att_ref
):
    half = att_own_ref.shape[1]
    att_ref[:, pl.ds(pl.multiple_of(place_ref[2] * half, 128), half)] = att_own_ref[...]
    att_ref[:, pl.ds(pl.multiple_of((1 - place_ref[2]) * half, 128), half)] = att_other_ref[...]
    branch = plain_product(att_ref[...], weight_ref[:, 3 * half :])
    middle = state_ref[...] + row_of(vec_ref, GATE_ONE) * branch
    branch_ref[...] = branch
    middle_ref[...] = middle
    n_ref[...] = norm_rows(middle, vec_ref, GAIN_TWO, SCALE_TWO, SHIFT_TWO)


def chunk_call(kernel, name, grid, operands, specs, shapes, out_specs, scratch, after=()):
    first_out = len(operands)
    return pl.pallas_call(
        lambda *refs: kernel(*refs[:first_out], *refs[first_out + len(after) :]),
        grid=(grid,),
        out_shape=tuple(jax.ShapeDtypeStruct(shape, kind) for shape, kind in shapes),
        in_specs=list(specs) + [pl.BlockSpec(memory_space=pl.ANY)] * len(after),
        out_specs=tuple(out_specs),
        scratch_shapes=scratch,
        compiler_params=pltpu.CompilerParams(vmem_limit_bytes=VMEM_BYTES),
        cost_estimate=FREE,
        name=name,
    )(*operands, *after)


def sent_and_kept(total_ref, part_ref, send_ref):
    @pl.when(pl.program_id(0) == pl.num_programs(0) - 1)
    def _():
        count = part_ref.shape[0]
        part_ref[...] = total_ref[:count, :]
        send_ref[...] = low(total_ref[count:, :])


def take_both(own_ref, other_ref, chip_ref):
    @pl.when(pl.program_id(0) == 0)
    def _():
        count = own_ref.shape[0]
        chip_ref[:count, :] = own_ref[...]
        chip_ref[count:, :] = other_ref[...]


def add_up(total_ref, term):
    @pl.when(pl.program_id(0) == 0)
    def _():
        total_ref[...] = term

    @pl.when(pl.program_id(0) > 0)
    def _():
        total_ref[...] += term


def mlp_kernel(
    own_ref, other_ref, hidden_ref, down_ref, bias_ref, act_ref, slope_ref, part_ref, send_ref, chip_ref, total_ref
):
    take_both(own_ref, other_ref, chip_ref)
    pre = plain_product(chip_ref[...], hidden_ref[...]) + bias_ref[...]
    square = pre * pre
    factor = math.sqrt(2.0 / math.pi)
    bent = jnp.tanh(pre * (factor + (factor * 0.044715) * square))
    near_half = 0.5 + 0.5 * bent
    act = low(pre * near_half)
    act_ref[...] = act
    slope_ref[...] = near_half + (0.5 * pre) * (1.0 - bent * bent) * (
        factor + (3.0 * factor * 0.044715) * square
    )
    add_up(total_ref, plain_product(act, down_ref[...]))
    sent_and_kept(total_ref, part_ref, send_ref)


def run_mlp(own, other, hiddens, downs, bias, after):
    count, width = own.shape
    cuts = hiddens.shape[1]
    size = 384
    fixed = lambda rows, columns: pl.BlockSpec((rows, columns), lambda at: (0, 0))
    across = lambda rows: pl.BlockSpec((rows, size), lambda at: (0, at))
    return chunk_call(
        mlp_kernel, "mlp", cuts // size,
        [own, other, hiddens, downs, bias],
        [
            fixed(count, width), fixed(count, width), across(width),
            pl.BlockSpec((size, width), lambda at: (at, 0)), across(1),
        ],
        [
            ((2 * count, cuts), jnp.bfloat16), ((2 * count, cuts), jnp.float32),
            ((count, width), jnp.float32), ((count, width), jnp.bfloat16), ((2 * count, width), jnp.bfloat16),
        ],
        [across(2 * count), across(2 * count), fixed(count, width), fixed(count, width), fixed(2 * count, width)],
        [pltpu.VMEM((2 * count, width), jnp.float32)],
        after,
    )


def leave_kernel(last, part_ref, arrived_ref, middle_ref, vec_ref, *refs):
    branch = part_ref[...] + wide(arrived_ref[...]) + row_of(vec_ref, BIAS_DOWN)
    state = middle_ref[...] + row_of(vec_ref, GATE_TWO) * branch
    if last:
        branch_ref, out_ref = refs
        out_ref[...] = low(state)
    else:
        next_vec_ref, branch_ref, state_ref, n_ref = refs
        state_ref[...] = state
        n_ref[...] = norm_rows(state, next_vec_ref, GAIN_ONE, SCALE_ONE, SHIFT_ONE)
    branch_ref[...] = branch


def start_back(grad, branch_ref, vec_ref, d_branch_ref, sums_ref, first):
    d_branch = low(row_of(vec_ref, GATE_TWO) * grad)
    d_branch_ref[...] = d_branch
    sums_ref[first : first + 1, :] = jnp.sum(grad * branch_ref[...], axis=0, keepdims=True)
    sums_ref[first + 1 : first + 2, :] = jnp.sum(wide(d_branch), axis=0, keepdims=True)


def top_kernel(masked_ref, vec_ref, grad_ref, d_branch_ref):
    grad = wide(masked_ref[...])
    grad_ref[...] = grad
    d_branch_ref[...] = low(row_of(vec_ref, GATE_TWO) * grad)


def top_sums_kernel(grad_ref, d_branch_ref, branch_ref, sums_ref):
    sums_ref[0:1, :] = jnp.sum(grad_ref[...] * branch_ref[...], axis=0, keepdims=True)
    sums_ref[1:2, :] = jnp.sum(wide(d_branch_ref[...]), axis=0, keepdims=True)


def mlp_back_kernel(
    own_ref, other_ref, slope_ref, hidden_ref, down_ref, d_pre_ref, part_ref, send_ref, bias_ref, chip_ref, total_ref
):
    take_both(own_ref, other_ref, chip_ref)
    d_pre = low(right_product(chip_ref[...], down_ref[...]) * slope_ref[...])
    d_pre_ref[...] = d_pre
    bias_ref[...] = jnp.sum(wide(d_pre), axis=0, keepdims=True)
    add_up(total_ref, right_product(d_pre, hidden_ref[...]))
    sent_and_kept(total_ref, part_ref, send_ref)


def run_mlp_back(own, other, slope, hiddens, downs, after):
    count, width = own.shape
    cuts = hiddens.shape[1]
    size = 384
    fixed = lambda rows, columns: pl.BlockSpec((rows, columns), lambda at: (0, 0))
    across = lambda rows: pl.BlockSpec((rows, size), lambda at: (0, at))
    return chunk_call(
        mlp_back_kernel, "mlp_back", cuts // size,
        [own, other, slope, hiddens, downs],
        [
            fixed(count, width), fixed(count, width), across(2 * count), across(width),
            pl.BlockSpec((size, width), lambda at: (at, 0)),
        ],
        [
            ((2 * count, cuts), jnp.bfloat16), ((count, width), jnp.float32), ((count, width), jnp.bfloat16),
            ((1, cuts), jnp.float32), ((2 * count, width), jnp.bfloat16),
        ],
        [across(2 * count), fixed(count, width), fixed(count, width), across(1), fixed(2 * count, width)],
        [pltpu.VMEM((2 * count, width), jnp.float32)],
        after,
    )


def norm_back(d_normed, values, gain, scale, shift_sum_ref):
    unit_values, inverse = normalise(values)
    first = jnp.sum(d_normed, axis=0, keepdims=True)
    second = jnp.sum(d_normed * unit_values, axis=0, keepdims=True)
    shift_sum_ref[0:1, :] = first
    shift_sum_ref[1:2, :] = gain * second
    shift_sum_ref[2:3, :] = (1.0 + scale) * second
    scaled = d_normed * ((1.0 + scale) * gain)
    inner = jnp.mean(scaled * unit_values, axis=-1, keepdims=True)
    return (scaled - jnp.mean(scaled, axis=-1, keepdims=True) - unit_values * inner) * inverse


def middle_back_kernel(
    place_ref, grad_ref, part_ref, arrived_ref, middle_ref, branch_ref, vec_ref, weight_ref,
    d_middle_ref, d_branch_ref, att_own_ref, att_other_ref, sums_ref, d_att_ref,
):
    half = att_own_ref.shape[1]
    d_normed = part_ref[...] + wide(arrived_ref[...])
    d_middle = grad_ref[...] + norm_back(
        d_normed, middle_ref[...], row_of(vec_ref, GAIN_TWO), row_of(vec_ref, SCALE_TWO), sums_ref
    )
    d_middle_ref[...] = d_middle
    sums_ref[3:4, :] = jnp.sum(d_middle * branch_ref[...], axis=0, keepdims=True)
    d_branch_ref[...] = low(row_of(vec_ref, GATE_ONE) * d_middle)
    d_att_ref[...] = low(right_product(d_branch_ref[...], weight_ref[:, 3 * half :]))
    att_own_ref[...] = d_att_ref[:, pl.ds(pl.multiple_of(place_ref[2] * half, 128), half)]
    att_other_ref[...] = d_att_ref[:, pl.ds(pl.multiple_of((1 - place_ref[2]) * half, 128), half)]


def project_back_kernel(d_qkv_ref, weight_ref, part_ref, send_ref):
    count = part_ref.shape[0]
    columns = d_qkv_ref.shape[1]
    part_ref[...] = right_product(d_qkv_ref[:count, :], weight_ref[:, :columns])
    send_ref[...] = low(right_product(d_qkv_ref[count:, :], weight_ref[:, :columns]))


def enter_back_kernel(last, d_middle_ref, part_ref, arrived_ref, state_ref, vec_ref, *refs):
    d_normed = part_ref[...] + wide(arrived_ref[...])
    if last:
        sums_ref, out_ref = refs
    else:
        branch_ref, next_vec_ref, sums_ref, grad_ref, d_branch_ref = refs
    grad = d_middle_ref[...] + norm_back(
        d_normed, wide(state_ref[...]), row_of(vec_ref, GAIN_ONE), row_of(vec_ref, SCALE_ONE), sums_ref
    )
    if last:
        out_ref[...] = low(grad)
    else:
        grad_ref[...] = grad
        start_back(grad, branch_ref, next_vec_ref, d_branch_ref, sums_ref, 3)


def attend_kernel(seg_q_ref, seg_k_ref, q_ref, kl_ref, vl_ref, kf_ref, vf_ref, *refs):
    own_ref, other_ref, of_ref, lse_ref = refs[-4:]
    count = kl_ref.shape[0]
    TILE = count // 2
    low_half = lax.broadcasted_iota(jnp.int32, (count, 128), 1) < 64
    for start in range(0, q_ref.shape[0], TILE):
        rows = pl.ds(start, TILE)
        seg_q = seg_q_ref[rows, :]
        allow_l = seg_q == seg_k_ref[:, :count]
        allow_f = seg_q == seg_k_ref[:, count:]
        query = q_ref[rows, :]
        query = query * jnp.asarray(0.125, query.dtype)
        outs, lses = [], []
        for head in range(2):
            half = low_half if head == 0 else jnp.logical_not(low_half)
            q_h = jnp.where(half[:TILE], query, jnp.zeros_like(query))
            s_l = jnp.where(allow_l, right_product(q_h, kl_ref[...]), neg_big)
            s_f = jnp.where(allow_f, right_product(q_h, kf_ref[...]), neg_big)
            top = jnp.maximum(
                jnp.max(s_l, axis=1, keepdims=True), jnp.max(s_f, axis=1, keepdims=True)
            )
            p_l = jnp.exp(s_l - top).astype(jnp.bfloat16)
            p_f = jnp.exp(s_f - top).astype(jnp.bfloat16)
            one = jnp.ones((count, 128), jnp.bfloat16)
            summed = plain_product(p_l, jnp.where(half, vl_ref[...], one)) + plain_product(
                p_f, jnp.where(half, vf_ref[...], one)
            )
            total = pltpu.roll(summed, 64, 1)
            outs.append(summed / total)
            lses.append(top + jnp.log(total))
        result = jnp.where(low_half[:TILE], outs[0], outs[1])
        of_ref[rows, :] = result
        (own_ref if start == 0 else other_ref)[...] = result.astype(jnp.bfloat16)
        lse_ref[rows, :] = jnp.where(low_half[:TILE], lses[0], lses[1])


def attend(query, near, far, seg_q, seg_k, after):
    count, half = query.shape
    pairs = half // 128
    block = lambda off: pl.BlockSpec((count, 128), lambda j: (0, off + j))
    part = pl.BlockSpec((count // 2, 128), lambda j: (0, j))
    return pl.pallas_call(
        attend_kernel,
        grid=(pairs,),
        out_shape=(
            jax.ShapeDtypeStruct((count // 2, half), jnp.bfloat16),
            jax.ShapeDtypeStruct((count // 2, half), jnp.bfloat16),
            jax.ShapeDtypeStruct((count, half), jnp.float32),
            jax.ShapeDtypeStruct((count, half), jnp.float32),
        ),
        in_specs=[
            pl.BlockSpec((count, 1), lambda j: (0, 0)),
            pl.BlockSpec((1, 2 * count), lambda j: (0, 0)),
            block(0),
            block(0),
            block(pairs),
            block(0),
            block(pairs),
        ]
        + [pl.BlockSpec(memory_space=pl.ANY)] * len(after),
        out_specs=(part, part, block(0), block(0)),
        compiler_params=pltpu.CompilerParams(vmem_limit_bytes=VMEM_BYTES),
        cost_estimate=FREE,
        name="attend",
    )(seg_q, seg_k, query, near, near, far, far, *after)


def back_kernel(has_more, seg_q_ref, seg_k_ref, q_ref, k_ref, v_ref, do_own_ref, do_other_ref, o_ref, lse_ref, *refs):
    count = k_ref.shape[0]
    TILE = count // 2
    low_half = lax.broadcasted_iota(jnp.int32, (TILE, 128), 1) < 64
    q_turned = (q_ref[...].astype(jnp.float32) * 0.125).T.astype(jnp.bfloat16)
    do_turned = [ref[...].astype(jnp.float32).T.astype(jnp.bfloat16) for ref in (do_own_ref, do_other_ref)]
    d_keys, d_values, d_queries = [0.0, 0.0], [0.0, 0.0], []
    for start in range(0, q_ref.shape[0], TILE):
        rows = pl.ds(start, TILE)
        allow = seg_q_ref[rows, :] == seg_k_ref[...]
        query = q_ref[rows, :]
        query = query * jnp.asarray(0.125, query.dtype)
        d_out = (do_own_ref if start == 0 else do_other_ref)[...]
        product = d_out.astype(jnp.float32) * o_ref[rows, :]
        d_query = []
        for head in range(2):
            half = low_half if head == 0 else jnp.logical_not(low_half)
            lanes = slice(64 * head, 64 * head + 64)
            q_h = jnp.where(half, query, jnp.zeros_like(query))
            do_h = jnp.where(half, d_out, jnp.zeros_like(d_out))
            scores = jnp.where(allow, right_product(q_h, k_ref[...]), neg_big)
            probs = jnp.exp(scores - lse_ref[rows, 64 * head : 64 * head + 1])
            d_probs = right_product(do_h, v_ref[...])
            delta = jnp.sum(jnp.where(half, product, 0.0), axis=1, keepdims=True)
            d_scores = (probs * (d_probs - delta)).astype(jnp.bfloat16)
            d_values[head] += plain_product(
                do_turned[start // TILE][lanes], probs.astype(jnp.bfloat16)
            )
            d_keys[head] += plain_product(q_turned[lanes, start : start + TILE], d_scores)
            d_query.append(plain_product(d_scores, k_ref[...]))
        d_queries.append(jnp.where(low_half, d_query[0], d_query[1]) * 0.125)
    d_key = jnp.concatenate(d_keys, axis=0).T
    d_value = jnp.concatenate(d_values, axis=0).T
    d_query = jnp.concatenate(d_queries, axis=0)
    if has_more:
        dq_more_ref, dk_more_ref, dv_more_ref, out_ref = refs
        half = out_ref.shape[1] // 3
        at = pl.multiple_of(pl.program_id(0) * 128, 128)
        out_ref[:, pl.ds(at, 128)] = (d_query + dq_more_ref[...]).astype(jnp.bfloat16)
        out_ref[:, pl.ds(half + at, 128)] = (d_key + dk_more_ref[...].astype(jnp.float32)).astype(
            jnp.bfloat16
        )
        out_ref[:, pl.ds(2 * half + at, 128)] = (
            d_value + dv_more_ref[...].astype(jnp.float32)
        ).astype(jnp.bfloat16)
    else:
        dq_ref, out_ref = refs
        half = out_ref.shape[1] // 2
        at = pl.multiple_of(pl.program_id(0) * 128, 128)
        dq_ref[...] = d_query
        out_ref[:, pl.ds(at, 128)] = d_key.astype(jnp.bfloat16)
        out_ref[:, pl.ds(half + at, 128)] = d_value.astype(jnp.bfloat16)


def attend_back(query, keys, seg_q, seg_k, d_outs, out, lse, more=None, after=()):
    count, half = query.shape
    pairs = half // 128
    block = lambda off: pl.BlockSpec((count, 128), lambda j: (0, off + j))
    part = pl.BlockSpec((count // 2, 128), lambda j: (0, j))
    whole = lambda width: pl.BlockSpec((count, width), lambda j: (0, 0))
    operands = [seg_q, seg_k, query, keys, keys, *d_outs, out, lse]
    specs = [
        pl.BlockSpec((count, 1), lambda j: (0, 0)),
        pl.BlockSpec((1, count), lambda j: (0, 0)),
        block(0),
        block(0),
        block(pairs),
        part,
        part,
        block(0),
        block(0),
    ]
    if more is None:
        out_shape = (
            jax.ShapeDtypeStruct((count, half), jnp.float32),
            jax.ShapeDtypeStruct((count, 2 * half), jnp.bfloat16),
        )
        out_specs = (block(0), whole(2 * half))
    else:
        operands += [more[0], more[1], more[1]]
        specs += [block(0), block(0), block(pairs)]
        out_shape = jax.ShapeDtypeStruct((count, 3 * half), jnp.bfloat16)
        out_specs = whole(3 * half)
    first_out = len(operands)
    operands += after
    specs += [pl.BlockSpec(memory_space=pl.ANY)] * len(after)
    return pl.pallas_call(
        lambda *refs: back_kernel(more is not None, *refs[:first_out], *refs[first_out + len(after) :]),
        grid=(pairs,),
        out_shape=out_shape,
        in_specs=specs,
        out_specs=out_specs,
        compiler_params=pltpu.CompilerParams(vmem_limit_bytes=VMEM_BYTES),
        cost_estimate=FREE,
        name="attend_back",
    )(*operands)


def local_paired(
    tokens,
    cotangent,
    segments,
    noised,
    levels,
    ada_weight,
    ada_bias,
    first_gain,
    qkv_weight,
    out_weight,
    second_gain,
    hidden_weight,
    hidden_bias,
    down_weight,
    down_bias,
):
    layers, ada_part, cond_width = ada_weight.shape
    part = first_gain.shape[1]
    hidden_part = hidden_bias.shape[1]
    width = tokens.shape[2]
    shards = width // part
    hidden = hidden_part * shards
    half = width // 2
    rows_in = part // 4
    rows_down = hidden_part // 8
    hidden_cut = hidden_part // 2
    blk = lax.axis_index("blk")
    uly = lax.axis_index("uly")
    core = uly // 2
    side = uly % 2
    quarter = blk * 2 + side
    shard = lax.axis_index("dp")
    row = shard * 2 + blk
    place = jnp.stack([shard, quarter, core]).astype(jnp.int32)

    def exchange(two_rows):
        return jnp.concatenate(
            [pick(two_rows, blk, 0), swap_blk(pick(two_rows, 1 - blk, 0))], axis=0
        )

    sizes = (rows_in, rows_down, half, hidden_cut, shards)
    columns = 4 * half
    attn_columns = 5 * half

    def spread(own, last):
        near, far = swap_half(own), swap_blk(own)
        return (own, near, far, swap_blk(near) if last == "blk" else swap_half(far))

    def whole_attn(index, spread, after=()):
        joined = copy_call(
            lambda *refs: join_attn_kernel(sizes, index, *refs), "join_attn", place,
            [qkv_weight, out_weight, *spread], [(shards, part, attn_columns)], 4 + 4 * (shards - 1), after,
        )[0]
        return joined.reshape(width, attn_columns)

    def whole_mlp(index, spread, after=()):
        hiddens, downs = copy_call(
            lambda *refs: join_mlp_kernel(sizes, index, *refs), "join_mlp", place,
            [hidden_weight, down_weight, *spread],
            [(shards, part, columns), (shards, hidden_cut, width)],
            shards + 1 + 12 * (shards - 1), after,
        )
        return hiddens.reshape(width, columns), downs.reshape(shards * hidden_cut, width)

    start = exchange(tokens)
    segs_two = exchange(segments)
    seg_chip = jnp.concatenate([segs_two, swap_core(segs_two)])
    seg_far = swap_half(seg_chip)
    attn_first = copy_call(
        lambda *refs: cut_attn_kernel(sizes, 0, *refs), "cut_attn", place,
        [qkv_weight, out_weight], [(rows_in, attn_columns)], 4,
    )[0]
    def every_shard_of(piece):
        return lax.all_gather(piece, "dp", axis=0, tiled=False)

    def others_of(piece):
        return jnp.stack([from_shard(piece, back, shards) for back in range(1, shards)])

    attn_own = others_of(attn_first)
    mlp_piece = copy_call(
        lambda *refs: cut_mlp_kernel(sizes, 0, *refs), "cut_mlp", place,
        [hidden_weight, down_weight], [(2 * rows_in, columns)], shards + 2, [attn_own, start, seg_far],
    )[0]
    mlp_first = every_shard_of(mlp_piece)
    attn = spread(attn_own, "half")

    def every_shard(vector):
        arrived = [vector] + [from_shard(vector, back, shards) for back in range(1, shards)]
        table = jnp.stack(arrived)
        return jnp.stack([pick(table, (shard + shards - at) % shards, 0) for at in range(shards)])

    all_levels = hold(every_shard(levels), mlp_piece).reshape(-1)
    conds = low(cond_vector(all_levels, cond_width))
    part_mods = jnp.stack(
        [right_product(conds, ada_weight[index]) + wide(ada_bias[index]) for index in range(layers)],
        axis=1,
    )
    own_vectors = wide(
        jnp.concatenate([first_gain, second_gain, down_bias, hidden_bias], axis=1)
    )

    def shared_for(target):
        return jnp.concatenate([pick(part_mods, target * 2 + blk, 0), own_vectors], axis=1)

    shared = [shared_for(shard)]
    for ahead in range(1, shards):
        shared.append(from_shard(shared_for((shard + ahead) % shards), ahead, shards))
    shared = jnp.stack(shared)
    shared = jnp.stack([pick(shared, (shard + shards - at) % shards, 0) for at in range(shards)])
    vectors = []
    for index in range(layers):
        table = shared[:, index]
        ends = [ada_part + number * part for number in range(4)]
        rows = [table[:, :ada_part].reshape(6, width)]
        rows += [table[:, first : first + part].reshape(1, width) for first in ends[:3]]
        bias_hidden = table[:, ends[3] :].reshape(shards, 2, hidden_cut)
        vectors.append(
            (jnp.concatenate(rows, axis=0), pick(bias_hidden, core, 1).reshape(1, shards * hidden_cut))
        )

    seg_q = seg_chip[:, None]
    seg_near_k, seg_far_k = seg_chip[None, :], seg_far[None, :]
    seg_k = jnp.concatenate([seg_near_k, seg_far_k], axis=1)

    def next_pieces(index, after):
        attn_piece = copy_call(
            lambda *refs: cut_attn_kernel(sizes, index, *refs), "cut_attn", place,
            [qkv_weight, out_weight], [(rows_in, attn_columns)], 4, after,
        )[0]
        mlp_piece = copy_call(
            lambda *refs: cut_mlp_kernel(sizes, index, *refs), "cut_mlp", place,
            [hidden_weight, down_weight], [(2 * rows_in, columns)], shards + 2, [attn_piece],
        )[0]
        return others_of(attn_piece), every_shard_of(mlp_piece)

    def spread_late(own, after):
        near, far = swap_half(own), hold(swap_blk(own), after)
        return (own, near, far, swap_half(far))

    tokens_here = start.shape[0]
    rows_f32 = ((tokens_here, width), jnp.float32)
    rows_low = ((tokens_here, width), jnp.bfloat16)
    half_low = ((tokens_here, half), jnp.bfloat16)
    chip_low = ((2 * tokens_here, width), jnp.bfloat16)
    cut_wide = shards * hidden_cut
    state = wide(start)
    normed = whole_call(enter_kernel, "enter", [rows_low], [start, vectors[0][0]])[0]
    masked = exchange(cotangent * low(noised)[..., None])
    grad, d_branch_two = whole_call(top_kernel, "top", [rows_f32, rows_low], [masked, vectors[-1][0]])
    d_branch_other = swap_core(d_branch_two)
    kept, gathered = [], []
    for index in range(layers):
        vec, bias_core = vectors[index]
        joined = whole_attn(index, attn, [start, seg_q, seg_far] if index == 0 else [])
        normed_other = swap_core(normed)
        near, normed_chip = whole_call(
            lambda *refs: project_kernel(half, 3 * half, *refs), "keys_values",
            [((2 * tokens_here, 2 * half), jnp.bfloat16), chip_low], [normed, normed_other, joined],
        )
        far = swap_half(near)
        if index == 0:
            mlp_own = others(place, mlp_first, 0, [2 * rows_in], [near])[0]
        query = whole_call(
            lambda *refs: project_kernel(0, half, *refs), "queries",
            [((2 * tokens_here, half), jnp.bfloat16)], [normed, normed_other, joined],
        )[0]
        if index + 1 < layers:
            attn_own, next_mlp = next_pieces(index + 1, [query])
        att_own, att_send, heads_out, lse = attend(query, near, far, seg_q, seg_k, ())
        if index == 0:
            mlp = spread_late(mlp_own, att_own)
        hiddens, downs = whole_mlp(index, mlp)
        gathered.append((hiddens, downs))
        branch_one, middle, normed_two, attended = whole_call(
            middle_kernel, "middle", [rows_f32, rows_f32, rows_low, rows_low],
            [att_own, swap_core(att_send), joined, state, vec], place,
        )
        normed_two_other = swap_core(normed_two)
        after, due_far = [], []
        if index + 1 < layers:
            attn = spread(attn_own, "half")
            mlp = spread(others(place, next_mlp, 0, [2 * rows_in], [normed_two])[0], "half")
            after, due_far = [attn[1], attn[2], mlp[1]], [mlp[2]]
        elif layers > 1:
            after = [d_branch_other]
        act, slope, part_own, part_send, normed_two_chip = run_mlp(
            normed_two, normed_two_other, hiddens, downs, bias_core, after
        )
        ends = [part_own, swap_core(part_send), middle, vec]
        keep = [
            state, normed_chip, joined, query, near, far, heads_out, lse, attended,
            branch_one, middle, normed_two_chip, act, slope,
        ]
        if index == layers - 1:
            branch_two, final = whole_call(
                lambda *refs: leave_kernel(True, *refs), "leave", [rows_f32, rows_low], ends
            )
        else:
            branch_two, state, normed = whole_call(
                lambda *refs: leave_kernel(False, *refs), "leave", [rows_f32, rows_f32, rows_low],
                ends + [vectors[index + 1][0]], None, due_far,
            )
        kept.append(keep + [branch_two])

    def give_back(rows):
        mine, other = rows[: rows.shape[0] // 2], rows[rows.shape[0] // 2 :]
        arrived = swap_blk(other)
        return jnp.where(blk == 0, jnp.stack([mine, arrived]), jnp.stack([arrived, mine]))

    output = give_back(final)

    def reduce_part(terms, first_blk):
        if first_blk:
            first = swap_blk(pick(terms, 1 - blk, 1))
            kept_terms = low(wide(pick(terms, blk, 1)) + wide(first))
            second = swap_half(pick(kept_terms, 1 - side, 1))
            mine = pick(kept_terms, side, 1)
        else:
            first = swap_half(pick(terms, 1 - side, 2))
            kept_terms = low(wide(pick(terms, side, 2)) + wide(first))
            second = swap_blk(pick(kept_terms, 1 - blk, 1))
            mine = pick(kept_terms, blk, 1)
        return low(wide(mine) + wide(second)), first, second

    def reduce_plane(array, rows, first_blk):
        return reduce_part(array.reshape(shards, 2, 2, rows, array.shape[1]), first_blk)

    def reduce_split(array, rows):
        terms = array.reshape(shards, 2, 2, rows, array.shape[1])
        middle = shards // 2
        upper, _, upper_last = reduce_part(terms[:middle], True)
        lower, _, lower_last = reduce_part(terms[middle:], False)
        return jnp.concatenate([upper, lower], axis=0), (token(upper_last), token(lower_last))

    def scatter_shards(array):
        return lax.psum_scatter(array, "dp", scatter_dimension=0, tiled=False)

    def sum_shards(array):
        arrived = [
            from_shard(pick(array, (shard + ahead) % shards, 0), ahead, shards)
            for ahead in range(1, shards)
        ]
        return low(wide(pick(array, shard, 0)) + sum(wide(item) for item in arrived))

    sums_top = whole_call(
        top_sums_kernel, "top_sums", [((2, width), jnp.float32)], [grad, d_branch_two, kept[-1][-1]]
    )[0]
    small = [None] * layers
    shards_out = [None] * layers
    due = [()] * 5
    for index in reversed(range(layers)):
        vec, _ = vectors[index]
        hiddens, downs = gathered[index]
        (
            state_in, normed_chip, joined, query, near, far, heads_out, lse, attended,
            branch_one, middle, normed_two_chip, act, slope, _,
        ) = kept[index]
        if index < layers - 1:
            d_branch_other = swap_core(d_branch_two)
        d_pre, part_own, part_send, d_bias_core, d_branch_chip = run_mlp_back(
            d_branch_two, d_branch_other, slope, hiddens, downs, due[0]
        )
        d_down = low(left_product(act, d_branch_chip))
        d_hidden = low(left_product(normed_two_chip, d_pre))
        down_sum, down_first, down_second = reduce_plane(d_down, rows_down, False)
        hidden_sum, hidden_first, hidden_second = reduce_plane(d_hidden, rows_in, False)
        down_sum = jnp.concatenate([down_sum[:, :rows_in], down_sum[:, rows_in:]], axis=2)
        d_mlp_shard = scatter_shards(jnp.concatenate([hidden_sum, down_sum], axis=1))
        d_middle, d_one, d_att_own, d_att_send, sums_middle, _ = whole_call(
            middle_back_kernel, "middle_back",
            [rows_f32, rows_low, half_low, half_low, ((4, width), jnp.float32), rows_low],
            [grad, part_own, swap_core(part_send), middle, branch_one, vec, joined], place, due[1],
        )
        d_heads = (d_att_own, swap_core(d_att_send))
        d_query_far, d_far = attend_back(
            query, far, seg_q, seg_far_k, d_heads, heads_out, lse, None, due[2],
        )
        d_near = swap_half(d_far)
        d_out = low(left_product(attended, d_one))
        d_qkv = attend_back(
            query, near, seg_q, seg_near_k, d_heads, heads_out, lse, (d_query_far, d_near),
            due[3],
        )
        d_qkv_core = low(left_product(normed_chip, d_qkv))
        attn_sum, attn_first, attn_second = reduce_plane(
            jnp.concatenate([d_qkv_core, d_out], axis=1), rows_in, False
        )
        out_sum = attn_sum[:, :, 3 * half :]
        out_sum = low(
            wide(lax.dynamic_slice_in_dim(out_sum, core * half, half, 2))
            + wide(swap_core(lax.dynamic_slice_in_dim(out_sum, (1 - core) * half, half, 2)))
        )
        attn_sum = jnp.concatenate([attn_sum[:, :, : 3 * half], out_sum], axis=2)
        d_attn_shard = scatter_shards(attn_sum) if index > 0 else sum_shards(attn_sum)
        if index == 0:
            due_last = (token(attn_second),)
        part_own, part_send = whole_call(
            project_back_kernel, "project_back", [rows_f32, rows_low], [d_qkv, joined], None, due[4]
        )
        ends = [d_middle, part_own, swap_core(part_send), state_in, vec]
        sums_next = None
        if index == 0:
            sums_in, last_grad = whole_call(
                lambda *refs: enter_back_kernel(True, *refs), "enter_back",
                [((3, width), jnp.float32), rows_low], ends,
            )
        else:
            sums_in, grad, d_branch_two = whole_call(
                lambda *refs: enter_back_kernel(False, *refs), "enter_back",
                [((5, width), jnp.float32), rows_f32, rows_low],
                ends + [kept[index - 1][-1], vectors[index - 1][0]], None,
                (),
            )
            sums_next = sums_in[3:]
        d_units = d_bias_core.reshape(shards, 1, hidden_cut)
        d_units = jnp.concatenate(
            [jnp.where(core == 0, d_units, 0.0), jnp.where(core == 1, d_units, 0.0)], axis=1
        )
        d_modulation = jnp.concatenate(
            [sums_in[:2], sums_middle[3:4], sums_middle[:2], sums_top[:1]], axis=0
        )
        small[index] = jnp.concatenate(
            [
                d_modulation.reshape(shards, -1),
                sums_in[2].reshape(shards, -1),
                sums_middle[2].reshape(shards, -1),
                sums_top[1].reshape(shards, -1),
                d_units.reshape(shards, -1),
            ],
            axis=1,
        )
        shards_out[index] = (d_attn_shard, d_mlp_shard)
        sums_top = sums_next

    tokens_grad = give_back(last_grad)

    vector = jnp.stack(small)
    vector = vector + swap_core(vector)
    vector = vector + swap_half(vector)
    other = swap_blk(vector)
    mods, other_mods = vector[:, :, :ada_part], other[:, :, :ada_part]
    two = jnp.concatenate(
        [
            jnp.where(blk == 0, mods, other_mods),
            jnp.where(blk == 0, other_mods, mods),
            vector[:, :, ada_part:] + other[:, :, ada_part:],
        ],
        axis=2,
    ).transpose(1, 0, 2)
    arrived = [pick(two, shard, 0)]
    for ahead in range(1, shards):
        arrived.append(from_shard(pick(two, (shard + ahead) % shards, 0), ahead, shards))
    arrived = jnp.stack(arrived)
    totals = jnp.sum(arrived, axis=0)
    by_row = arrived[:, :, : 2 * ada_part].reshape(shards, layers, 2, ada_part)
    cond_rows = wide(conds).reshape(shards, 2, cond_width)
    cond_rows = jnp.stack([pick(cond_rows, (shard + shards - at) % shards, 0) for at in range(shards)])
    grad_ada = jnp.einsum(
        "slrm,src->lmc", by_row, cond_rows, precision=lax.Precision.HIGHEST
    )
    grad_ada_bias = totals[:, :ada_part] + totals[:, ada_part : 2 * ada_part]
    at = 2 * ada_part
    grad_gain_one = totals[:, at : at + part]
    grad_gain_two = totals[:, at + part : at + 2 * part]
    grad_bias_down = totals[:, at + 2 * part : at + 3 * part]
    grad_bias_hidden = totals[:, at + 3 * part :]

    def every_piece(piece):
        far, across = swap_blk(piece), swap_core(piece)
        mine = jnp.stack([piece, far, across, swap_core(far)])
        other = swap_half(mine)
        return (
            jnp.stack([mine[0], other[0], mine[1], other[1]]),
            jnp.stack([mine[2], other[2], mine[3], other[3]]),
        )

    shapes = {
        "attn": [(layers, part, 3 * width), (layers, part, width)],
        "mlp": [(layers, part, hidden), (layers, 2, 4, rows_down, width)],
    }
    grads = None
    for index in reversed(range(1, layers)):
        pieces = every_piece(hold(jnp.concatenate(shards_out[index], axis=0), *due_last))
        grads = finish(place, index, ("attn", "mlp"), pieces, shapes, half, rows_in, shards, grads)
    mlp_pieces = every_piece(shards_out[0][1])
    grad_hidden, grad_down = finish(
        place, 0, ("mlp",), mlp_pieces, shapes, half, rows_in, shards, grads and grads[2:]
    )
    attn_pieces = every_piece(shards_out[0][0])
    grad_qkv, grad_out = finish(
        place, 0, ("attn",), attn_pieces, shapes, half, rows_in, shards, grads and grads[:2]
    )
    grad_down = grad_down.reshape(layers, hidden_part, width)
    return (
        output,
        tokens_grad,
        grad_ada,
        grad_ada_bias,
        grad_gain_one,
        grad_qkv,
        grad_out,
        grad_gain_two,
        grad_hidden,
        grad_bias_hidden,
        grad_down,
        grad_bias_down,
    )


def pick_plan(mesh):
    def run(*arrays):
        tokens, first_gain, hidden_bias = arrays[0], arrays[7], arrays[12]
        fits = (
            mesh.shape["blk"] == 2
            and mesh.shape["uly"] == 4
            and tokens.shape[0] == 2
            and tokens.shape[1] % 64 == 0
            and tokens.shape[2] == HEADS * 64
            and HEADS % 4 == 0
            and first_gain.shape[1] % 64 == 0
            and hidden_bias.shape[1] % 256 == 0
        )
        return (local_paired if fits else local)(*arrays)

    return run


def solution(mesh):
    in_specs = (
        P("dp", ("blk", "uly"), None),
        P("dp", ("blk", "uly"), None),
        P("dp", ("blk", "uly")),
        P("dp", ("blk", "uly")),
        P("dp"),
        P(None, "dp", None),
        P(None, "dp"),
        P(None, "dp"),
        P(None, "dp", None),
        P(None, "dp", None),
        P(None, "dp"),
        P(None, "dp", None),
        P(None, "dp"),
        P(None, "dp", None),
        P(None, "dp"),
    )
    out_specs = (
        P("dp", ("blk", "uly"), None),
        P("dp", ("blk", "uly"), None),
        P(None, "dp", None),
        P(None, "dp"),
        P(None, "dp"),
        P(None, "dp", None),
        P(None, "dp", None),
        P(None, "dp"),
        P(None, "dp", None),
        P(None, "dp"),
        P(None, "dp", None),
        P(None, "dp"),
    )
    return jax.shard_map(pick_plan(mesh), mesh=mesh, in_specs=in_specs, out_specs=out_specs, check_vma=False)
```

```python
import math

import jax
import jax.numpy as jnp
from jax import lax
from jax.experimental import pallas as pl
from jax.experimental.pallas import tpu as pltpu
from jax.sharding import PartitionSpec as P

HEADS = 12


epsilon = 1e-05
neg_big = -1e30


def cond_vector(levels, width):
    half_width = width // 2
    freqs = jnp.exp(-math.log(10000.0) * jnp.arange(half_width, dtype=jnp.float32) / half_width)
    angles = levels.astype(jnp.float32)[:, None] * freqs[None, :]
    return jax.nn.silu(jnp.concatenate([jnp.cos(angles), jnp.sin(angles)], axis=-1))


def norm_mod(values, gain_vec, shift_vec, scale_vec):
    average = jnp.mean(values, axis=-1, keepdims=True)
    centered = values - average
    variance = jnp.mean(centered * centered, axis=-1, keepdims=True)
    return centered * lax.rsqrt(variance + epsilon) * gain_vec * (1.0 + scale_vec) + shift_vec


def gelu_tanh(values):
    return jax.nn.gelu(values, approximate=True)


def left_product(first, second):
    return lax.dot_general(
        first, second, (((0,), (0,)), ((), ())), preferred_element_type=jnp.float32
    )


def right_product(first, second):
    return lax.dot_general(
        first, second, (((1,), (1,)), ((), ())), preferred_element_type=jnp.float32
    )


def fetch(params, layer_index):
    p_ada, p_bias, p_gain, p_qkv, p_out, p_gain_two, p_hidden, p_hbias, p_down, p_dbias = params
    return (
        lax.all_gather(p_ada[layer_index], "dp", axis=0, tiled=True),
        lax.all_gather(p_bias[layer_index], "dp", axis=0, tiled=True),
        lax.all_gather(p_gain[layer_index], "dp", axis=0, tiled=True),
        lax.all_gather(p_qkv[layer_index], "dp", axis=0, tiled=True),
        lax.all_gather(p_out[layer_index], "dp", axis=0, tiled=True),
        lax.all_gather(p_gain_two[layer_index], "dp", axis=0, tiled=True),
        lax.all_gather(p_hidden[layer_index], "dp", axis=0, tiled=True),
        lax.all_gather(p_hbias[layer_index], "dp", axis=0, tiled=True),
        lax.all_gather(p_down[layer_index], "dp", axis=0, tiled=True),
        lax.all_gather(p_dbias[layer_index], "dp", axis=0, tiled=True),
    )


def reduce_grads(grads):
    shards = (
        lax.psum_scatter(
            grads[0].astype(jnp.bfloat16), "dp", scatter_dimension=0, tiled=True
        ).astype(jnp.float32),
        lax.psum_scatter(
            grads[1].astype(jnp.bfloat16), "dp", scatter_dimension=0, tiled=True
        ).astype(jnp.float32),
        lax.psum_scatter(
            grads[2].astype(jnp.bfloat16), "dp", scatter_dimension=0, tiled=True
        ).astype(jnp.float32),
        lax.psum_scatter(
            grads[3].astype(jnp.bfloat16), "dp", scatter_dimension=0, tiled=True
        ).astype(jnp.float32),
        lax.psum_scatter(
            grads[4].astype(jnp.bfloat16), "dp", scatter_dimension=0, tiled=True
        ).astype(jnp.float32),
        lax.psum_scatter(
            grads[5].astype(jnp.bfloat16), "dp", scatter_dimension=0, tiled=True
        ).astype(jnp.float32),
        lax.psum_scatter(
            grads[6].astype(jnp.bfloat16), "dp", scatter_dimension=0, tiled=True
        ).astype(jnp.float32),
        lax.psum_scatter(
            grads[7].astype(jnp.bfloat16), "dp", scatter_dimension=0, tiled=True
        ).astype(jnp.float32),
        lax.psum_scatter(
            grads[8].astype(jnp.bfloat16), "dp", scatter_dimension=0, tiled=True
        ).astype(jnp.float32),
        lax.psum_scatter(
            grads[9].astype(jnp.bfloat16), "dp", scatter_dimension=0, tiled=True
        ).astype(jnp.float32),
    )
    return (
        lax.psum(shards[0].astype(jnp.bfloat16), ("blk", "uly")).astype(jnp.float32),
        lax.psum(shards[1].astype(jnp.bfloat16), ("blk", "uly")).astype(jnp.float32),
        lax.psum(shards[2].astype(jnp.bfloat16), ("blk", "uly")).astype(jnp.float32),
        lax.psum(shards[3].astype(jnp.bfloat16), ("blk", "uly")).astype(jnp.float32),
        lax.psum(shards[4].astype(jnp.bfloat16), ("blk", "uly")).astype(jnp.float32),
        lax.psum(shards[5].astype(jnp.bfloat16), ("blk", "uly")).astype(jnp.float32),
        lax.psum(shards[6].astype(jnp.bfloat16), ("blk", "uly")).astype(jnp.float32),
        lax.psum(shards[7].astype(jnp.bfloat16), ("blk", "uly")).astype(jnp.float32),
        lax.psum(shards[8].astype(jnp.bfloat16), ("blk", "uly")).astype(jnp.float32),
        lax.psum(shards[9].astype(jnp.bfloat16), ("blk", "uly")).astype(jnp.float32),
    )


def over_blocks(block_fn, carry, key_piece, value_piece, seg_piece):
    count = key_piece.shape[2]
    size = 512

    def block_step(inner, position):
        offset = position * size
        key_blk = lax.dynamic_slice_in_dim(key_piece, offset, size, 2)
        value_blk = lax.dynamic_slice_in_dim(value_piece, offset, size, 2)
        seg_blk = lax.dynamic_slice_in_dim(seg_piece, offset, size, 0)
        return (block_fn(inner, key_blk, value_blk, seg_blk, offset), None)

    return lax.scan(block_step, carry, jnp.arange(count // size, dtype=jnp.int32))[0]


def split_heads(qkv_b):
    tokens_dev = qkv_b.shape[0]
    width = qkv_b.shape[1] // 3
    heads_all = lax.all_to_all(
        qkv_b.reshape(tokens_dev, 3, width), "uly", split_axis=2, concat_axis=0, tiled=True
    )
    span = heads_all.shape[0]
    head_dim = width // HEADS
    local_heads = heads_all.shape[2] // head_dim
    layout = heads_all.reshape(span, 3, local_heads, head_dim).transpose(1, 2, 3, 0)
    return (layout[0], layout[1], layout[2])


def layer_forward(state, weights_now, cond_b, seg_row):
    (
        ada_weight,
        ada_bias,
        first_gain,
        qkv_weight,
        out_weight,
        second_gain,
        hidden_weight,
        hidden_bias,
        down_weight,
        down_bias,
    ) = weights_now
    modulation = jnp.dot(ada_weight, cond_b, preferred_element_type=jnp.float32) + ada_bias.astype(
        jnp.float32
    )
    shift_one, scale_one, gate_one, shift_two, scale_two, gate_two = jnp.split(modulation, 6)
    normed_b = norm_mod(state, first_gain.astype(jnp.float32), shift_one, scale_one).astype(
        jnp.bfloat16
    )
    qkv_b = jnp.dot(normed_b, qkv_weight, preferred_element_type=jnp.float32).astype(jnp.bfloat16)
    query_t, key_t, value_t = split_heads(qkv_b)
    local_heads, head_dim, span = query_t.shape
    factor = head_dim ** (-0.5)
    query_seg = lax.dynamic_slice_in_dim(seg_row, lax.axis_index("blk") * span, span, 0)

    def forward_block(carry, key_blk, value_blk, seg_blk, start):
        running_max, running_total, weighted = carry
        scores = (
            jnp.einsum("hdq,hdk->hqk", query_t, key_blk, preferred_element_type=jnp.float32)
            * factor
        )
        allowed = (query_seg[:, None] == seg_blk[None, :])[None]
        masked = jnp.where(allowed, scores, neg_big)
        new_max = jnp.maximum(running_max, jnp.max(masked, axis=-1))
        probabilities = jnp.where(allowed, jnp.exp(masked - new_max[..., None]), 0.0)
        rescale = jnp.exp(running_max - new_max)
        running_total = running_total * rescale + jnp.sum(probabilities, axis=-1)
        update = jnp.einsum(
            "hqk,hdk->hdq",
            probabilities.astype(jnp.bfloat16),
            value_blk,
            preferred_element_type=jnp.float32,
        )
        weighted = weighted * rescale[:, None, :] + update
        return (new_max, running_total, weighted)

    initial = (
        jnp.full((local_heads, span), neg_big, jnp.float32),
        jnp.zeros((local_heads, span), jnp.float32),
        jnp.zeros((local_heads, head_dim, span), jnp.float32),
    )
    running_max, running_total, weighted = over_blocks(
        forward_block,
        initial,
        lax.all_gather(key_t, "blk", axis=2, tiled=True),
        lax.all_gather(value_t, "blk", axis=2, tiled=True),
        seg_row,
    )
    attended_heads = weighted / running_total[:, None, :]
    log_total = running_max + jnp.log(running_total)
    sendable = (
        attended_heads.astype(jnp.bfloat16).transpose(2, 0, 1).reshape(span, local_heads * head_dim)
    )
    attended_b = lax.all_to_all(sendable, "uly", split_axis=0, concat_axis=1, tiled=True)
    branch_one = jnp.dot(attended_b, out_weight, preferred_element_type=jnp.float32)
    middle = state + gate_one * branch_one
    normed_two = norm_mod(middle, second_gain.astype(jnp.float32), shift_two, scale_two).astype(
        jnp.bfloat16
    )
    hidden_pre = jnp.dot(
        normed_two, hidden_weight, preferred_element_type=jnp.float32
    ) + hidden_bias.astype(jnp.float32)
    activated = gelu_tanh(hidden_pre).astype(jnp.bfloat16)
    branch_two = jnp.dot(
        activated, down_weight, preferred_element_type=jnp.float32
    ) + down_bias.astype(jnp.float32)
    result = middle + gate_two * branch_two
    kept = (
        state,
        modulation,
        normed_b,
        query_t,
        key_t,
        value_t,
        attended_heads,
        log_total,
        attended_b,
        branch_one,
        middle,
        normed_two,
        hidden_pre,
        activated,
        branch_two,
    )
    return (result, kept)


def layer_backward(grad, weights_now, kept, cond_b, seg_row):
    (
        ada_weight,
        ada_bias,
        first_gain,
        qkv_weight,
        out_weight,
        second_gain,
        hidden_weight,
        hidden_bias,
        down_weight,
        down_bias,
    ) = weights_now
    (
        state,
        modulation,
        normed_b,
        query_t,
        key_t,
        value_t,
        attended_heads,
        log_total,
        attended_b,
        branch_one,
        middle,
        normed_two,
        hidden_pre,
        activated,
        branch_two,
    ) = kept
    shift_one, scale_one, gate_one, shift_two, scale_two, gate_two = jnp.split(modulation, 6)
    gain_one = first_gain.astype(jnp.float32)
    gain_two = second_gain.astype(jnp.float32)
    d_gate_two = jnp.sum(grad * branch_two, axis=0)
    d_branch_two = (gate_two * grad).astype(jnp.bfloat16)
    d_down_weight = left_product(activated, d_branch_two)
    d_down_bias = jnp.sum(d_branch_two.astype(jnp.float32), axis=0)
    d_activated = right_product(d_branch_two, down_weight)
    gelu_back = jax.vjp(gelu_tanh, hidden_pre)[1]
    d_pre = gelu_back(d_activated)[0].astype(jnp.bfloat16)
    d_hidden_weight = left_product(normed_two, d_pre)
    d_hidden_bias = jnp.sum(d_pre.astype(jnp.float32), axis=0)
    d_normed_two = right_product(d_pre, hidden_weight)
    norm_back_two = jax.vjp(norm_mod, middle, gain_two, shift_two, scale_two)[1]
    d_middle_part, d_gain_two, d_shift_two, d_scale_two = norm_back_two(d_normed_two)
    d_middle = grad + d_middle_part
    d_gate_one = jnp.sum(d_middle * branch_one, axis=0)
    d_branch_one = (gate_one * d_middle).astype(jnp.bfloat16)
    d_out_weight = left_product(attended_b, d_branch_one)
    d_attended_b = right_product(d_branch_one, out_weight).astype(jnp.bfloat16)
    local_heads, head_dim, span = query_t.shape
    factor = head_dim ** (-0.5)
    d_heads_t = (
        lax.all_to_all(d_attended_b, "uly", split_axis=1, concat_axis=0, tiled=True)
        .reshape(span, local_heads, head_dim)
        .transpose(1, 2, 0)
    )
    row_delta = jnp.sum(d_heads_t.astype(jnp.float32) * attended_heads, axis=1)
    query_seg = lax.dynamic_slice_in_dim(seg_row, lax.axis_index("blk") * span, span, 0)

    def backward_block(carry, key_blk, value_blk, seg_blk, start):
        d_query, d_key_all, d_value_all = carry
        scores = (
            jnp.einsum("hdq,hdk->hqk", query_t, key_blk, preferred_element_type=jnp.float32)
            * factor
        )
        allowed = (query_seg[:, None] == seg_blk[None, :])[None]
        probabilities = jnp.where(allowed, jnp.exp(scores - log_total[..., None]), 0.0)
        d_probs = jnp.einsum(
            "hdq,hdk->hqk", d_heads_t, value_blk, preferred_element_type=jnp.float32
        )
        d_scores = (probabilities * (d_probs - row_delta[..., None])).astype(jnp.bfloat16)
        d_query = (
            d_query
            + jnp.einsum("hqk,hdk->hdq", d_scores, key_blk, preferred_element_type=jnp.float32)
            * factor
        )
        d_key_new = (
            jnp.einsum("hqk,hdq->hdk", d_scores, query_t, preferred_element_type=jnp.float32)
            * factor
        )
        d_value_new = jnp.einsum(
            "hqk,hdq->hdk",
            probabilities.astype(jnp.bfloat16),
            d_heads_t,
            preferred_element_type=jnp.float32,
        )
        size = key_blk.shape[2]
        d_key_all = lax.dynamic_update_slice_in_dim(
            d_key_all, lax.dynamic_slice_in_dim(d_key_all, start, size, 2) + d_key_new, start, 2
        )
        d_value_all = lax.dynamic_update_slice_in_dim(
            d_value_all,
            lax.dynamic_slice_in_dim(d_value_all, start, size, 2) + d_value_new,
            start,
            2,
        )
        return (d_query, d_key_all, d_value_all)

    row_len = seg_row.shape[0]
    initial = (
        jnp.zeros((local_heads, head_dim, span), jnp.float32),
        jnp.zeros((local_heads, head_dim, row_len), jnp.float32),
        jnp.zeros((local_heads, head_dim, row_len), jnp.float32),
    )
    d_query, d_key_all, d_value_all = over_blocks(
        backward_block,
        initial,
        lax.all_gather(key_t, "blk", axis=2, tiled=True),
        lax.all_gather(value_t, "blk", axis=2, tiled=True),
        seg_row,
    )
    d_key, d_value = (
        lax.psum_scatter(
            d_key_all.astype(jnp.bfloat16), "blk", scatter_dimension=2, tiled=True
        ).astype(jnp.float32),
        lax.psum_scatter(
            d_value_all.astype(jnp.bfloat16), "blk", scatter_dimension=2, tiled=True
        ).astype(jnp.float32),
    )
    joined = jnp.stack([d_query, d_key, d_value], axis=0).astype(jnp.bfloat16)
    stacked = joined.transpose(3, 0, 1, 2).reshape(span, 3, local_heads * head_dim)
    returned = lax.all_to_all(stacked, "uly", split_axis=0, concat_axis=2, tiled=True)
    tokens_dev = state.shape[0]
    d_qkv_b = returned.reshape(tokens_dev, returned.shape[1] * returned.shape[2])
    d_qkv_weight = left_product(normed_b, d_qkv_b)
    d_normed = right_product(d_qkv_b, qkv_weight)
    norm_back_one = jax.vjp(norm_mod, state, gain_one, shift_one, scale_one)[1]
    d_state_part, d_gain_one, d_shift_one, d_scale_one = norm_back_one(d_normed)
    d_state = d_middle + d_state_part
    d_modulation = jnp.concatenate(
        [d_shift_one, d_scale_one, d_gate_one, d_shift_two, d_scale_two, d_gate_two]
    )
    d_ada_weight = d_modulation[:, None] * cond_b.astype(jnp.float32)[None, :]
    grads = (
        d_ada_weight,
        d_modulation,
        d_gain_one,
        d_qkv_weight,
        d_out_weight,
        d_gain_two,
        d_hidden_weight,
        d_hidden_bias,
        d_down_weight,
        d_down_bias,
    )
    return (d_state, grads)


def add_tuples(first, second):
    if first is None:
        return second
    return tuple((left_item + right_item for left_item, right_item in zip(first, second)))


def local(
    tokens,
    cotangent,
    segments,
    noised,
    levels,
    ada_weight,
    ada_bias,
    first_gain,
    qkv_weight,
    out_weight,
    second_gain,
    hidden_weight,
    hidden_bias,
    down_weight,
    down_bias,
):
    params = (
        ada_weight,
        ada_bias,
        first_gain,
        qkv_weight,
        out_weight,
        second_gain,
        hidden_weight,
        hidden_bias,
        down_weight,
        down_bias,
    )
    layers = ada_weight.shape[0]
    batches = tokens.shape[0]
    row_segs = lax.all_gather(segments, ("blk", "uly"), axis=1, tiled=True)
    conds = cond_vector(levels, ada_weight.shape[2]).astype(jnp.bfloat16)
    stored = [fetch(params, layer_index) for layer_index in range(layers)]
    sums = [None] * layers
    outputs = []
    input_grads = []
    for batch_index in range(batches):
        state = tokens[batch_index].astype(jnp.float32)
        cond_b = conds[batch_index]
        seg_row = row_segs[batch_index]
        kept_all = []
        for layer_index in range(layers):
            weights_now = stored[layer_index]
            state, kept = layer_forward(state, weights_now, cond_b, seg_row)
            kept_all.append(kept)
        outputs.append(state.astype(jnp.bfloat16))
        grad = (
            cotangent[batch_index].astype(jnp.float32)
            * noised[batch_index].astype(jnp.float32)[:, None]
        )
        for layer_index in reversed(range(layers)):
            weights_now = stored[layer_index]
            grad, grads = layer_backward(grad, weights_now, kept_all[layer_index], cond_b, seg_row)
            sums[layer_index] = add_tuples(sums[layer_index], reduce_grads(grads))
        input_grads.append(grad.astype(jnp.bfloat16))
    stacked = [
        jnp.stack([sums[layer_index][member] for layer_index in range(layers)])
        for member in range(10)
    ]
    return (
        jnp.stack(outputs),
        jnp.stack(input_grads),
        stacked[0],
        stacked[1],
        stacked[2],
        stacked[3],
        stacked[4],
        stacked[5],
        stacked[6],
        stacked[7],
        stacked[8],
        stacked[9],
    )


SWAP = [(0, 1), (1, 0)]
PAIR = [(0, 1), (1, 0), (2, 3), (3, 2)]
ACROSS = [(0, 2), (2, 0), (1, 3), (3, 1)]
VMEM_BYTES = 16 * 1024 * 1024
COPY_BYTES = 12 * 1024 * 1024
FREE = pl.CostEstimate(flops=0, bytes_accessed=0, transcendentals=0)
COPIES = pl.CostEstimate(flops=0, bytes_accessed=7_000_000, transcendentals=0)


def swap_blk(value):
    return lax.ppermute(value, "blk", SWAP)


def swap_half(value):
    return lax.ppermute(value, "uly", PAIR)


def swap_core(value):
    return lax.ppermute(value, "uly", ACROSS)


def from_shard(value, back, shards):
    return lax.ppermute(value, "dp", [(at, (at + back) % shards) for at in range(shards)])


def plain_product(first, second):
    return jnp.dot(first, second, preferred_element_type=jnp.float32)


def normalise(values):
    average = jnp.mean(values, axis=-1, keepdims=True)
    centered = values - average
    variance = jnp.mean(centered * centered, axis=-1, keepdims=True)
    inverse = lax.rsqrt(variance + epsilon)
    return centered * inverse, inverse


def pick(array, index, axis):
    return lax.dynamic_index_in_dim(array, index, axis, keepdims=False)


def low(value):
    return value.astype(jnp.bfloat16)


def wide(value):
    return value.astype(jnp.float32)


def token(array):
    while array.ndim > 2:
        array = array[0]
    return array[:16, :128]


def whole_call(kernel, name, shapes, operands, place=None, after=()):
    specs = [] if place is None else [pl.BlockSpec(memory_space=pltpu.SMEM)]
    specs += [pl.BlockSpec(memory_space=pltpu.VMEM)] * len(operands)
    specs += [pl.BlockSpec(memory_space=pl.ANY)] * len(after)
    count = len(operands) + (place is not None)

    def body(*refs):
        kernel(*refs[:count], *refs[count + len(after) :])

    return pl.pallas_call(
        body,
        out_shape=tuple(jax.ShapeDtypeStruct(shape, kind) for shape, kind in shapes),
        in_specs=specs,
        out_specs=(pl.BlockSpec(memory_space=pltpu.VMEM),) * len(shapes),
        compiler_params=pltpu.CompilerParams(vmem_limit_bytes=VMEM_BYTES),
        cost_estimate=FREE,
        name=name,
    )(*([] if place is None else [place]), *operands, *after)


def hold(value, *after):
    return pl.pallas_call(
        lambda *refs: None,
        out_shape=jax.ShapeDtypeStruct(value.shape, value.dtype),
        in_specs=[pl.BlockSpec(memory_space=pl.ANY)] * (1 + len(after)),
        out_specs=pl.BlockSpec(memory_space=pl.ANY),
        input_output_aliases={0: 0},
        cost_estimate=FREE,
        name="hold",
    )(value, *after)


def run_copies(pairs, sems):
    copies = [
        pltpu.make_async_copy(source, target, sems.at[number])
        for number, (source, target) in enumerate(pairs)
    ]
    for copy in copies:
        copy.start()
    for copy in copies:
        copy.wait()


def attn_pairs(sizes, layer, rows, core, qkv_ref, target_ref):
    rows_in, rows_down, half, hidden_cut, shards = sizes
    lanes = pl.multiple_of(core * half, 128)
    pairs = [
        (
            qkv_ref.at[layer, rows, pl.ds(kind * 2 * half + lanes, half)],
            target_ref.at[:, pl.ds(kind * half, half)],
        )
        for kind in range(3)
    ]
    return pairs


def hidden_pairs(sizes, layer, rows, core, hidden_ref, target_ref):
    rows_in, rows_down, half, hidden_cut, shards = sizes
    lanes = pl.multiple_of(core * hidden_cut, 128)
    return [
        (
            hidden_ref.at[layer, rows, pl.ds(at * 2 * hidden_cut + lanes, hidden_cut)],
            target_ref.at[:, pl.ds(at * hidden_cut, hidden_cut)],
        )
        for at in range(shards)
    ]


def down_pairs(sizes, layer, place_ref, down_ref, target_ref):
    rows_in, rows_down, half, hidden_cut, shards = sizes
    first = pl.multiple_of(place_ref[2] * hidden_cut + place_ref[1] * rows_down, 16)
    return [
        (
            down_ref.at[layer, pl.ds(first + side * rows_in, rows_in)],
            target_ref.at[:, pl.ds(side * 2 * half, 2 * half)],
        )
        for side in range(2)
    ]


def mlp_pairs(sizes, layer, place_ref, out_ref, hidden_ref, down_ref, target_ref):
    rows_in, rows_down, half, hidden_cut, shards = sizes
    rows = pl.ds(pl.multiple_of(place_ref[1] * rows_in, 16), rows_in)
    above, below = target_ref.at[pl.ds(0, rows_in)], target_ref.at[pl.ds(rows_in, rows_in)]
    pairs = hidden_pairs(sizes, layer, rows, place_ref[2], hidden_ref, above)
    pairs += down_pairs(sizes, layer, place_ref, down_ref, below)
    for number, part_ref in enumerate((above, below)):
        pairs.append(
            (out_ref.at[layer, rows, pl.ds(number * half, half)], part_ref.at[:, pl.ds(4 * half, half)])
        )
    return pairs


def cut_attn_kernel(sizes, layer, place_ref, qkv_ref, *refs):
    piece_ref, sems = refs[-2:]
    rows = pl.ds(pl.multiple_of(place_ref[1] * sizes[0], 16), sizes[0])
    run_copies(attn_pairs(sizes, layer, rows, place_ref[2], qkv_ref, piece_ref), sems)


def cut_mlp_kernel(sizes, layer, place_ref, out_ref, hidden_ref, down_ref, *refs):
    piece_ref, sems = refs[-2:]
    run_copies(mlp_pairs(sizes, layer, place_ref, out_ref, hidden_ref, down_ref, piece_ref), sems)


def cut_next_kernel(sizes, layer, place_ref, qkv_ref, out_ref, hidden_ref, down_ref, *refs):
    piece_ref, sems = refs[-2:]
    rows_in, rows_down, half, hidden_cut, shards = sizes
    rows = pl.ds(pl.multiple_of(place_ref[1] * rows_in, 16), rows_in)
    pairs = mlp_pairs(
        sizes, layer, place_ref, out_ref, hidden_ref, down_ref, piece_ref.at[pl.ds(0, 2 * rows_in)]
    )
    pairs += attn_pairs(
        sizes, layer, rows, place_ref[2], qkv_ref,
        piece_ref.at[pl.ds(2 * rows_in, rows_in), pl.ds(0, 3 * half)],
    )
    piece_ref[2 * rows_in :, 3 * half :] = jnp.zeros((rows_in, 2 * half), piece_ref.dtype)
    run_copies(pairs, sems)


def others_kernel(cuts, place_ref, all_ref, *refs):
    outs, sems = refs[-1 - len(cuts) : -1], refs[-1]
    shards = all_ref.shape[0]
    pairs = []
    for (first, rows, columns), out_ref in zip(cuts, outs):
        for back in range(1, shards):
            source = all_ref.at[
                lax.rem(place_ref[0] + shards - back, shards), pl.ds(first, rows), pl.ds(0, columns)
            ]
            pairs.append((source, out_ref.at[back - 1]))
    run_copies(pairs, sems)


def others(place, whole, cuts, after=()):
    shards = whole.shape[0]
    return copy_call(
        lambda *refs: others_kernel(cuts, *refs), "others", place, [whole],
        [(shards - 1, rows, columns) for _, rows, columns in cuts], len(cuts) * (shards - 1), after,
    )


def copy_call(kernel, name, place, operands, shapes, count, after=(), keep=False):
    kind = operands[0].dtype
    return pl.pallas_call(
        kernel,
        out_shape=tuple(
            pltpu.VMEM(shape, kind) if keep else jax.ShapeDtypeStruct(shape, kind) for shape in shapes
        ),
        in_specs=[pl.BlockSpec(memory_space=pltpu.SMEM)]
        + [pl.BlockSpec(memory_space=pl.ANY)] * len(operands)
        + [pl.BlockSpec(memory_space=pl.ANY)] * len(after),
        out_specs=(pl.BlockSpec(memory_space=pltpu.VMEM),) * len(shapes),
        scratch_shapes=[pltpu.SemaphoreType.DMA((count,))],
        compiler_params=pltpu.CompilerParams(vmem_limit_bytes=COPY_BYTES),
        cost_estimate=COPIES,
        name=name,
    )(place, *operands, *after)


def join_attn_kernel(sizes, layer, place_ref, qkv_ref, *refs):
    pieces, whole_ref, sems = refs[:4], refs[-2], refs[-1]
    rows_in, shards = sizes[0], sizes[-1]
    shard, quarter = place_ref[0], place_ref[1]
    pairs = attn_pairs(sizes, layer, slice(None), place_ref[2], qkv_ref, whole_ref.at[shard])
    for relative, piece_ref in enumerate(pieces):
        rows = pl.ds(pl.multiple_of((quarter ^ relative) * rows_in, 16), rows_in)
        for back in range(1, shards):
            target = whole_ref.at[lax.rem(shard + shards - back, shards), rows]
            pairs.append((piece_ref.at[back - 1], target))
    run_copies(pairs, sems)


def join_mlp_kernel(sizes, layer, place_ref, out_ref, hidden_ref, down_ref, *refs):
    pieces = refs[:4]
    whole_o_ref, whole_h_ref, whole_d_ref, sems = refs[-4:]
    rows_in, rows_down, half, hidden_cut, shards = sizes
    shard, quarter, core = place_ref[0], place_ref[1], place_ref[2]
    pairs = hidden_pairs(sizes, layer, slice(None), core, hidden_ref, whole_h_ref.at[shard])
    first = pl.multiple_of(core * hidden_cut, 128)
    pairs.append((down_ref.at[layer, pl.ds(first, hidden_cut)], whole_d_ref.at[shard]))
    pairs.append((out_ref.at[layer], whole_o_ref.at[shard]))
    for relative in range(4):
        at_h = pl.multiple_of((quarter ^ relative) * rows_in, 16)
        at_d = pl.multiple_of((quarter ^ relative) * rows_down, 16)
        for back in range(1, shards):
            place = lax.rem(shard + shards - back, shards)
            above = pieces[relative].at[back - 1, pl.ds(0, rows_in)]
            below = pieces[relative].at[back - 1, pl.ds(rows_in, rows_in)]
            pairs.append(
                (above.at[:, pl.ds(0, 4 * half)], whole_h_ref.at[place, pl.ds(at_h, rows_in)])
            )
            for number, part in enumerate((above, below)):
                pairs.append(
                    (
                        below.at[:, pl.ds(number * 2 * half, 2 * half)],
                        whole_d_ref.at[place, pl.ds(at_d + number * rows_in, rows_in)],
                    )
                )
                pairs.append(
                    (
                        part.at[:, pl.ds(4 * half, half)],
                        whole_o_ref.at[place, pl.ds(at_h, rows_in), pl.ds(number * half, half)],
                    )
                )
    run_copies(pairs, sems)


def finish_attn_part(owner, half, rows, piece, qkv_ref, out_ref):
    width = 2 * half
    lanes = pl.multiple_of(owner * half, 128)
    for kind in range(3):
        qkv_ref[0, :, pl.ds(kind * width + lanes, half)] = wide(
            piece[0, :rows, kind * half : (kind + 1) * half]
        )
    out_ref[0, :, pl.ds(lanes, half)] = wide(piece[0, :rows, 3 * half :])


def finish_mlp_part(owner, half, rows, shards, start, piece, hidden_ref, down_ref):
    width = 2 * half
    hidden_cut = hidden_ref.shape[2] // (2 * shards)
    lanes = pl.multiple_of(owner * hidden_cut, 128)
    for at in range(shards):
        hidden_ref[0, :, pl.ds(at * 2 * hidden_cut + lanes, hidden_cut)] = wide(
            piece[0, start : start + rows, at * hidden_cut : (at + 1) * hidden_cut]
        )
    for side in range(2):
        down_ref[0, owner, 0, side * rows : (side + 1) * rows] = wide(
            piece[0, start + rows :, side * width : (side + 1) * width]
        )


def finish_kernel(parts, half, rows, shards, place_ref, *refs):
    outs = refs[len(refs) - 2 * len(parts) :]
    for relative in range(2):
        owner, at = place_ref[2] ^ relative, 0
        for number, part in enumerate(parts):
            if part == "attn":
                finish_attn_part(owner, half, rows, refs[relative], *outs[2 * number : 2 * number + 2])
                at += rows
            else:
                finish_mlp_part(
                    owner, half, rows, shards, at, refs[relative], *outs[2 * number : 2 * number + 2]
                )


def finish(place, layer, parts, pieces, shapes, half, rows, shards, before=None):
    width = 2 * half
    blocks = {
        "attn": [
            pl.BlockSpec((1, rows, 3 * width), lambda at, place: (layer, place[1] ^ at, 0)),
            pl.BlockSpec((1, rows, width), lambda at, place: (layer, place[1] ^ at, 0)),
        ],
        "mlp": [
            pl.BlockSpec((1, rows, shapes["mlp"][0][2]), lambda at, place: (layer, place[1] ^ at, 0)),
            pl.BlockSpec(
                (1, 2, 1, 2 * rows, width), lambda at, place: (layer, 0, place[1] ^ at, 0, 0)
            ),
        ],
    }
    operands, aliases = list(pieces), {}
    specs = [pl.BlockSpec((1, *piece.shape[1:]), lambda at, place: (at, 0, 0)) for piece in pieces]
    if before is not None:
        operands += list(before)
        specs += [pl.BlockSpec(memory_space=pl.ANY)] * len(before)
        aliases = {3 + number: number for number in range(len(before))}
    return pl.pallas_call(
        lambda *refs: finish_kernel(parts, half, rows, shards, *refs),
        grid_spec=pltpu.PrefetchScalarGridSpec(
            num_scalar_prefetch=1,
            grid=(4,),
            in_specs=specs,
            out_specs=tuple(block for part in parts for block in blocks[part]),
        ),
        out_shape=tuple(
            jax.ShapeDtypeStruct(shape, jnp.float32) for part in parts for shape in shapes[part]
        ),
        input_output_aliases=aliases,
        compiler_params=pltpu.CompilerParams(vmem_limit_bytes=VMEM_BYTES),
        cost_estimate=COPIES,
        name="finish",
    )(place, *operands)


TILE = 256
SHIFT_ONE, SCALE_ONE, GATE_ONE, SHIFT_TWO, SCALE_TWO, GATE_TWO, GAIN_ONE, GAIN_TWO, BIAS_DOWN = range(9)


def row_of(ref, number):
    return ref[number : number + 1, :]


def norm_rows(values, vec_ref, gain, scale, shift):
    unit_values, _ = normalise(values)
    return low(
        unit_values * row_of(vec_ref, gain) * (1.0 + row_of(vec_ref, scale)) + row_of(vec_ref, shift)
    )


def enter_kernel(x_ref, vec_ref, n_ref):
    n_ref[...] = norm_rows(wide(x_ref[...]), vec_ref, GAIN_ONE, SCALE_ONE, SHIFT_ONE)


def project_kernel(first, last, own_ref, other_ref, weight_ref, out_ref, *refs):
    count = own_ref.shape[0]
    for chip_ref in refs:
        chip_ref[:count, :] = own_ref[...]
        chip_ref[count:, :] = other_ref[...]
    out_ref[:count, :] = low(plain_product(own_ref[...], weight_ref[:, first:last]))
    out_ref[count:, :] = low(plain_product(other_ref[...], weight_ref[:, first:last]))


def middle_kernel(
    place_ref, att_own_ref, att_other_ref, weight_ref, state_ref, vec_ref, branch_ref, middle_ref, n_ref, att_ref
):
    half = att_own_ref.shape[1]
    att_ref[:, pl.ds(pl.multiple_of(place_ref[2] * half, 128), half)] = att_own_ref[...]
    att_ref[:, pl.ds(pl.multiple_of((1 - place_ref[2]) * half, 128), half)] = att_other_ref[...]
    branch = plain_product(att_ref[...], weight_ref[...])
    middle = state_ref[...] + row_of(vec_ref, GATE_ONE) * branch
    branch_ref[...] = low(branch)
    middle_ref[...] = middle
    n_ref[...] = norm_rows(middle, vec_ref, GAIN_TWO, SCALE_TWO, SHIFT_TWO)


def chunk_call(kernel, name, grid, operands, specs, shapes, out_specs, scratch, after=(), far=()):
    first_out = len(operands)
    return pl.pallas_call(
        lambda *refs: kernel(*refs[:first_out], *refs[first_out + len(after) :]),
        grid=(grid,),
        out_shape=tuple(
            pltpu.HBM(shape, kind) if number in far else jax.ShapeDtypeStruct(shape, kind)
            for number, (shape, kind) in enumerate(shapes)
        ),
        in_specs=list(specs) + [pl.BlockSpec(memory_space=pl.ANY)] * len(after),
        out_specs=tuple(out_specs),
        scratch_shapes=scratch,
        compiler_params=pltpu.CompilerParams(vmem_limit_bytes=VMEM_BYTES),
        cost_estimate=FREE,
        name=name,
    )(*operands, *after)


def sent_and_kept(total_ref, part_ref, send_ref):
    @pl.when(pl.program_id(0) == pl.num_programs(0) - 1)
    def _():
        count = part_ref.shape[0]
        part_ref[...] = total_ref[:count, :]
        send_ref[...] = low(total_ref[count:, :])


def take_both(own_ref, other_ref, chip_ref):
    @pl.when(pl.program_id(0) == 0)
    def _():
        count = own_ref.shape[0]
        chip_ref[:count, :] = own_ref[...]
        chip_ref[count:, :] = other_ref[...]


def add_up(total_ref, term):
    @pl.when(pl.program_id(0) == 0)
    def _():
        total_ref[...] = term

    @pl.when(pl.program_id(0) > 0)
    def _():
        total_ref[...] += term


def mlp_kernel(
    own_ref, other_ref, hidden_ref, down_ref, bias_ref, act_ref, slope_ref, part_ref, send_ref, chip_ref, total_ref
):
    take_both(own_ref, other_ref, chip_ref)
    pre = plain_product(chip_ref[...], hidden_ref[...]) + bias_ref[...]
    square = pre * pre
    factor = math.sqrt(2.0 / math.pi)
    bent = jnp.tanh(pre * (factor + (factor * 0.044715) * square))
    near_half = 0.5 + 0.5 * bent
    act = low(pre * near_half)
    act_ref[...] = act
    slope_ref[...] = low(
        near_half
        + (0.5 * pre) * (1.0 - bent * bent) * (factor + (3.0 * factor * 0.044715) * square)
    )
    add_up(total_ref, plain_product(act, down_ref[...]))
    sent_and_kept(total_ref, part_ref, send_ref)


def run_mlp(own, other, hiddens, downs, bias, after):
    count, width = own.shape
    cuts = hiddens.shape[1]
    size = 384
    fixed = lambda rows, columns: pl.BlockSpec((rows, columns), lambda at: (0, 0))
    across = lambda rows: pl.BlockSpec((rows, size), lambda at: (0, at))
    return chunk_call(
        mlp_kernel, "mlp", cuts // size,
        [own, other, hiddens, downs, bias],
        [
            fixed(count, width), fixed(count, width), across(width),
            pl.BlockSpec((size, width), lambda at: (at, 0)), across(1),
        ],
        [
            ((2 * count, cuts), jnp.bfloat16), ((2 * count, cuts), jnp.bfloat16),
            ((count, width), jnp.float32), ((count, width), jnp.bfloat16), ((2 * count, width), jnp.bfloat16),
        ],
        [across(2 * count), across(2 * count), fixed(count, width), fixed(count, width), fixed(2 * count, width)],
        [pltpu.VMEM((2 * count, width), jnp.float32)],
        after,
        (0, 1),
    )


def leave_kernel(last, part_ref, arrived_ref, middle_ref, vec_ref, *refs):
    branch = part_ref[...] + wide(arrived_ref[...]) + row_of(vec_ref, BIAS_DOWN)
    state = middle_ref[...] + row_of(vec_ref, GATE_TWO) * branch
    if last:
        branch_ref, out_ref = refs
        out_ref[...] = low(state)
    else:
        next_vec_ref, branch_ref, state_ref, n_ref = refs
        state_ref[...] = state
        n_ref[...] = norm_rows(state, next_vec_ref, GAIN_ONE, SCALE_ONE, SHIFT_ONE)
    branch_ref[...] = low(branch)


def start_back(grad, branch_ref, vec_ref, d_branch_ref, sums_ref, first):
    d_branch = low(row_of(vec_ref, GATE_TWO) * grad)
    d_branch_ref[...] = d_branch
    sums_ref[first : first + 1, :] = jnp.sum(grad * wide(branch_ref[...]), axis=0, keepdims=True)
    sums_ref[first + 1 : first + 2, :] = jnp.sum(wide(d_branch), axis=0, keepdims=True)


def top_kernel(masked_ref, vec_ref, grad_ref, d_branch_ref):
    grad = wide(masked_ref[...])
    grad_ref[...] = grad
    d_branch_ref[...] = low(row_of(vec_ref, GATE_TWO) * grad)


def top_sums_kernel(grad_ref, d_branch_ref, branch_ref, sums_ref):
    sums_ref[0:1, :] = jnp.sum(grad_ref[...] * wide(branch_ref[...]), axis=0, keepdims=True)
    sums_ref[1:2, :] = jnp.sum(wide(d_branch_ref[...]), axis=0, keepdims=True)


def mlp_back_kernel(
    own_ref, other_ref, slope_ref, hidden_ref, down_ref, d_pre_ref, part_ref, send_ref, bias_ref, chip_ref, total_ref
):
    take_both(own_ref, other_ref, chip_ref)
    d_pre = low(right_product(chip_ref[...], down_ref[...]) * wide(slope_ref[...]))
    d_pre_ref[...] = d_pre
    bias_ref[...] = jnp.sum(wide(d_pre), axis=0, keepdims=True)
    add_up(total_ref, right_product(d_pre, hidden_ref[...]))
    sent_and_kept(total_ref, part_ref, send_ref)


def run_mlp_back(own, other, slope, hiddens, downs, after):
    count, width = own.shape
    cuts = hiddens.shape[1]
    size = 384
    fixed = lambda rows, columns: pl.BlockSpec((rows, columns), lambda at: (0, 0))
    across = lambda rows: pl.BlockSpec((rows, size), lambda at: (0, at))
    return chunk_call(
        mlp_back_kernel, "mlp_back", cuts // size,
        [own, other, pltpu.with_memory_space_constraint(slope, pltpu.HBM), hiddens, downs],
        [
            fixed(count, width), fixed(count, width), across(2 * count), across(width),
            pl.BlockSpec((size, width), lambda at: (at, 0)),
        ],
        [
            ((2 * count, cuts), jnp.bfloat16), ((count, width), jnp.float32), ((count, width), jnp.bfloat16),
            ((1, cuts), jnp.float32), ((2 * count, width), jnp.bfloat16),
        ],
        [across(2 * count), fixed(count, width), fixed(count, width), across(1), fixed(2 * count, width)],
        [pltpu.VMEM((2 * count, width), jnp.float32)],
        after,
    )


def norm_back(d_normed, values, gain, scale, shift_sum_ref):
    unit_values, inverse = normalise(values)
    first = jnp.sum(d_normed, axis=0, keepdims=True)
    second = jnp.sum(d_normed * unit_values, axis=0, keepdims=True)
    shift_sum_ref[0:1, :] = first
    shift_sum_ref[1:2, :] = gain * second
    shift_sum_ref[2:3, :] = (1.0 + scale) * second
    scaled = d_normed * ((1.0 + scale) * gain)
    inner = jnp.mean(scaled * unit_values, axis=-1, keepdims=True)
    return (scaled - jnp.mean(scaled, axis=-1, keepdims=True) - unit_values * inner) * inverse


def middle_back_kernel(
    place_ref, grad_ref, part_ref, arrived_ref, middle_ref, branch_ref, vec_ref, weight_ref,
    d_middle_ref, d_branch_ref, att_own_ref, att_other_ref, sums_ref, d_att_ref,
):
    half = att_own_ref.shape[1]
    d_normed = part_ref[...] + wide(arrived_ref[...])
    d_middle = grad_ref[...] + norm_back(
        d_normed, middle_ref[...], row_of(vec_ref, GAIN_TWO), row_of(vec_ref, SCALE_TWO), sums_ref
    )
    d_middle_ref[...] = d_middle
    sums_ref[3:4, :] = jnp.sum(d_middle * wide(branch_ref[...]), axis=0, keepdims=True)
    d_branch_ref[...] = low(row_of(vec_ref, GATE_ONE) * d_middle)
    d_att_ref[...] = low(right_product(d_branch_ref[...], weight_ref[...]))
    att_own_ref[...] = d_att_ref[:, pl.ds(pl.multiple_of(place_ref[2] * half, 128), half)]
    att_other_ref[...] = d_att_ref[:, pl.ds(pl.multiple_of((1 - place_ref[2]) * half, 128), half)]


def project_back_kernel(d_qkv_ref, weight_ref, part_ref, send_ref):
    count = part_ref.shape[0]
    columns = d_qkv_ref.shape[1]
    part_ref[...] = right_product(d_qkv_ref[:count, :], weight_ref[:, :columns])
    send_ref[...] = low(right_product(d_qkv_ref[count:, :], weight_ref[:, :columns]))


def enter_back_kernel(last, d_middle_ref, part_ref, arrived_ref, state_ref, vec_ref, *refs):
    d_normed = part_ref[...] + wide(arrived_ref[...])
    if last:
        sums_ref, out_ref = refs
    else:
        branch_ref, next_vec_ref, sums_ref, grad_ref, d_branch_ref = refs
    grad = d_middle_ref[...] + norm_back(
        d_normed, wide(state_ref[...]), row_of(vec_ref, GAIN_ONE), row_of(vec_ref, SCALE_ONE), sums_ref
    )
    if last:
        out_ref[...] = low(grad)
    else:
        grad_ref[...] = grad
        start_back(grad, branch_ref, next_vec_ref, d_branch_ref, sums_ref, 3)


def attend_kernel(seg_q_ref, seg_k_ref, q_ref, kl_ref, vl_ref, kf_ref, vf_ref, *refs):
    own_ref, other_ref, lse_ref = refs[-3:]
    count = kl_ref.shape[0]
    TILE = count // 2
    low_half = lax.broadcasted_iota(jnp.int32, (count, 128), 1) < 64
    for start in range(0, q_ref.shape[0], TILE):
        rows = pl.ds(start, TILE)
        seg_q = seg_q_ref[rows, :]
        allow_l = seg_q == seg_k_ref[:, :count]
        allow_f = seg_q == seg_k_ref[:, count:]
        query = q_ref[rows, :]
        query = query * jnp.asarray(0.125, query.dtype)
        outs, lses = [], []
        for head in range(2):
            half = low_half if head == 0 else jnp.logical_not(low_half)
            q_h = jnp.where(half[:TILE], query, jnp.zeros_like(query))
            s_l = jnp.where(allow_l, right_product(q_h, kl_ref[...]), neg_big)
            s_f = jnp.where(allow_f, right_product(q_h, kf_ref[...]), neg_big)
            top = jnp.maximum(
                jnp.max(s_l, axis=1, keepdims=True), jnp.max(s_f, axis=1, keepdims=True)
            )
            p_l = jnp.exp(s_l - top).astype(jnp.bfloat16)
            p_f = jnp.exp(s_f - top).astype(jnp.bfloat16)
            one = jnp.ones((count, 128), jnp.bfloat16)
            summed = plain_product(p_l, jnp.where(half, vl_ref[...], one)) + plain_product(
                p_f, jnp.where(half, vf_ref[...], one)
            )
            total = pltpu.roll(summed, 64, 1)
            outs.append(summed / total)
            lses.append(top + jnp.log(total))
        result = jnp.where(low_half[:TILE], outs[0], outs[1])
        (own_ref if start == 0 else other_ref)[...] = result.astype(jnp.bfloat16)
        lse_ref[rows, :] = jnp.where(low_half[:TILE], lses[0], lses[1])


def attend(query, near, far, seg_q, seg_k, after):
    count, half = query.shape
    pairs = half // 128
    block = lambda off: pl.BlockSpec((count, 128), lambda j: (0, off + j))
    part = pl.BlockSpec((count // 2, 128), lambda j: (0, j))
    return pl.pallas_call(
        attend_kernel,
        grid=(pairs,),
        out_shape=(
            jax.ShapeDtypeStruct((count // 2, half), jnp.bfloat16),
            jax.ShapeDtypeStruct((count // 2, half), jnp.bfloat16),
            pltpu.HBM((count, half), jnp.float32),
        ),
        in_specs=[
            pl.BlockSpec((count, 1), lambda j: (0, 0)),
            pl.BlockSpec((1, 2 * count), lambda j: (0, 0)),
            block(0),
            block(0),
            block(pairs),
            block(0),
            block(pairs),
        ]
        + [pl.BlockSpec(memory_space=pl.ANY)] * len(after),
        out_specs=(part, part, block(0)),
        compiler_params=pltpu.CompilerParams(vmem_limit_bytes=VMEM_BYTES),
        cost_estimate=FREE,
        name="attend",
    )(seg_q, seg_k, query, near, near, far, far, *after)


def back_kernel(has_more, seg_q_ref, seg_k_ref, q_ref, k_ref, v_ref, do_own_ref, do_other_ref, o_own_ref, o_other_ref, lse_ref, *refs):
    count = k_ref.shape[0]
    TILE = count // 2
    low_half = lax.broadcasted_iota(jnp.int32, (TILE, 128), 1) < 64
    q_turned = (q_ref[...].astype(jnp.float32) * 0.125).T.astype(jnp.bfloat16)
    do_turned = [ref[...].astype(jnp.float32).T.astype(jnp.bfloat16) for ref in (do_own_ref, do_other_ref)]
    d_keys, d_values, d_queries = [0.0, 0.0], [0.0, 0.0], []
    for start in range(0, q_ref.shape[0], TILE):
        rows = pl.ds(start, TILE)
        allow = seg_q_ref[rows, :] == seg_k_ref[...]
        query = q_ref[rows, :]
        query = query * jnp.asarray(0.125, query.dtype)
        d_out = (do_own_ref if start == 0 else do_other_ref)[...]
        product = wide(d_out) * wide((o_own_ref if start == 0 else o_other_ref)[...])
        d_query = []
        for head in range(2):
            half = low_half if head == 0 else jnp.logical_not(low_half)
            lanes = slice(64 * head, 64 * head + 64)
            q_h = jnp.where(half, query, jnp.zeros_like(query))
            do_h = jnp.where(half, d_out, jnp.zeros_like(d_out))
            scores = jnp.where(allow, right_product(q_h, k_ref[...]), neg_big)
            probs = jnp.exp(scores - lse_ref[rows, 64 * head : 64 * head + 1])
            d_probs = right_product(do_h, v_ref[...])
            delta = jnp.sum(jnp.where(half, product, 0.0), axis=1, keepdims=True)
            d_scores = (probs * (d_probs - delta)).astype(jnp.bfloat16)
            d_values[head] += plain_product(
                do_turned[start // TILE][lanes], probs.astype(jnp.bfloat16)
            )
            d_keys[head] += plain_product(q_turned[lanes, start : start + TILE], d_scores)
            d_query.append(plain_product(d_scores, k_ref[...]))
        d_queries.append(jnp.where(low_half, d_query[0], d_query[1]) * 0.125)
    d_key = jnp.concatenate(d_keys, axis=0).T
    d_value = jnp.concatenate(d_values, axis=0).T
    d_query = jnp.concatenate(d_queries, axis=0)
    if has_more:
        dq_more_ref, dk_more_ref, dv_more_ref, out_ref = refs
        half = out_ref.shape[1] // 3
        at = pl.multiple_of(pl.program_id(0) * 128, 128)
        out_ref[:, pl.ds(at, 128)] = (d_query + dq_more_ref[...]).astype(jnp.bfloat16)
        out_ref[:, pl.ds(half + at, 128)] = (d_key + dk_more_ref[...].astype(jnp.float32)).astype(
            jnp.bfloat16
        )
        out_ref[:, pl.ds(2 * half + at, 128)] = (
            d_value + dv_more_ref[...].astype(jnp.float32)
        ).astype(jnp.bfloat16)
    else:
        dq_ref, out_ref = refs
        half = out_ref.shape[1] // 2
        at = pl.multiple_of(pl.program_id(0) * 128, 128)
        dq_ref[...] = d_query
        out_ref[:, pl.ds(at, 128)] = d_key.astype(jnp.bfloat16)
        out_ref[:, pl.ds(half + at, 128)] = d_value.astype(jnp.bfloat16)


def attend_back(query, keys, seg_q, seg_k, d_outs, out, lse, more=None, after=()):
    count, half = query.shape
    pairs = half // 128
    block = lambda off: pl.BlockSpec((count, 128), lambda j: (0, off + j))
    part = pl.BlockSpec((count // 2, 128), lambda j: (0, j))
    whole = lambda width: pl.BlockSpec((count, width), lambda j: (0, 0))
    operands = [seg_q, seg_k, query, keys, keys, *d_outs, *out]
    operands.append(pltpu.with_memory_space_constraint(lse, pltpu.HBM))
    specs = [
        pl.BlockSpec((count, 1), lambda j: (0, 0)),
        pl.BlockSpec((1, count), lambda j: (0, 0)),
        block(0),
        block(0),
        block(pairs),
        part,
        part,
        part,
        part,
        block(0),
    ]
    if more is None:
        out_shape = (
            jax.ShapeDtypeStruct((count, half), jnp.float32),
            jax.ShapeDtypeStruct((count, 2 * half), jnp.bfloat16),
        )
        out_specs = (block(0), whole(2 * half))
    else:
        operands += [more[0], more[1], more[1]]
        specs += [block(0), block(0), block(pairs)]
        out_shape = jax.ShapeDtypeStruct((count, 3 * half), jnp.bfloat16)
        out_specs = whole(3 * half)
    first_out = len(operands)
    operands += after
    specs += [pl.BlockSpec(memory_space=pl.ANY)] * len(after)
    return pl.pallas_call(
        lambda *refs: back_kernel(more is not None, *refs[:first_out], *refs[first_out + len(after) :]),
        grid=(pairs,),
        out_shape=out_shape,
        in_specs=specs,
        out_specs=out_specs,
        compiler_params=pltpu.CompilerParams(vmem_limit_bytes=VMEM_BYTES),
        cost_estimate=FREE,
        name="attend_back",
    )(*operands)


def local_paired(
    tokens,
    cotangent,
    segments,
    noised,
    levels,
    ada_weight,
    ada_bias,
    first_gain,
    qkv_weight,
    out_weight,
    second_gain,
    hidden_weight,
    hidden_bias,
    down_weight,
    down_bias,
):
    layers, ada_part, cond_width = ada_weight.shape
    part = first_gain.shape[1]
    hidden_part = hidden_bias.shape[1]
    width = tokens.shape[2]
    shards = width // part
    hidden = hidden_part * shards
    half = width // 2
    rows_in = part // 4
    rows_down = hidden_part // 8
    hidden_cut = hidden_part // 2
    blk = lax.axis_index("blk")
    uly = lax.axis_index("uly")
    core = uly // 2
    side = uly % 2
    quarter = blk * 2 + side
    shard = lax.axis_index("dp")
    row = shard * 2 + blk
    place = jnp.stack([shard, quarter, core]).astype(jnp.int32)

    def exchange(two_rows):
        return jnp.concatenate(
            [pick(two_rows, blk, 0), swap_blk(pick(two_rows, 1 - blk, 0))], axis=0
        )

    sizes = (rows_in, rows_down, half, hidden_cut, shards)
    qkv_weight, out_weight, hidden_weight, down_weight = (
        pltpu.with_memory_space_constraint(weight, pltpu.HBM)
        for weight in (qkv_weight, out_weight, hidden_weight, down_weight)
    )
    columns = 4 * half
    attn_columns = 3 * half
    mlp_columns = 5 * half

    def spread(own, last):
        near, far = swap_half(own), swap_blk(own)
        return (own, near, far, swap_blk(near) if last == "blk" else swap_half(far))

    def cut_attn(index, after):
        return copy_call(
            lambda *refs: cut_attn_kernel(sizes, index, *refs), "cut_attn", place,
            [qkv_weight], [(rows_in, attn_columns)], 3, after,
        )[0]

    def cut_mlp(index, after):
        return copy_call(
            lambda *refs: cut_mlp_kernel(sizes, index, *refs), "cut_mlp", place,
            [out_weight, hidden_weight, down_weight], [(2 * rows_in, mlp_columns)], shards + 4, after,
        )[0]

    def cut_next(index, after):
        return copy_call(
            lambda *refs: cut_next_kernel(sizes, index, *refs), "cut_next", place,
            [qkv_weight, out_weight, hidden_weight, down_weight],
            [(3 * rows_in, mlp_columns)], shards + 7, after,
        )[0]

    def whole_attn(index, spread):
        joined = copy_call(
            lambda *refs: join_attn_kernel(sizes, index, *refs), "join_attn", place,
            [qkv_weight, *spread], [(shards, part, attn_columns)], 3 + 4 * (shards - 1), (), True,
        )[0]
        return joined.reshape(width, attn_columns)

    def whole_mlp(index, spread):
        outs, hiddens, downs = copy_call(
            lambda *refs: join_mlp_kernel(sizes, index, *refs), "join_mlp", place,
            [out_weight, hidden_weight, down_weight, *spread],
            [(shards, part, width), (shards, part, columns), (shards, hidden_cut, width)],
            shards + 2 + 20 * (shards - 1), (), True,
        )
        return (
            outs.reshape(width, width), hiddens.reshape(width, columns),
            downs.reshape(shards * hidden_cut, width),
        )

    start = exchange(tokens)
    segs_two = exchange(segments)
    seg_chip = jnp.concatenate([segs_two, swap_core(segs_two)])
    seg_far = swap_half(seg_chip)
    def every_shard_of(piece):
        return lax.all_gather(piece, "dp", axis=0, tiled=False)

    def others_of(piece):
        return jnp.stack([from_shard(piece, back, shards) for back in range(1, shards)])

    def every_shard(vector):
        table = jnp.stack([vector] + [from_shard(vector, back, shards) for back in range(1, shards)])
        return jnp.stack([pick(table, (shard + shards - at) % shards, 0) for at in range(shards)])

    all_levels = every_shard(levels)
    attn_piece = cut_attn(0, [])
    attn_own = others_of(attn_piece)
    attn = spread(attn_own, "half")
    mlp_piece = cut_mlp(0, [attn_own])
    mlp_whole = every_shard_of(mlp_piece)
    next_whole = [every_shard_of(cut_next(index, [mlp_piece])) for index in range(1, layers)]

    all_levels = all_levels.reshape(-1)
    conds = low(cond_vector(all_levels, cond_width))
    part_mods = jnp.stack(
        [right_product(conds, ada_weight[index]) + wide(ada_bias[index]) for index in range(layers)],
        axis=1,
    )
    own_vectors = wide(
        jnp.concatenate([first_gain, second_gain, down_bias, hidden_bias], axis=1)
    )

    def shared_for(target):
        return jnp.concatenate([pick(part_mods, target * 2 + blk, 0), own_vectors], axis=1)

    shared = [shared_for(shard)]
    for ahead in range(1, shards):
        shared.append(from_shard(shared_for((shard + ahead) % shards), ahead, shards))
    shared = jnp.stack(shared)
    shared = jnp.stack([pick(shared, (shard + shards - at) % shards, 0) for at in range(shards)])
    vectors = []
    for index in range(layers):
        table = shared[:, index]
        ends = [ada_part + number * part for number in range(4)]
        rows = [table[:, :ada_part].reshape(6, width)]
        rows += [table[:, first : first + part].reshape(1, width) for first in ends[:3]]
        bias_hidden = table[:, ends[3] :].reshape(shards, 2, hidden_cut)
        vectors.append(
            (jnp.concatenate(rows, axis=0), pick(bias_hidden, core, 1).reshape(1, shards * hidden_cut))
        )

    seg_q = seg_chip[:, None]
    seg_near_k, seg_far_k = seg_chip[None, :], seg_far[None, :]
    seg_k = jnp.concatenate([seg_near_k, seg_far_k], axis=1)

    def spread_late(own, after):
        near, far = swap_half(own), hold(swap_blk(own), after)
        return (own, near, far, swap_half(far))

    tokens_here = start.shape[0]
    rows_f32 = ((tokens_here, width), jnp.float32)
    rows_low = ((tokens_here, width), jnp.bfloat16)
    half_low = ((tokens_here, half), jnp.bfloat16)
    chip_low = ((2 * tokens_here, width), jnp.bfloat16)
    cut_wide = shards * hidden_cut
    state = wide(start)
    normed = whole_call(
        enter_kernel, "enter", [rows_low], [start, vectors[0][0]], None, [seg_far]
    )[0]
    masked = exchange(cotangent * low(noised)[..., None])
    grad, d_branch_two = whole_call(top_kernel, "top", [rows_f32, rows_low], [masked, vectors[-1][0]])
    d_branch_other = swap_core(d_branch_two)
    kept, gathered = [], []
    for index in range(layers):
        vec, bias_core = vectors[index]
        joined = whole_attn(index, attn)
        normed_other = swap_core(normed)
        near, normed_chip = whole_call(
            lambda *refs: project_kernel(half, 3 * half, *refs), "keys_values",
            [((2 * tokens_here, 2 * half), jnp.bfloat16), chip_low], [normed, normed_other, joined],
        )
        far = swap_half(near)
        query = whole_call(
            lambda *refs: project_kernel(0, half, *refs), "queries",
            [((2 * tokens_here, half), jnp.bfloat16)], [normed, normed_other, joined], None, [near],
        )[0]
        att_own, att_send, lse = attend(query, near, far, seg_q, seg_k, ())
        att_other = swap_core(att_send)
        if index == 0:
            mlp_own = others(place, mlp_whole, [(0, 2 * rows_in, mlp_columns)], [att_own])[0]
        mlp = spread_late(mlp_own, att_other)
        out_whole, hiddens, downs = whole_mlp(index, mlp)
        gathered.append((hiddens, downs))
        branch_one, middle, normed_two, attended = whole_call(
            middle_kernel, "middle", [rows_low, rows_f32, rows_low, rows_low],
            [att_own, att_other, out_whole, state, vec], place,
        )
        normed_two_other = swap_core(normed_two)
        after = [d_branch_other] if index == layers - 1 else []
        act, slope, part_own, part_send, normed_two_chip = run_mlp(
            normed_two, normed_two_other, hiddens, downs, bias_core, after
        )
        if index + 1 < layers:
            mlp_own, attn_own = others(
                place, next_whole[index],
                [(0, 2 * rows_in, mlp_columns), (2 * rows_in, rows_in, attn_columns)], [part_own],
            )
            attn = spread(attn_own, "half")
        ends = [part_own, swap_core(part_send), middle, vec]
        keep = [
            state, normed_chip, joined, out_whole, query, near, far, (att_own, att_send), lse, attended,
            branch_one, middle, normed_two_chip, act, slope,
        ]
        if index == layers - 1:
            branch_two, final = whole_call(
                lambda *refs: leave_kernel(True, *refs), "leave", [rows_low, rows_low], ends
            )
        else:
            branch_two, state, normed = whole_call(
                lambda *refs: leave_kernel(False, *refs), "leave", [rows_low, rows_f32, rows_low],
                ends + [vectors[index + 1][0]], None, (),
            )
        kept.append(keep + [branch_two])

    def give_back(rows):
        mine, other = rows[: rows.shape[0] // 2], rows[rows.shape[0] // 2 :]
        arrived = swap_blk(other)
        return jnp.where(blk == 0, jnp.stack([mine, arrived]), jnp.stack([arrived, mine]))

    output = give_back(final)

    def reduce_start(array, rows):
        terms = array.reshape(shards, 2, 2, rows, array.shape[1])
        first = swap_half(pick(terms, 1 - side, 2))
        kept_terms = low(wide(pick(terms, side, 2)) + wide(first))
        return pick(kept_terms, blk, 1), swap_blk(pick(kept_terms, 1 - blk, 1))

    def reduce_end(pair, *after):
        mine, arrived = pair
        return low(wide(mine) + wide(hold(arrived, *after) if after else arrived))

    def scatter_shards(array):
        return lax.psum_scatter(array, "dp", scatter_dimension=0, tiled=False)

    def sum_shards(array):
        arrived = [
            from_shard(pick(array, (shard + ahead) % shards, 0), ahead, shards)
            for ahead in range(1, shards)
        ]
        return low(wide(pick(array, shard, 0)) + sum(wide(item) for item in arrived)), arrived[0]

    sums_top = whole_call(
        top_sums_kernel, "top_sums", [((2, width), jnp.float32)], [grad, d_branch_two, kept[-1][-1]]
    )[0]
    def end_mlp_sums(pending, late):
        index, down_pair, hidden_pair, _, _ = pending
        down_sum, hidden_sum = reduce_end(down_pair, late), reduce_end(hidden_pair, late)
        down_sum = jnp.concatenate([down_sum[:, :rows_in], down_sum[:, rows_in:]], axis=2)
        return scatter_shards(jnp.concatenate([hidden_sum, down_sum], axis=1))

    def end_attn_sums(pending, late):
        index, _, _, attn_pair, out_sum = pending
        attn_sum = reduce_end(attn_pair, late) if index > 0 else reduce_end(attn_pair)
        attn_sum = jnp.concatenate([attn_sum, out_sum], axis=2)
        return (scatter_shards(attn_sum), None) if index > 0 else sum_shards(attn_sum)

    pending = None
    small = [None] * layers
    shards_out = [None] * layers
    due = [()] * 5
    for index in reversed(range(layers)):
        vec, _ = vectors[index]
        hiddens, downs = gathered[index]
        (
            state_in, normed_chip, joined, out_whole, query, near, far, heads_out, lse, attended,
            branch_one, middle, normed_two_chip, act, slope, _,
        ) = kept[index]
        if index < layers - 1:
            d_branch_other = swap_core(d_branch_two)
        d_pre, part_own, part_send, d_bias_core, d_branch_chip = run_mlp_back(
            d_branch_two, d_branch_other, slope, hiddens, downs, due[0]
        )
        if pending is not None:
            shards_out[pending[0]] = (None, end_mlp_sums(pending, d_pre))
        d_down = low(left_product(act, d_branch_chip))
        d_hidden = low(left_product(normed_two_chip, d_pre))
        down_pair, hidden_pair = reduce_start(d_down, rows_down), reduce_start(d_hidden, rows_in)
        d_middle, d_one, d_att_own, d_att_send, sums_middle, _ = whole_call(
            middle_back_kernel, "middle_back",
            [rows_f32, rows_low, half_low, half_low, ((4, width), jnp.float32), rows_low],
            [grad, part_own, swap_core(part_send), middle, branch_one, vec, out_whole], place, due[1],
        )
        d_heads = (d_att_own, swap_core(d_att_send))
        d_query_far, d_far = attend_back(
            query, far, seg_q, seg_far_k, d_heads, heads_out, lse, None, due[2],
        )
        if pending is not None:
            shards_out[pending[0]] = (end_attn_sums(pending, d_query_far)[0], shards_out[pending[0]][1])
        d_near = swap_half(d_far)
        out_sum = reduce_end(reduce_start(low(left_product(attended, d_one)), rows_in))
        out_sum = low(
            wide(lax.dynamic_slice_in_dim(out_sum, core * half, half, 2))
            + wide(swap_core(lax.dynamic_slice_in_dim(out_sum, (1 - core) * half, half, 2)))
        )
        d_qkv = attend_back(
            query, near, seg_q, seg_near_k, d_heads, heads_out, lse, (d_query_far, d_near),
            due[3],
        )
        d_qkv_core = low(left_product(normed_chip, d_qkv))
        attn_pair = reduce_start(d_qkv_core, rows_in)
        part_own, part_send = whole_call(
            project_back_kernel, "project_back", [rows_f32, rows_low], [d_qkv, joined], None, due[4]
        )
        ends = [d_middle, part_own, swap_core(part_send), state_in, vec]
        sums_next = None
        if index == 0:
            sums_in, last_grad = whole_call(
                lambda *refs: enter_back_kernel(True, *refs), "enter_back",
                [((3, width), jnp.float32), rows_low], ends,
            )
        else:
            sums_in, grad, d_branch_two = whole_call(
                lambda *refs: enter_back_kernel(False, *refs), "enter_back",
                [((5, width), jnp.float32), rows_f32, rows_low],
                ends + [kept[index - 1][-1], vectors[index - 1][0]], None,
                (),
            )
            sums_next = sums_in[3:]
        pending = (index, down_pair, hidden_pair, attn_pair, out_sum)
        d_units = d_bias_core.reshape(shards, 1, hidden_cut)
        d_units = jnp.concatenate(
            [jnp.where(core == 0, d_units, 0.0), jnp.where(core == 1, d_units, 0.0)], axis=1
        )
        d_modulation = jnp.concatenate(
            [sums_in[:2], sums_middle[3:4], sums_middle[:2], sums_top[:1]], axis=0
        )
        small[index] = jnp.concatenate(
            [
                d_modulation.reshape(shards, -1),
                sums_in[2].reshape(shards, -1),
                sums_middle[2].reshape(shards, -1),
                sums_top[1].reshape(shards, -1),
                d_units.reshape(shards, -1),
            ],
            axis=1,
        )
        sums_top = sums_next

    attn_shard, shard_arrived = end_attn_sums(pending, None)
    shards_out[0] = (attn_shard, end_mlp_sums(pending, last_grad))
    tokens_grad = give_back(last_grad)

    vector = jnp.stack(small)
    vector = vector + swap_core(vector)
    vector = vector + swap_half(vector)
    parts = vector.transpose(1, 0, 2)
    arrived = [pick(parts, shard, 0)]
    for ahead in range(1, shards):
        arrived.append(from_shard(pick(parts, (shard + ahead) % shards, 0), ahead, shards))
    arrived = jnp.stack(arrived)
    other = swap_blk(arrived)
    totals = jnp.sum(arrived + other, axis=0)
    cond_rows = wide(conds).reshape(shards, 2, cond_width)
    cond_rows = jnp.stack([pick(cond_rows, (shard + shards - at) % shards, 0) for at in range(shards)])
    by_row = jnp.concatenate([arrived[:, :, :ada_part], other[:, :, :ada_part]], axis=0)
    cond_both = jnp.concatenate([pick(cond_rows, blk, 1), pick(cond_rows, 1 - blk, 1)], axis=0)
    grad_ada = jnp.einsum(
        "slm,sc->lmc", by_row, cond_both, precision=lax.Precision.HIGHEST
    )
    grad_ada_bias = totals[:, :ada_part]
    at = ada_part
    grad_gain_one = totals[:, at : at + part]
    grad_gain_two = totals[:, at + part : at + 2 * part]
    grad_bias_down = totals[:, at + 2 * part : at + 3 * part]
    grad_bias_hidden = totals[:, at + 3 * part :]

    def every_piece(piece, after):
        far, across = swap_blk(piece), swap_core(piece)
        cut = 4 * rows_in // 3
        last = jnp.concatenate([swap_blk(across[:cut]), swap_core(far[cut:])], axis=0)
        mine = jnp.stack([piece, far, across, last])
        other = swap_half(hold(mine, after) if after is not None else mine)
        return (
            jnp.stack([mine[0], other[0], mine[1], other[1]]),
            jnp.stack([mine[2], other[2], mine[3], other[3]]),
        )

    shapes = {
        "attn": [(layers, part, 3 * width), (layers, part, width)],
        "mlp": [(layers, part, hidden), (layers, 2, 4, rows_down, width)],
    }
    grads = None
    for index in reversed(range(layers)):
        piece = jnp.concatenate(shards_out[index], axis=0)
        if index > 0:
            piece = hold(piece, token(shard_arrived))
        grads = finish(
            place, index, ("attn", "mlp"), every_piece(piece, None), shapes, half, rows_in, shards, grads
        )
    grad_qkv, grad_out, grad_hidden, grad_down = grads
    grad_down = grad_down.reshape(layers, hidden_part, width)
    return (
        output,
        tokens_grad,
        grad_ada,
        grad_ada_bias,
        grad_gain_one,
        grad_qkv,
        grad_out,
        grad_gain_two,
        grad_hidden,
        grad_bias_hidden,
        grad_down,
        grad_bias_down,
    )


def pick_plan(mesh):
    def run(*arrays):
        tokens, first_gain, hidden_bias = arrays[0], arrays[7], arrays[12]
        fits = (
            mesh.shape["blk"] == 2
            and mesh.shape["uly"] == 4
            and tokens.shape[0] == 2
            and tokens.shape[1] % 64 == 0
            and tokens.shape[2] == HEADS * 64
            and HEADS % 4 == 0
            and first_gain.shape[1] % 64 == 0
            and hidden_bias.shape[1] % 256 == 0
        )
        return (local_paired if fits else local)(*arrays)

    return run


def solution(mesh):
    in_specs = (
        P("dp", ("blk", "uly"), None),
        P("dp", ("blk", "uly"), None),
        P("dp", ("blk", "uly")),
        P("dp", ("blk", "uly")),
        P("dp"),
        P(None, "dp", None),
        P(None, "dp"),
        P(None, "dp"),
        P(None, "dp", None),
        P(None, "dp", None),
        P(None, "dp"),
        P(None, "dp", None),
        P(None, "dp"),
        P(None, "dp", None),
        P(None, "dp"),
    )
    out_specs = (
        P("dp", ("blk", "uly"), None),
        P("dp", ("blk", "uly"), None),
        P(None, "dp", None),
        P(None, "dp"),
        P(None, "dp"),
        P(None, "dp", None),
        P(None, "dp", None),
        P(None, "dp"),
        P(None, "dp", None),
        P(None, "dp"),
        P(None, "dp", None),
        P(None, "dp"),
    )
    return jax.shard_map(pick_plan(mesh), mesh=mesh, in_specs=in_specs, out_specs=out_specs, check_vma=False)
```

```python
import math

import jax
import jax.numpy as jnp
from jax import lax
from jax.experimental import pallas as pl
from jax.experimental.pallas import tpu as pltpu
from jax.sharding import PartitionSpec as P

HEADS = 12


epsilon = 1e-05
neg_big = -1e30


def cond_vector(levels, width):
    half_width = width // 2
    freqs = jnp.exp(-math.log(10000.0) * jnp.arange(half_width, dtype=jnp.float32) / half_width)
    angles = levels.astype(jnp.float32)[:, None] * freqs[None, :]
    return jax.nn.silu(jnp.concatenate([jnp.cos(angles), jnp.sin(angles)], axis=-1))


def norm_mod(values, gain_vec, shift_vec, scale_vec):
    average = jnp.mean(values, axis=-1, keepdims=True)
    centered = values - average
    variance = jnp.mean(centered * centered, axis=-1, keepdims=True)
    return centered * lax.rsqrt(variance + epsilon) * gain_vec * (1.0 + scale_vec) + shift_vec


def gelu_tanh(values):
    return jax.nn.gelu(values, approximate=True)


def left_product(first, second):
    return lax.dot_general(
        first, second, (((0,), (0,)), ((), ())), preferred_element_type=jnp.float32
    )


def right_product(first, second):
    return lax.dot_general(
        first, second, (((1,), (1,)), ((), ())), preferred_element_type=jnp.float32
    )


def fetch(params, layer_index):
    p_ada, p_bias, p_gain, p_qkv, p_out, p_gain_two, p_hidden, p_hbias, p_down, p_dbias = params
    return (
        lax.all_gather(p_ada[layer_index], "dp", axis=0, tiled=True),
        lax.all_gather(p_bias[layer_index], "dp", axis=0, tiled=True),
        lax.all_gather(p_gain[layer_index], "dp", axis=0, tiled=True),
        lax.all_gather(p_qkv[layer_index], "dp", axis=0, tiled=True),
        lax.all_gather(p_out[layer_index], "dp", axis=0, tiled=True),
        lax.all_gather(p_gain_two[layer_index], "dp", axis=0, tiled=True),
        lax.all_gather(p_hidden[layer_index], "dp", axis=0, tiled=True),
        lax.all_gather(p_hbias[layer_index], "dp", axis=0, tiled=True),
        lax.all_gather(p_down[layer_index], "dp", axis=0, tiled=True),
        lax.all_gather(p_dbias[layer_index], "dp", axis=0, tiled=True),
    )


def reduce_grads(grads):
    shards = (
        lax.psum_scatter(
            grads[0].astype(jnp.bfloat16), "dp", scatter_dimension=0, tiled=True
        ).astype(jnp.float32),
        lax.psum_scatter(
            grads[1].astype(jnp.bfloat16), "dp", scatter_dimension=0, tiled=True
        ).astype(jnp.float32),
        lax.psum_scatter(
            grads[2].astype(jnp.bfloat16), "dp", scatter_dimension=0, tiled=True
        ).astype(jnp.float32),
        lax.psum_scatter(
            grads[3].astype(jnp.bfloat16), "dp", scatter_dimension=0, tiled=True
        ).astype(jnp.float32),
        lax.psum_scatter(
            grads[4].astype(jnp.bfloat16), "dp", scatter_dimension=0, tiled=True
        ).astype(jnp.float32),
        lax.psum_scatter(
            grads[5].astype(jnp.bfloat16), "dp", scatter_dimension=0, tiled=True
        ).astype(jnp.float32),
        lax.psum_scatter(
            grads[6].astype(jnp.bfloat16), "dp", scatter_dimension=0, tiled=True
        ).astype(jnp.float32),
        lax.psum_scatter(
            grads[7].astype(jnp.bfloat16), "dp", scatter_dimension=0, tiled=True
        ).astype(jnp.float32),
        lax.psum_scatter(
            grads[8].astype(jnp.bfloat16), "dp", scatter_dimension=0, tiled=True
        ).astype(jnp.float32),
        lax.psum_scatter(
            grads[9].astype(jnp.bfloat16), "dp", scatter_dimension=0, tiled=True
        ).astype(jnp.float32),
    )
    return (
        lax.psum(shards[0].astype(jnp.bfloat16), ("blk", "uly")).astype(jnp.float32),
        lax.psum(shards[1].astype(jnp.bfloat16), ("blk", "uly")).astype(jnp.float32),
        lax.psum(shards[2].astype(jnp.bfloat16), ("blk", "uly")).astype(jnp.float32),
        lax.psum(shards[3].astype(jnp.bfloat16), ("blk", "uly")).astype(jnp.float32),
        lax.psum(shards[4].astype(jnp.bfloat16), ("blk", "uly")).astype(jnp.float32),
        lax.psum(shards[5].astype(jnp.bfloat16), ("blk", "uly")).astype(jnp.float32),
        lax.psum(shards[6].astype(jnp.bfloat16), ("blk", "uly")).astype(jnp.float32),
        lax.psum(shards[7].astype(jnp.bfloat16), ("blk", "uly")).astype(jnp.float32),
        lax.psum(shards[8].astype(jnp.bfloat16), ("blk", "uly")).astype(jnp.float32),
        lax.psum(shards[9].astype(jnp.bfloat16), ("blk", "uly")).astype(jnp.float32),
    )


def over_blocks(block_fn, carry, key_piece, value_piece, seg_piece):
    count = key_piece.shape[2]
    size = 512

    def block_step(inner, position):
        offset = position * size
        key_blk = lax.dynamic_slice_in_dim(key_piece, offset, size, 2)
        value_blk = lax.dynamic_slice_in_dim(value_piece, offset, size, 2)
        seg_blk = lax.dynamic_slice_in_dim(seg_piece, offset, size, 0)
        return (block_fn(inner, key_blk, value_blk, seg_blk, offset), None)

    return lax.scan(block_step, carry, jnp.arange(count // size, dtype=jnp.int32))[0]


def split_heads(qkv_b):
    tokens_dev = qkv_b.shape[0]
    width = qkv_b.shape[1] // 3
    heads_all = lax.all_to_all(
        qkv_b.reshape(tokens_dev, 3, width), "uly", split_axis=2, concat_axis=0, tiled=True
    )
    span = heads_all.shape[0]
    head_dim = width // HEADS
    local_heads = heads_all.shape[2] // head_dim
    layout = heads_all.reshape(span, 3, local_heads, head_dim).transpose(1, 2, 3, 0)
    return (layout[0], layout[1], layout[2])


def layer_forward(state, weights_now, cond_b, seg_row):
    (
        ada_weight,
        ada_bias,
        first_gain,
        qkv_weight,
        out_weight,
        second_gain,
        hidden_weight,
        hidden_bias,
        down_weight,
        down_bias,
    ) = weights_now
    modulation = jnp.dot(ada_weight, cond_b, preferred_element_type=jnp.float32) + ada_bias.astype(
        jnp.float32
    )
    shift_one, scale_one, gate_one, shift_two, scale_two, gate_two = jnp.split(modulation, 6)
    normed_b = norm_mod(state, first_gain.astype(jnp.float32), shift_one, scale_one).astype(
        jnp.bfloat16
    )
    qkv_b = jnp.dot(normed_b, qkv_weight, preferred_element_type=jnp.float32).astype(jnp.bfloat16)
    query_t, key_t, value_t = split_heads(qkv_b)
    local_heads, head_dim, span = query_t.shape
    factor = head_dim ** (-0.5)
    query_seg = lax.dynamic_slice_in_dim(seg_row, lax.axis_index("blk") * span, span, 0)

    def forward_block(carry, key_blk, value_blk, seg_blk, start):
        running_max, running_total, weighted = carry
        scores = (
            jnp.einsum("hdq,hdk->hqk", query_t, key_blk, preferred_element_type=jnp.float32)
            * factor
        )
        allowed = (query_seg[:, None] == seg_blk[None, :])[None]
        masked = jnp.where(allowed, scores, neg_big)
        new_max = jnp.maximum(running_max, jnp.max(masked, axis=-1))
        probabilities = jnp.where(allowed, jnp.exp(masked - new_max[..., None]), 0.0)
        rescale = jnp.exp(running_max - new_max)
        running_total = running_total * rescale + jnp.sum(probabilities, axis=-1)
        update = jnp.einsum(
            "hqk,hdk->hdq",
            probabilities.astype(jnp.bfloat16),
            value_blk,
            preferred_element_type=jnp.float32,
        )
        weighted = weighted * rescale[:, None, :] + update
        return (new_max, running_total, weighted)

    initial = (
        jnp.full((local_heads, span), neg_big, jnp.float32),
        jnp.zeros((local_heads, span), jnp.float32),
        jnp.zeros((local_heads, head_dim, span), jnp.float32),
    )
    running_max, running_total, weighted = over_blocks(
        forward_block,
        initial,
        lax.all_gather(key_t, "blk", axis=2, tiled=True),
        lax.all_gather(value_t, "blk", axis=2, tiled=True),
        seg_row,
    )
    attended_heads = weighted / running_total[:, None, :]
    log_total = running_max + jnp.log(running_total)
    sendable = (
        attended_heads.astype(jnp.bfloat16).transpose(2, 0, 1).reshape(span, local_heads * head_dim)
    )
    attended_b = lax.all_to_all(sendable, "uly", split_axis=0, concat_axis=1, tiled=True)
    branch_one = jnp.dot(attended_b, out_weight, preferred_element_type=jnp.float32)
    middle = state + gate_one * branch_one
    normed_two = norm_mod(middle, second_gain.astype(jnp.float32), shift_two, scale_two).astype(
        jnp.bfloat16
    )
    hidden_pre = jnp.dot(
        normed_two, hidden_weight, preferred_element_type=jnp.float32
    ) + hidden_bias.astype(jnp.float32)
    activated = gelu_tanh(hidden_pre).astype(jnp.bfloat16)
    branch_two = jnp.dot(
        activated, down_weight, preferred_element_type=jnp.float32
    ) + down_bias.astype(jnp.float32)
    result = middle + gate_two * branch_two
    kept = (
        state,
        modulation,
        normed_b,
        query_t,
        key_t,
        value_t,
        attended_heads,
        log_total,
        attended_b,
        branch_one,
        middle,
        normed_two,
        hidden_pre,
        activated,
        branch_two,
    )
    return (result, kept)


def layer_backward(grad, weights_now, kept, cond_b, seg_row):
    (
        ada_weight,
        ada_bias,
        first_gain,
        qkv_weight,
        out_weight,
        second_gain,
        hidden_weight,
        hidden_bias,
        down_weight,
        down_bias,
    ) = weights_now
    (
        state,
        modulation,
        normed_b,
        query_t,
        key_t,
        value_t,
        attended_heads,
        log_total,
        attended_b,
        branch_one,
        middle,
        normed_two,
        hidden_pre,
        activated,
        branch_two,
    ) = kept
    shift_one, scale_one, gate_one, shift_two, scale_two, gate_two = jnp.split(modulation, 6)
    gain_one = first_gain.astype(jnp.float32)
    gain_two = second_gain.astype(jnp.float32)
    d_gate_two = jnp.sum(grad * branch_two, axis=0)
    d_branch_two = (gate_two * grad).astype(jnp.bfloat16)
    d_down_weight = left_product(activated, d_branch_two)
    d_down_bias = jnp.sum(d_branch_two.astype(jnp.float32), axis=0)
    d_activated = right_product(d_branch_two, down_weight)
    gelu_back = jax.vjp(gelu_tanh, hidden_pre)[1]
    d_pre = gelu_back(d_activated)[0].astype(jnp.bfloat16)
    d_hidden_weight = left_product(normed_two, d_pre)
    d_hidden_bias = jnp.sum(d_pre.astype(jnp.float32), axis=0)
    d_normed_two = right_product(d_pre, hidden_weight)
    norm_back_two = jax.vjp(norm_mod, middle, gain_two, shift_two, scale_two)[1]
    d_middle_part, d_gain_two, d_shift_two, d_scale_two = norm_back_two(d_normed_two)
    d_middle = grad + d_middle_part
    d_gate_one = jnp.sum(d_middle * branch_one, axis=0)
    d_branch_one = (gate_one * d_middle).astype(jnp.bfloat16)
    d_out_weight = left_product(attended_b, d_branch_one)
    d_attended_b = right_product(d_branch_one, out_weight).astype(jnp.bfloat16)
    local_heads, head_dim, span = query_t.shape
    factor = head_dim ** (-0.5)
    d_heads_t = (
        lax.all_to_all(d_attended_b, "uly", split_axis=1, concat_axis=0, tiled=True)
        .reshape(span, local_heads, head_dim)
        .transpose(1, 2, 0)
    )
    row_delta = jnp.sum(d_heads_t.astype(jnp.float32) * attended_heads, axis=1)
    query_seg = lax.dynamic_slice_in_dim(seg_row, lax.axis_index("blk") * span, span, 0)

    def backward_block(carry, key_blk, value_blk, seg_blk, start):
        d_query, d_key_all, d_value_all = carry
        scores = (
            jnp.einsum("hdq,hdk->hqk", query_t, key_blk, preferred_element_type=jnp.float32)
            * factor
        )
        allowed = (query_seg[:, None] == seg_blk[None, :])[None]
        probabilities = jnp.where(allowed, jnp.exp(scores - log_total[..., None]), 0.0)
        d_probs = jnp.einsum(
            "hdq,hdk->hqk", d_heads_t, value_blk, preferred_element_type=jnp.float32
        )
        d_scores = (probabilities * (d_probs - row_delta[..., None])).astype(jnp.bfloat16)
        d_query = (
            d_query
            + jnp.einsum("hqk,hdk->hdq", d_scores, key_blk, preferred_element_type=jnp.float32)
            * factor
        )
        d_key_new = (
            jnp.einsum("hqk,hdq->hdk", d_scores, query_t, preferred_element_type=jnp.float32)
            * factor
        )
        d_value_new = jnp.einsum(
            "hqk,hdq->hdk",
            probabilities.astype(jnp.bfloat16),
            d_heads_t,
            preferred_element_type=jnp.float32,
        )
        size = key_blk.shape[2]
        d_key_all = lax.dynamic_update_slice_in_dim(
            d_key_all, lax.dynamic_slice_in_dim(d_key_all, start, size, 2) + d_key_new, start, 2
        )
        d_value_all = lax.dynamic_update_slice_in_dim(
            d_value_all,
            lax.dynamic_slice_in_dim(d_value_all, start, size, 2) + d_value_new,
            start,
            2,
        )
        return (d_query, d_key_all, d_value_all)

    row_len = seg_row.shape[0]
    initial = (
        jnp.zeros((local_heads, head_dim, span), jnp.float32),
        jnp.zeros((local_heads, head_dim, row_len), jnp.float32),
        jnp.zeros((local_heads, head_dim, row_len), jnp.float32),
    )
    d_query, d_key_all, d_value_all = over_blocks(
        backward_block,
        initial,
        lax.all_gather(key_t, "blk", axis=2, tiled=True),
        lax.all_gather(value_t, "blk", axis=2, tiled=True),
        seg_row,
    )
    d_key, d_value = (
        lax.psum_scatter(
            d_key_all.astype(jnp.bfloat16), "blk", scatter_dimension=2, tiled=True
        ).astype(jnp.float32),
        lax.psum_scatter(
            d_value_all.astype(jnp.bfloat16), "blk", scatter_dimension=2, tiled=True
        ).astype(jnp.float32),
    )
    joined = jnp.stack([d_query, d_key, d_value], axis=0).astype(jnp.bfloat16)
    stacked = joined.transpose(3, 0, 1, 2).reshape(span, 3, local_heads * head_dim)
    returned = lax.all_to_all(stacked, "uly", split_axis=0, concat_axis=2, tiled=True)
    tokens_dev = state.shape[0]
    d_qkv_b = returned.reshape(tokens_dev, returned.shape[1] * returned.shape[2])
    d_qkv_weight = left_product(normed_b, d_qkv_b)
    d_normed = right_product(d_qkv_b, qkv_weight)
    norm_back_one = jax.vjp(norm_mod, state, gain_one, shift_one, scale_one)[1]
    d_state_part, d_gain_one, d_shift_one, d_scale_one = norm_back_one(d_normed)
    d_state = d_middle + d_state_part
    d_modulation = jnp.concatenate(
        [d_shift_one, d_scale_one, d_gate_one, d_shift_two, d_scale_two, d_gate_two]
    )
    d_ada_weight = d_modulation[:, None] * cond_b.astype(jnp.float32)[None, :]
    grads = (
        d_ada_weight,
        d_modulation,
        d_gain_one,
        d_qkv_weight,
        d_out_weight,
        d_gain_two,
        d_hidden_weight,
        d_hidden_bias,
        d_down_weight,
        d_down_bias,
    )
    return (d_state, grads)


def add_tuples(first, second):
    if first is None:
        return second
    return tuple((left_item + right_item for left_item, right_item in zip(first, second)))


def local(
    tokens,
    cotangent,
    segments,
    noised,
    levels,
    ada_weight,
    ada_bias,
    first_gain,
    qkv_weight,
    out_weight,
    second_gain,
    hidden_weight,
    hidden_bias,
    down_weight,
    down_bias,
):
    params = (
        ada_weight,
        ada_bias,
        first_gain,
        qkv_weight,
        out_weight,
        second_gain,
        hidden_weight,
        hidden_bias,
        down_weight,
        down_bias,
    )
    layers = ada_weight.shape[0]
    batches = tokens.shape[0]
    row_segs = lax.all_gather(segments, ("blk", "uly"), axis=1, tiled=True)
    conds = cond_vector(levels, ada_weight.shape[2]).astype(jnp.bfloat16)
    stored = [fetch(params, layer_index) for layer_index in range(layers)]
    sums = [None] * layers
    outputs = []
    input_grads = []
    for batch_index in range(batches):
        state = tokens[batch_index].astype(jnp.float32)
        cond_b = conds[batch_index]
        seg_row = row_segs[batch_index]
        kept_all = []
        for layer_index in range(layers):
            weights_now = stored[layer_index]
            state, kept = layer_forward(state, weights_now, cond_b, seg_row)
            kept_all.append(kept)
        outputs.append(state.astype(jnp.bfloat16))
        grad = (
            cotangent[batch_index].astype(jnp.float32)
            * noised[batch_index].astype(jnp.float32)[:, None]
        )
        for layer_index in reversed(range(layers)):
            weights_now = stored[layer_index]
            grad, grads = layer_backward(grad, weights_now, kept_all[layer_index], cond_b, seg_row)
            sums[layer_index] = add_tuples(sums[layer_index], reduce_grads(grads))
        input_grads.append(grad.astype(jnp.bfloat16))
    stacked = [
        jnp.stack([sums[layer_index][member] for layer_index in range(layers)])
        for member in range(10)
    ]
    return (
        jnp.stack(outputs),
        jnp.stack(input_grads),
        stacked[0],
        stacked[1],
        stacked[2],
        stacked[3],
        stacked[4],
        stacked[5],
        stacked[6],
        stacked[7],
        stacked[8],
        stacked[9],
    )


SWAP = [(0, 1), (1, 0)]
PAIR = [(0, 1), (1, 0), (2, 3), (3, 2)]
ACROSS = [(0, 2), (2, 0), (1, 3), (3, 1)]
VMEM_BYTES = 16 * 1024 * 1024
COPY_BYTES = 12 * 1024 * 1024
FREE = pl.CostEstimate(flops=0, bytes_accessed=0, transcendentals=0)
COPIES = pl.CostEstimate(flops=0, bytes_accessed=7_000_000, transcendentals=0)


def swap_blk(value):
    return lax.ppermute(value, "blk", SWAP)


def swap_half(value):
    return lax.ppermute(value, "uly", PAIR)


def swap_core(value):
    return lax.ppermute(value, "uly", ACROSS)


def from_shard(value, back, shards):
    return lax.ppermute(value, "dp", [(at, (at + back) % shards) for at in range(shards)])


def plain_product(first, second):
    return jnp.dot(first, second, preferred_element_type=jnp.float32)


def normalise(values):
    average = jnp.mean(values, axis=-1, keepdims=True)
    centered = values - average
    variance = jnp.mean(centered * centered, axis=-1, keepdims=True)
    inverse = lax.rsqrt(variance + epsilon)
    return centered * inverse, inverse


def pick(array, index, axis):
    return lax.dynamic_index_in_dim(array, index, axis, keepdims=False)


def low(value):
    return value.astype(jnp.bfloat16)


def wide(value):
    return value.astype(jnp.float32)


def token(array):
    while array.ndim > 2:
        array = array[0]
    return array[:16, :128]


def whole_call(kernel, name, shapes, operands, place=None, after=()):
    specs = [] if place is None else [pl.BlockSpec(memory_space=pltpu.SMEM)]
    specs += [pl.BlockSpec(memory_space=pltpu.VMEM)] * len(operands)
    specs += [pl.BlockSpec(memory_space=pl.ANY)] * len(after)
    count = len(operands) + (place is not None)

    def body(*refs):
        kernel(*refs[:count], *refs[count + len(after) :])

    return pl.pallas_call(
        body,
        out_shape=tuple(jax.ShapeDtypeStruct(shape, kind) for shape, kind in shapes),
        in_specs=specs,
        out_specs=(pl.BlockSpec(memory_space=pltpu.VMEM),) * len(shapes),
        compiler_params=pltpu.CompilerParams(vmem_limit_bytes=VMEM_BYTES),
        cost_estimate=FREE,
        name=name,
    )(*([] if place is None else [place]), *operands, *after)


def hold(value, *after):
    return pl.pallas_call(
        lambda *refs: None,
        out_shape=jax.ShapeDtypeStruct(value.shape, value.dtype),
        in_specs=[pl.BlockSpec(memory_space=pl.ANY)] * (1 + len(after)),
        out_specs=pl.BlockSpec(memory_space=pl.ANY),
        input_output_aliases={0: 0},
        cost_estimate=FREE,
        name="hold",
    )(value, *after)


def run_copies(pairs, sems):
    copies = [
        pltpu.make_async_copy(source, target, sems.at[number])
        for number, (source, target) in enumerate(pairs)
    ]
    for copy in copies:
        copy.start()
    for copy in copies:
        copy.wait()


def attn_pairs(sizes, layer, rows, core, qkv_ref, target_ref):
    rows_in, rows_down, half, hidden_cut, shards = sizes
    lanes = pl.multiple_of(core * half, 128)
    pairs = [
        (
            qkv_ref.at[layer, rows, pl.ds(kind * 2 * half + lanes, half)],
            target_ref.at[:, pl.ds(kind * half, half)],
        )
        for kind in range(3)
    ]
    return pairs


def hidden_pairs(sizes, layer, rows, core, hidden_ref, target_ref):
    rows_in, rows_down, half, hidden_cut, shards = sizes
    lanes = pl.multiple_of(core * hidden_cut, 128)
    return [
        (
            hidden_ref.at[layer, rows, pl.ds(at * 2 * hidden_cut + lanes, hidden_cut)],
            target_ref.at[:, pl.ds(at * hidden_cut, hidden_cut)],
        )
        for at in range(shards)
    ]


def down_pairs(sizes, layer, place_ref, down_ref, target_ref):
    rows_in, rows_down, half, hidden_cut, shards = sizes
    first = pl.multiple_of(place_ref[2] * hidden_cut + place_ref[1] * rows_down, 16)
    return [
        (
            down_ref.at[layer, pl.ds(first + side * rows_in, rows_in)],
            target_ref.at[:, pl.ds(side * 2 * half, 2 * half)],
        )
        for side in range(2)
    ]


def mlp_pairs(sizes, layer, place_ref, out_ref, hidden_ref, down_ref, target_ref):
    rows_in, rows_down, half, hidden_cut, shards = sizes
    rows = pl.ds(pl.multiple_of(place_ref[1] * rows_in, 16), rows_in)
    above, below = target_ref.at[pl.ds(0, rows_in)], target_ref.at[pl.ds(rows_in, rows_in)]
    pairs = hidden_pairs(sizes, layer, rows, place_ref[2], hidden_ref, above)
    pairs += down_pairs(sizes, layer, place_ref, down_ref, below)
    for number, part_ref in enumerate((above, below)):
        pairs.append(
            (out_ref.at[layer, rows, pl.ds(number * half, half)], part_ref.at[:, pl.ds(4 * half, half)])
        )
    return pairs


def cut_attn_kernel(sizes, layer, place_ref, qkv_ref, *refs):
    piece_ref, sems = refs[-2:]
    rows = pl.ds(pl.multiple_of(place_ref[1] * sizes[0], 16), sizes[0])
    run_copies(attn_pairs(sizes, layer, rows, place_ref[2], qkv_ref, piece_ref), sems)


def cut_mlp_kernel(sizes, layer, place_ref, out_ref, hidden_ref, down_ref, *refs):
    piece_ref, sems = refs[-2:]
    run_copies(mlp_pairs(sizes, layer, place_ref, out_ref, hidden_ref, down_ref, piece_ref), sems)


def cut_next_kernel(sizes, layer, place_ref, qkv_ref, out_ref, hidden_ref, down_ref, *refs):
    piece_ref, sems = refs[-2:]
    rows_in, rows_down, half, hidden_cut, shards = sizes
    rows = pl.ds(pl.multiple_of(place_ref[1] * rows_in, 16), rows_in)
    pairs = mlp_pairs(
        sizes, layer, place_ref, out_ref, hidden_ref, down_ref, piece_ref.at[pl.ds(0, 2 * rows_in)]
    )
    pairs += attn_pairs(
        sizes, layer, rows, place_ref[2], qkv_ref,
        piece_ref.at[pl.ds(2 * rows_in, rows_in), pl.ds(0, 3 * half)],
    )
    piece_ref[2 * rows_in :, 3 * half :] = jnp.zeros((rows_in, 2 * half), piece_ref.dtype)
    run_copies(pairs, sems)


def others_kernel(cuts, place_ref, all_ref, *refs):
    outs, sems = refs[-1 - len(cuts) : -1], refs[-1]
    shards = all_ref.shape[0]
    pairs = []
    for (first, rows, columns), out_ref in zip(cuts, outs):
        for back in range(1, shards):
            source = all_ref.at[
                lax.rem(place_ref[0] + shards - back, shards), pl.ds(first, rows), pl.ds(0, columns)
            ]
            pairs.append((source, out_ref.at[back - 1]))
    run_copies(pairs, sems)


def others(place, whole, cuts, after=()):
    shards = whole.shape[0]
    return copy_call(
        lambda *refs: others_kernel(cuts, *refs), "others", place, [whole],
        [(shards - 1, rows, columns) for _, rows, columns in cuts], len(cuts) * (shards - 1), after,
    )


def copy_call(kernel, name, place, operands, shapes, count, after=(), keep=False):
    kind = operands[0].dtype
    return pl.pallas_call(
        kernel,
        out_shape=tuple(
            pltpu.VMEM(shape, kind) if keep else jax.ShapeDtypeStruct(shape, kind) for shape in shapes
        ),
        in_specs=[pl.BlockSpec(memory_space=pltpu.SMEM)]
        + [pl.BlockSpec(memory_space=pl.ANY)] * len(operands)
        + [pl.BlockSpec(memory_space=pl.ANY)] * len(after),
        out_specs=(pl.BlockSpec(memory_space=pltpu.VMEM),) * len(shapes),
        scratch_shapes=[pltpu.SemaphoreType.DMA((count,))],
        compiler_params=pltpu.CompilerParams(vmem_limit_bytes=COPY_BYTES),
        cost_estimate=COPIES,
        name=name,
    )(place, *operands, *after)


def join_attn_kernel(sizes, layer, place_ref, qkv_ref, *refs):
    pieces, whole_ref, sems = refs[:4], refs[-2], refs[-1]
    rows_in, shards = sizes[0], sizes[-1]
    shard, quarter = place_ref[0], place_ref[1]
    pairs = attn_pairs(sizes, layer, slice(None), place_ref[2], qkv_ref, whole_ref.at[shard])
    for relative, piece_ref in enumerate(pieces):
        rows = pl.ds(pl.multiple_of((quarter ^ relative) * rows_in, 16), rows_in)
        for back in range(1, shards):
            target = whole_ref.at[lax.rem(shard + shards - back, shards), rows]
            pairs.append((piece_ref.at[back - 1], target))
    run_copies(pairs, sems)


def join_mlp_kernel(sizes, layer, place_ref, out_ref, hidden_ref, down_ref, *refs):
    pieces = refs[:4]
    whole_o_ref, whole_h_ref, whole_d_ref, sems = refs[-4:]
    rows_in, rows_down, half, hidden_cut, shards = sizes
    shard, quarter, core = place_ref[0], place_ref[1], place_ref[2]
    pairs = hidden_pairs(sizes, layer, slice(None), core, hidden_ref, whole_h_ref.at[shard])
    first = pl.multiple_of(core * hidden_cut, 128)
    pairs.append((down_ref.at[layer, pl.ds(first, hidden_cut)], whole_d_ref.at[shard]))
    pairs.append((out_ref.at[layer], whole_o_ref.at[shard]))
    for relative in range(4):
        at_h = pl.multiple_of((quarter ^ relative) * rows_in, 16)
        at_d = pl.multiple_of((quarter ^ relative) * rows_down, 16)
        for back in range(1, shards):
            place = lax.rem(shard + shards - back, shards)
            above = pieces[relative].at[back - 1, pl.ds(0, rows_in)]
            below = pieces[relative].at[back - 1, pl.ds(rows_in, rows_in)]
            pairs.append(
                (above.at[:, pl.ds(0, 4 * half)], whole_h_ref.at[place, pl.ds(at_h, rows_in)])
            )
            for number, part in enumerate((above, below)):
                pairs.append(
                    (
                        below.at[:, pl.ds(number * 2 * half, 2 * half)],
                        whole_d_ref.at[place, pl.ds(at_d + number * rows_in, rows_in)],
                    )
                )
                pairs.append(
                    (
                        part.at[:, pl.ds(4 * half, half)],
                        whole_o_ref.at[place, pl.ds(at_h, rows_in), pl.ds(number * half, half)],
                    )
                )
    run_copies(pairs, sems)


def finish_attn_part(owner, half, rows, piece, qkv_ref, out_ref):
    width = 2 * half
    lanes = pl.multiple_of(owner * half, 128)
    for kind in range(3):
        qkv_ref[0, :, pl.ds(kind * width + lanes, half)] = wide(
            piece[0, :rows, kind * half : (kind + 1) * half]
        )
    out_ref[0, :, pl.ds(lanes, half)] = wide(piece[0, :rows, 3 * half :])


def finish_mlp_part(owner, half, rows, shards, start, piece, hidden_ref, down_ref):
    width = 2 * half
    hidden_cut = hidden_ref.shape[2] // (2 * shards)
    lanes = pl.multiple_of(owner * hidden_cut, 128)
    for at in range(shards):
        hidden_ref[0, :, pl.ds(at * 2 * hidden_cut + lanes, hidden_cut)] = wide(
            piece[0, start : start + rows, at * hidden_cut : (at + 1) * hidden_cut]
        )
    for side in range(2):
        down_ref[0, owner, 0, side * rows : (side + 1) * rows] = wide(
            piece[0, start + rows :, side * width : (side + 1) * width]
        )


def finish_kernel(parts, half, rows, shards, place_ref, *refs):
    outs = refs[len(refs) - 2 * len(parts) :]
    for relative in range(2):
        owner, at = place_ref[2] ^ relative, 0
        for number, part in enumerate(parts):
            if part == "attn":
                finish_attn_part(owner, half, rows, refs[relative], *outs[2 * number : 2 * number + 2])
                at += rows
            else:
                finish_mlp_part(
                    owner, half, rows, shards, at, refs[relative], *outs[2 * number : 2 * number + 2]
                )


def finish(place, layer, parts, pieces, shapes, half, rows, shards, before=None):
    width = 2 * half
    blocks = {
        "attn": [
            pl.BlockSpec((1, rows, 3 * width), lambda at, place: (layer, place[1] ^ at, 0)),
            pl.BlockSpec((1, rows, width), lambda at, place: (layer, place[1] ^ at, 0)),
        ],
        "mlp": [
            pl.BlockSpec((1, rows, shapes["mlp"][0][2]), lambda at, place: (layer, place[1] ^ at, 0)),
            pl.BlockSpec(
                (1, 2, 1, 2 * rows, width), lambda at, place: (layer, 0, place[1] ^ at, 0, 0)
            ),
        ],
    }
    operands, aliases = list(pieces), {}
    specs = [pl.BlockSpec((1, *piece.shape[1:]), lambda at, place: (at, 0, 0)) for piece in pieces]
    if before is not None:
        operands += list(before)
        specs += [pl.BlockSpec(memory_space=pl.ANY)] * len(before)
        aliases = {3 + number: number for number in range(len(before))}
    return pl.pallas_call(
        lambda *refs: finish_kernel(parts, half, rows, shards, *refs),
        grid_spec=pltpu.PrefetchScalarGridSpec(
            num_scalar_prefetch=1,
            grid=(4,),
            in_specs=specs,
            out_specs=tuple(block for part in parts for block in blocks[part]),
        ),
        out_shape=tuple(
            jax.ShapeDtypeStruct(shape, jnp.float32) for part in parts for shape in shapes[part]
        ),
        input_output_aliases=aliases,
        compiler_params=pltpu.CompilerParams(vmem_limit_bytes=VMEM_BYTES),
        cost_estimate=COPIES,
        name="finish",
    )(place, *operands)


TILE = 256
SHIFT_ONE, SCALE_ONE, GATE_ONE, SHIFT_TWO, SCALE_TWO, GATE_TWO, GAIN_ONE, GAIN_TWO, BIAS_DOWN = range(9)


def row_of(ref, number):
    return ref[number : number + 1, :]


def norm_rows(values, vec_ref, gain, scale, shift):
    unit_values, _ = normalise(values)
    return low(
        unit_values * row_of(vec_ref, gain) * (1.0 + row_of(vec_ref, scale)) + row_of(vec_ref, shift)
    )


def enter_kernel(x_ref, vec_ref, n_ref):
    n_ref[...] = norm_rows(wide(x_ref[...]), vec_ref, GAIN_ONE, SCALE_ONE, SHIFT_ONE)


def project_kernel(first, last, own_ref, other_ref, weight_ref, out_ref, *refs):
    count = own_ref.shape[0]
    for chip_ref in refs:
        chip_ref[:count, :] = own_ref[...]
        chip_ref[count:, :] = other_ref[...]
    out_ref[:count, :] = low(plain_product(own_ref[...], weight_ref[:, first:last]))
    out_ref[count:, :] = low(plain_product(other_ref[...], weight_ref[:, first:last]))


def middle_kernel(
    place_ref, att_own_ref, att_other_ref, weight_ref, state_ref, vec_ref, branch_ref, middle_ref, n_ref, att_ref
):
    half = att_own_ref.shape[1]
    att_ref[:, pl.ds(pl.multiple_of(place_ref[2] * half, 128), half)] = att_own_ref[...]
    att_ref[:, pl.ds(pl.multiple_of((1 - place_ref[2]) * half, 128), half)] = att_other_ref[...]
    branch = plain_product(att_ref[...], weight_ref[...])
    middle = state_ref[...] + row_of(vec_ref, GATE_ONE) * branch
    branch_ref[...] = low(branch)
    middle_ref[...] = middle
    n_ref[...] = norm_rows(middle, vec_ref, GAIN_TWO, SCALE_TWO, SHIFT_TWO)


def chunk_call(kernel, name, grid, operands, specs, shapes, out_specs, scratch, after=(), far=()):
    first_out = len(operands)
    return pl.pallas_call(
        lambda *refs: kernel(*refs[:first_out], *refs[first_out + len(after) :]),
        grid=(grid,),
        out_shape=tuple(
            pltpu.HBM(shape, kind) if number in far else jax.ShapeDtypeStruct(shape, kind)
            for number, (shape, kind) in enumerate(shapes)
        ),
        in_specs=list(specs) + [pl.BlockSpec(memory_space=pl.ANY)] * len(after),
        out_specs=tuple(out_specs),
        scratch_shapes=scratch,
        compiler_params=pltpu.CompilerParams(vmem_limit_bytes=VMEM_BYTES),
        cost_estimate=FREE,
        name=name,
    )(*operands, *after)


def sent_and_kept(total_ref, part_ref, send_ref):
    @pl.when(pl.program_id(0) == pl.num_programs(0) - 1)
    def _():
        count = part_ref.shape[0]
        part_ref[...] = total_ref[:count, :]
        send_ref[...] = low(total_ref[count:, :])


def take_both(own_ref, other_ref, chip_ref):
    @pl.when(pl.program_id(0) == 0)
    def _():
        count = own_ref.shape[0]
        chip_ref[:count, :] = own_ref[...]
        chip_ref[count:, :] = other_ref[...]


def add_up(total_ref, term):
    @pl.when(pl.program_id(0) == 0)
    def _():
        total_ref[...] = term

    @pl.when(pl.program_id(0) > 0)
    def _():
        total_ref[...] += term


def mlp_kernel(
    own_ref, other_ref, hidden_ref, down_ref, bias_ref, act_ref, slope_ref, part_ref, send_ref, chip_ref, total_ref
):
    take_both(own_ref, other_ref, chip_ref)
    pre = plain_product(chip_ref[...], hidden_ref[...]) + bias_ref[...]
    square = pre * pre
    factor = math.sqrt(2.0 / math.pi)
    bent = jnp.tanh(pre * (factor + (factor * 0.044715) * square))
    near_half = 0.5 + 0.5 * bent
    act = low(pre * near_half)
    act_ref[...] = act
    slope_ref[...] = low(
        near_half
        + (0.5 * pre) * (1.0 - bent * bent) * (factor + (3.0 * factor * 0.044715) * square)
    )
    add_up(total_ref, plain_product(act, down_ref[...]))
    sent_and_kept(total_ref, part_ref, send_ref)


def run_mlp(own, other, hiddens, downs, bias, after):
    count, width = own.shape
    cuts = hiddens.shape[1]
    size = 384
    fixed = lambda rows, columns: pl.BlockSpec((rows, columns), lambda at: (0, 0))
    across = lambda rows: pl.BlockSpec((rows, size), lambda at: (0, at))
    return chunk_call(
        mlp_kernel, "mlp", cuts // size,
        [own, other, hiddens, downs, bias],
        [
            fixed(count, width), fixed(count, width), across(width),
            pl.BlockSpec((size, width), lambda at: (at, 0)), across(1),
        ],
        [
            ((2 * count, cuts), jnp.bfloat16), ((2 * count, cuts), jnp.bfloat16),
            ((count, width), jnp.float32), ((count, width), jnp.bfloat16), ((2 * count, width), jnp.bfloat16),
        ],
        [across(2 * count), across(2 * count), fixed(count, width), fixed(count, width), fixed(2 * count, width)],
        [pltpu.VMEM((2 * count, width), jnp.float32)],
        after,
        (0, 1),
    )


def leave_kernel(last, part_ref, arrived_ref, middle_ref, vec_ref, *refs):
    branch = part_ref[...] + wide(arrived_ref[...]) + row_of(vec_ref, BIAS_DOWN)
    state = middle_ref[...] + row_of(vec_ref, GATE_TWO) * branch
    if last:
        branch_ref, out_ref = refs
        out_ref[...] = low(state)
    else:
        next_vec_ref, branch_ref, state_ref, n_ref = refs
        state_ref[...] = state
        n_ref[...] = norm_rows(state, next_vec_ref, GAIN_ONE, SCALE_ONE, SHIFT_ONE)
    branch_ref[...] = low(branch)


def start_back(grad, branch_ref, vec_ref, d_branch_ref, sums_ref, first):
    d_branch = low(row_of(vec_ref, GATE_TWO) * grad)
    d_branch_ref[...] = d_branch
    sums_ref[first : first + 1, :] = jnp.sum(grad * wide(branch_ref[...]), axis=0, keepdims=True)
    sums_ref[first + 1 : first + 2, :] = jnp.sum(wide(d_branch), axis=0, keepdims=True)


def top_kernel(masked_ref, vec_ref, grad_ref, d_branch_ref):
    grad = wide(masked_ref[...])
    grad_ref[...] = grad
    d_branch_ref[...] = low(row_of(vec_ref, GATE_TWO) * grad)


def top_sums_kernel(grad_ref, d_branch_ref, branch_ref, sums_ref):
    sums_ref[0:1, :] = jnp.sum(grad_ref[...] * wide(branch_ref[...]), axis=0, keepdims=True)
    sums_ref[1:2, :] = jnp.sum(wide(d_branch_ref[...]), axis=0, keepdims=True)


def mlp_back_kernel(
    own_ref, other_ref, slope_ref, hidden_ref, down_ref, d_pre_ref, part_ref, send_ref, bias_ref, chip_ref, total_ref
):
    take_both(own_ref, other_ref, chip_ref)
    d_pre = low(right_product(chip_ref[...], down_ref[...]) * wide(slope_ref[...]))
    d_pre_ref[...] = d_pre
    bias_ref[...] = jnp.sum(wide(d_pre), axis=0, keepdims=True)
    add_up(total_ref, right_product(d_pre, hidden_ref[...]))
    sent_and_kept(total_ref, part_ref, send_ref)


def run_mlp_back(own, other, slope, hiddens, downs, after):
    count, width = own.shape
    cuts = hiddens.shape[1]
    size = 384
    fixed = lambda rows, columns: pl.BlockSpec((rows, columns), lambda at: (0, 0))
    across = lambda rows: pl.BlockSpec((rows, size), lambda at: (0, at))
    return chunk_call(
        mlp_back_kernel, "mlp_back", cuts // size,
        [own, other, pltpu.with_memory_space_constraint(slope, pltpu.HBM), hiddens, downs],
        [
            fixed(count, width), fixed(count, width), across(2 * count), across(width),
            pl.BlockSpec((size, width), lambda at: (at, 0)),
        ],
        [
            ((2 * count, cuts), jnp.bfloat16), ((count, width), jnp.float32), ((count, width), jnp.bfloat16),
            ((1, cuts), jnp.float32), ((2 * count, width), jnp.bfloat16),
        ],
        [across(2 * count), fixed(count, width), fixed(count, width), across(1), fixed(2 * count, width)],
        [pltpu.VMEM((2 * count, width), jnp.float32)],
        after,
    )


def norm_back(d_normed, values, gain, scale, shift_sum_ref):
    unit_values, inverse = normalise(values)
    first = jnp.sum(d_normed, axis=0, keepdims=True)
    second = jnp.sum(d_normed * unit_values, axis=0, keepdims=True)
    shift_sum_ref[0:1, :] = first
    shift_sum_ref[1:2, :] = gain * second
    shift_sum_ref[2:3, :] = (1.0 + scale) * second
    scaled = d_normed * ((1.0 + scale) * gain)
    inner = jnp.mean(scaled * unit_values, axis=-1, keepdims=True)
    return (scaled - jnp.mean(scaled, axis=-1, keepdims=True) - unit_values * inner) * inverse


def middle_back_kernel(
    place_ref, grad_ref, part_ref, arrived_ref, middle_ref, branch_ref, vec_ref, weight_ref,
    d_middle_ref, d_branch_ref, att_own_ref, att_other_ref, sums_ref, d_att_ref,
):
    half = att_own_ref.shape[1]
    d_normed = part_ref[...] + wide(arrived_ref[...])
    d_middle = grad_ref[...] + norm_back(
        d_normed, middle_ref[...], row_of(vec_ref, GAIN_TWO), row_of(vec_ref, SCALE_TWO), sums_ref
    )
    d_middle_ref[...] = d_middle
    sums_ref[3:4, :] = jnp.sum(d_middle * wide(branch_ref[...]), axis=0, keepdims=True)
    d_branch_ref[...] = low(row_of(vec_ref, GATE_ONE) * d_middle)
    d_att_ref[...] = low(right_product(d_branch_ref[...], weight_ref[...]))
    att_own_ref[...] = d_att_ref[:, pl.ds(pl.multiple_of(place_ref[2] * half, 128), half)]
    att_other_ref[...] = d_att_ref[:, pl.ds(pl.multiple_of((1 - place_ref[2]) * half, 128), half)]


def project_back_kernel(d_qkv_ref, weight_ref, part_ref, send_ref):
    count = part_ref.shape[0]
    columns = d_qkv_ref.shape[1]
    part_ref[...] = right_product(d_qkv_ref[:count, :], weight_ref[:, :columns])
    send_ref[...] = low(right_product(d_qkv_ref[count:, :], weight_ref[:, :columns]))


def enter_back_kernel(last, d_middle_ref, part_ref, arrived_ref, state_ref, vec_ref, *refs):
    d_normed = part_ref[...] + wide(arrived_ref[...])
    if last:
        sums_ref, out_ref = refs
    else:
        branch_ref, next_vec_ref, sums_ref, grad_ref, d_branch_ref = refs
    grad = d_middle_ref[...] + norm_back(
        d_normed, wide(state_ref[...]), row_of(vec_ref, GAIN_ONE), row_of(vec_ref, SCALE_ONE), sums_ref
    )
    if last:
        out_ref[...] = low(grad)
    else:
        grad_ref[...] = grad
        start_back(grad, branch_ref, next_vec_ref, d_branch_ref, sums_ref, 3)


def attend_kernel(seg_q_ref, seg_k_ref, q_ref, kl_ref, vl_ref, kf_ref, vf_ref, *refs):
    own_ref, other_ref, lse_ref = refs[-3:]
    count = kl_ref.shape[0]
    TILE = count // 2
    low_half = lax.broadcasted_iota(jnp.int32, (count, 128), 1) < 64
    for start in range(0, q_ref.shape[0], TILE):
        rows = pl.ds(start, TILE)
        seg_q = seg_q_ref[rows, :]
        allow_l = seg_q == seg_k_ref[:, :count]
        allow_f = seg_q == seg_k_ref[:, count:]
        query = q_ref[rows, :]
        query = query * jnp.asarray(0.125, query.dtype)
        outs, lses = [], []
        for head in range(2):
            half = low_half if head == 0 else jnp.logical_not(low_half)
            q_h = jnp.where(half[:TILE], query, jnp.zeros_like(query))
            s_l = jnp.where(allow_l, right_product(q_h, kl_ref[...]), neg_big)
            s_f = jnp.where(allow_f, right_product(q_h, kf_ref[...]), neg_big)
            top = jnp.maximum(
                jnp.max(s_l, axis=1, keepdims=True), jnp.max(s_f, axis=1, keepdims=True)
            )
            p_l = jnp.exp(s_l - top).astype(jnp.bfloat16)
            p_f = jnp.exp(s_f - top).astype(jnp.bfloat16)
            one = jnp.ones((count, 128), jnp.bfloat16)
            summed = plain_product(p_l, jnp.where(half, vl_ref[...], one)) + plain_product(
                p_f, jnp.where(half, vf_ref[...], one)
            )
            total = pltpu.roll(summed, 64, 1)
            outs.append(summed / total)
            lses.append(top + jnp.log(total))
        result = jnp.where(low_half[:TILE], outs[0], outs[1])
        (own_ref if start == 0 else other_ref)[...] = result.astype(jnp.bfloat16)
        lse_ref[rows, :] = jnp.where(low_half[:TILE], lses[0], lses[1])


def attend(query, near, far, seg_q, seg_k, after):
    count, half = query.shape
    pairs = half // 128
    block = lambda off: pl.BlockSpec((count, 128), lambda j: (0, off + j))
    part = pl.BlockSpec((count // 2, 128), lambda j: (0, j))
    return pl.pallas_call(
        attend_kernel,
        grid=(pairs,),
        out_shape=(
            jax.ShapeDtypeStruct((count // 2, half), jnp.bfloat16),
            jax.ShapeDtypeStruct((count // 2, half), jnp.bfloat16),
            pltpu.HBM((count, half), jnp.float32),
        ),
        in_specs=[
            pl.BlockSpec((count, 1), lambda j: (0, 0)),
            pl.BlockSpec((1, 2 * count), lambda j: (0, 0)),
            block(0),
            block(0),
            block(pairs),
            block(0),
            block(pairs),
        ]
        + [pl.BlockSpec(memory_space=pl.ANY)] * len(after),
        out_specs=(part, part, block(0)),
        compiler_params=pltpu.CompilerParams(vmem_limit_bytes=VMEM_BYTES),
        cost_estimate=FREE,
        name="attend",
    )(seg_q, seg_k, query, near, near, far, far, *after)


def back_kernel(has_more, seg_q_ref, seg_k_ref, q_ref, k_ref, v_ref, do_own_ref, do_other_ref, o_own_ref, o_other_ref, lse_ref, *refs):
    count = k_ref.shape[0]
    TILE = count // 2
    low_half = lax.broadcasted_iota(jnp.int32, (TILE, 128), 1) < 64
    q_turned = (q_ref[...].astype(jnp.float32) * 0.125).T.astype(jnp.bfloat16)
    do_turned = [ref[...].astype(jnp.float32).T.astype(jnp.bfloat16) for ref in (do_own_ref, do_other_ref)]
    d_keys, d_values, d_queries = [0.0, 0.0], [0.0, 0.0], []
    for start in range(0, q_ref.shape[0], TILE):
        rows = pl.ds(start, TILE)
        allow = seg_q_ref[rows, :] == seg_k_ref[...]
        query = q_ref[rows, :]
        query = query * jnp.asarray(0.125, query.dtype)
        d_out = (do_own_ref if start == 0 else do_other_ref)[...]
        product = wide(d_out) * wide((o_own_ref if start == 0 else o_other_ref)[...])
        d_query = []
        for head in range(2):
            half = low_half if head == 0 else jnp.logical_not(low_half)
            lanes = slice(64 * head, 64 * head + 64)
            q_h = jnp.where(half, query, jnp.zeros_like(query))
            do_h = jnp.where(half, d_out, jnp.zeros_like(d_out))
            scores = jnp.where(allow, right_product(q_h, k_ref[...]), neg_big)
            probs = jnp.exp(scores - lse_ref[rows, 64 * head : 64 * head + 1])
            d_probs = right_product(do_h, v_ref[...])
            delta = jnp.sum(jnp.where(half, product, 0.0), axis=1, keepdims=True)
            d_scores = (probs * (d_probs - delta)).astype(jnp.bfloat16)
            d_values[head] += plain_product(
                do_turned[start // TILE][lanes], probs.astype(jnp.bfloat16)
            )
            d_keys[head] += plain_product(q_turned[lanes, start : start + TILE], d_scores)
            d_query.append(plain_product(d_scores, k_ref[...]))
        d_queries.append(jnp.where(low_half, d_query[0], d_query[1]) * 0.125)
    d_key = jnp.concatenate(d_keys, axis=0).T
    d_value = jnp.concatenate(d_values, axis=0).T
    d_query = jnp.concatenate(d_queries, axis=0)
    if has_more:
        dq_more_ref, dk_more_ref, dv_more_ref, out_ref = refs
        half = out_ref.shape[1] // 3
        at = pl.multiple_of(pl.program_id(0) * 128, 128)
        out_ref[:, pl.ds(at, 128)] = (d_query + dq_more_ref[...]).astype(jnp.bfloat16)
        out_ref[:, pl.ds(half + at, 128)] = (d_key + dk_more_ref[...].astype(jnp.float32)).astype(
            jnp.bfloat16
        )
        out_ref[:, pl.ds(2 * half + at, 128)] = (
            d_value + dv_more_ref[...].astype(jnp.float32)
        ).astype(jnp.bfloat16)
    else:
        dq_ref, out_ref = refs
        half = out_ref.shape[1] // 2
        at = pl.multiple_of(pl.program_id(0) * 128, 128)
        dq_ref[...] = d_query
        out_ref[:, pl.ds(at, 128)] = d_key.astype(jnp.bfloat16)
        out_ref[:, pl.ds(half + at, 128)] = d_value.astype(jnp.bfloat16)


def attend_back(query, keys, seg_q, seg_k, d_outs, out, lse, more=None, after=()):
    count, half = query.shape
    pairs = half // 128
    block = lambda off: pl.BlockSpec((count, 128), lambda j: (0, off + j))
    part = pl.BlockSpec((count // 2, 128), lambda j: (0, j))
    whole = lambda width: pl.BlockSpec((count, width), lambda j: (0, 0))
    operands = [seg_q, seg_k, query, keys, keys, *d_outs, *out]
    operands.append(pltpu.with_memory_space_constraint(lse, pltpu.HBM))
    specs = [
        pl.BlockSpec((count, 1), lambda j: (0, 0)),
        pl.BlockSpec((1, count), lambda j: (0, 0)),
        block(0),
        block(0),
        block(pairs),
        part,
        part,
        part,
        part,
        block(0),
    ]
    if more is None:
        out_shape = (
            jax.ShapeDtypeStruct((count, half), jnp.float32),
            jax.ShapeDtypeStruct((count, 2 * half), jnp.bfloat16),
        )
        out_specs = (block(0), whole(2 * half))
    else:
        operands += [more[0], more[1], more[1]]
        specs += [block(0), block(0), block(pairs)]
        out_shape = jax.ShapeDtypeStruct((count, 3 * half), jnp.bfloat16)
        out_specs = whole(3 * half)
    first_out = len(operands)
    operands += after
    specs += [pl.BlockSpec(memory_space=pl.ANY)] * len(after)
    return pl.pallas_call(
        lambda *refs: back_kernel(more is not None, *refs[:first_out], *refs[first_out + len(after) :]),
        grid=(pairs,),
        out_shape=out_shape,
        in_specs=specs,
        out_specs=out_specs,
        compiler_params=pltpu.CompilerParams(vmem_limit_bytes=VMEM_BYTES),
        cost_estimate=FREE,
        name="attend_back",
    )(*operands)


def local_paired(
    tokens,
    cotangent,
    segments,
    noised,
    levels,
    ada_weight,
    ada_bias,
    first_gain,
    qkv_weight,
    out_weight,
    second_gain,
    hidden_weight,
    hidden_bias,
    down_weight,
    down_bias,
):
    layers, ada_part, cond_width = ada_weight.shape
    part = first_gain.shape[1]
    hidden_part = hidden_bias.shape[1]
    width = tokens.shape[2]
    shards = width // part
    hidden = hidden_part * shards
    half = width // 2
    rows_in = part // 4
    rows_down = hidden_part // 8
    hidden_cut = hidden_part // 2
    blk = lax.axis_index("blk")
    uly = lax.axis_index("uly")
    core = uly // 2
    side = uly % 2
    quarter = blk * 2 + side
    shard = lax.axis_index("dp")
    row = shard * 2 + blk
    place = jnp.stack([shard, quarter, core]).astype(jnp.int32)

    def exchange(two_rows):
        return jnp.concatenate(
            [pick(two_rows, blk, 0), swap_blk(pick(two_rows, 1 - blk, 0))], axis=0
        )

    sizes = (rows_in, rows_down, half, hidden_cut, shards)
    qkv_weight, out_weight, hidden_weight, down_weight = (
        pltpu.with_memory_space_constraint(weight, pltpu.HBM)
        for weight in (qkv_weight, out_weight, hidden_weight, down_weight)
    )
    columns = 4 * half
    attn_columns = 3 * half
    mlp_columns = 5 * half

    def spread(own, last):
        near, far = swap_half(own), swap_blk(own)
        return (own, near, far, swap_blk(near) if last == "blk" else swap_half(far))

    def cut_attn(index, after):
        return copy_call(
            lambda *refs: cut_attn_kernel(sizes, index, *refs), "cut_attn", place,
            [qkv_weight], [(rows_in, attn_columns)], 3, after,
        )[0]

    def cut_mlp(index, after):
        return copy_call(
            lambda *refs: cut_mlp_kernel(sizes, index, *refs), "cut_mlp", place,
            [out_weight, hidden_weight, down_weight], [(2 * rows_in, mlp_columns)], shards + 4, after,
        )[0]

    def cut_next(index, after):
        return copy_call(
            lambda *refs: cut_next_kernel(sizes, index, *refs), "cut_next", place,
            [qkv_weight, out_weight, hidden_weight, down_weight],
            [(3 * rows_in, mlp_columns)], shards + 7, after,
        )[0]

    def whole_attn(index, spread):
        joined = copy_call(
            lambda *refs: join_attn_kernel(sizes, index, *refs), "join_attn", place,
            [qkv_weight, *spread], [(shards, part, attn_columns)], 3 + 4 * (shards - 1), (), True,
        )[0]
        return joined.reshape(width, attn_columns)

    def whole_mlp(index, spread):
        outs, hiddens, downs = copy_call(
            lambda *refs: join_mlp_kernel(sizes, index, *refs), "join_mlp", place,
            [out_weight, hidden_weight, down_weight, *spread],
            [(shards, part, width), (shards, part, columns), (shards, hidden_cut, width)],
            shards + 2 + 20 * (shards - 1), (), True,
        )
        return (
            outs.reshape(width, width), hiddens.reshape(width, columns),
            downs.reshape(shards * hidden_cut, width),
        )

    start = exchange(tokens)
    segs_two = exchange(segments)
    seg_chip = jnp.concatenate([segs_two, swap_core(segs_two)])
    seg_far = swap_half(seg_chip)
    def every_shard_of(piece):
        return lax.all_gather(piece, "dp", axis=0, tiled=False)

    def others_of(piece):
        return jnp.stack([from_shard(piece, back, shards) for back in range(1, shards)])

    def every_shard(vector):
        table = jnp.stack([vector] + [from_shard(vector, back, shards) for back in range(1, shards)])
        return jnp.stack([pick(table, (shard + shards - at) % shards, 0) for at in range(shards)])

    all_levels = every_shard(levels)
    attn_piece = cut_attn(0, [])
    attn_own = others_of(attn_piece)
    attn = spread(attn_own, "half")
    mlp_piece = cut_mlp(0, [attn_own])
    mlp_whole = every_shard_of(mlp_piece)
    next_whole = [every_shard_of(cut_next(index, [mlp_piece])) for index in range(1, layers)]

    all_levels = all_levels.reshape(-1)
    conds = low(cond_vector(all_levels, cond_width))
    part_mods = jnp.stack(
        [right_product(conds, ada_weight[index]) + wide(ada_bias[index]) for index in range(layers)],
        axis=1,
    )
    own_vectors = wide(
        jnp.concatenate([first_gain, second_gain, down_bias, hidden_bias], axis=1)
    )

    def shared_for(target):
        return jnp.concatenate([pick(part_mods, target * 2 + blk, 0), own_vectors], axis=1)

    shared = [shared_for(shard)]
    for ahead in range(1, shards):
        shared.append(from_shard(shared_for((shard + ahead) % shards), ahead, shards))
    shared = jnp.stack(shared)
    shared = jnp.stack([pick(shared, (shard + shards - at) % shards, 0) for at in range(shards)])
    vectors = []
    for index in range(layers):
        table = shared[:, index]
        ends = [ada_part + number * part for number in range(4)]
        rows = [table[:, :ada_part].reshape(6, width)]
        rows += [table[:, first : first + part].reshape(1, width) for first in ends[:3]]
        bias_hidden = table[:, ends[3] :].reshape(shards, 2, hidden_cut)
        vectors.append(
            (jnp.concatenate(rows, axis=0), pick(bias_hidden, core, 1).reshape(1, shards * hidden_cut))
        )

    seg_q = seg_chip[:, None]
    seg_near_k, seg_far_k = seg_chip[None, :], seg_far[None, :]
    seg_k = jnp.concatenate([seg_near_k, seg_far_k], axis=1)

    def spread_late(own, after):
        near, far = swap_half(own), hold(swap_blk(own), after)
        return (own, near, far, swap_half(far))

    tokens_here = start.shape[0]
    rows_f32 = ((tokens_here, width), jnp.float32)
    rows_low = ((tokens_here, width), jnp.bfloat16)
    half_low = ((tokens_here, half), jnp.bfloat16)
    chip_low = ((2 * tokens_here, width), jnp.bfloat16)
    cut_wide = shards * hidden_cut
    state = wide(start)
    normed = whole_call(
        enter_kernel, "enter", [rows_low], [start, vectors[0][0]], None, [seg_far]
    )[0]
    masked = exchange(cotangent * low(noised)[..., None])
    grad, d_branch_two = whole_call(top_kernel, "top", [rows_f32, rows_low], [masked, vectors[-1][0]])
    d_branch_other = swap_core(d_branch_two)
    kept, gathered = [], []
    for index in range(layers):
        vec, bias_core = vectors[index]
        joined = whole_attn(index, attn)
        normed_other = swap_core(normed)
        near, normed_chip = whole_call(
            lambda *refs: project_kernel(half, 3 * half, *refs), "keys_values",
            [((2 * tokens_here, 2 * half), jnp.bfloat16), chip_low], [normed, normed_other, joined],
        )
        far = swap_half(near)
        query = whole_call(
            lambda *refs: project_kernel(0, half, *refs), "queries",
            [((2 * tokens_here, half), jnp.bfloat16)], [normed, normed_other, joined], None, [near],
        )[0]
        att_own, att_send, lse = attend(query, near, far, seg_q, seg_k, ())
        att_other = swap_core(att_send)
        if index == 0:
            mlp_own = others(place, mlp_whole, [(0, 2 * rows_in, mlp_columns)], [query])[0]
        mlp = spread_late(mlp_own, att_other)
        out_whole, hiddens, downs = whole_mlp(index, mlp)
        gathered.append((hiddens, downs))
        branch_one, middle, normed_two, attended = whole_call(
            middle_kernel, "middle", [rows_low, rows_f32, rows_low, rows_low],
            [att_own, att_other, out_whole, state, vec], place,
        )
        normed_two_other = swap_core(normed_two)
        after = [d_branch_other] if index == layers - 1 else []
        act, slope, part_own, part_send, normed_two_chip = run_mlp(
            normed_two, normed_two_other, hiddens, downs, bias_core, after
        )
        if index + 1 < layers:
            mlp_own, attn_own = others(
                place, next_whole[index],
                [(0, 2 * rows_in, mlp_columns), (2 * rows_in, rows_in, attn_columns)], [part_own],
            )
            attn = spread(attn_own, "half")
        ends = [part_own, swap_core(part_send), middle, vec]
        keep = [
            state, normed_chip, joined, out_whole, query, near, far, (att_own, att_send), lse, attended,
            branch_one, middle, normed_two_chip, act, slope,
        ]
        if index == layers - 1:
            branch_two, final = whole_call(
                lambda *refs: leave_kernel(True, *refs), "leave", [rows_low, rows_low], ends
            )
        else:
            branch_two, state, normed = whole_call(
                lambda *refs: leave_kernel(False, *refs), "leave", [rows_low, rows_f32, rows_low],
                ends + [vectors[index + 1][0]], None, (),
            )
        kept.append(keep + [branch_two])

    def give_back(rows):
        mine, other = rows[: rows.shape[0] // 2], rows[rows.shape[0] // 2 :]
        arrived = swap_blk(other)
        return jnp.where(blk == 0, jnp.stack([mine, arrived]), jnp.stack([arrived, mine]))

    output = give_back(final)

    def reduce_start(array, rows):
        terms = array.reshape(shards, 2, 2, rows, array.shape[1])
        first = swap_half(pick(terms, 1 - side, 2))
        kept_terms = low(wide(pick(terms, side, 2)) + wide(first))
        return pick(kept_terms, blk, 1), swap_blk(pick(kept_terms, 1 - blk, 1))

    def reduce_end(pair, *after):
        mine, arrived = pair
        return low(wide(mine) + wide(hold(arrived, *after) if after else arrived))

    def scatter_shards(array):
        return lax.psum_scatter(array, "dp", scatter_dimension=0, tiled=False)

    def sum_shards(array):
        arrived = [
            from_shard(pick(array, (shard + ahead) % shards, 0), ahead, shards)
            for ahead in range(1, shards)
        ]
        return low(wide(pick(array, shard, 0)) + sum(wide(item) for item in arrived)), arrived[0]

    sums_top = whole_call(
        top_sums_kernel, "top_sums", [((2, width), jnp.float32)], [grad, d_branch_two, kept[-1][-1]]
    )[0]
    def end_mlp_sums(pending, late):
        index, down_pair, hidden_pair, _, _ = pending
        down_sum, hidden_sum = (
            reduce_end(down_pair, *((late,) if pending[0] == 0 else ())),
            reduce_end(hidden_pair, *((late,) if pending[0] == 0 else ())),
        )
        down_sum = jnp.concatenate([down_sum[:, :rows_in], down_sum[:, rows_in:]], axis=2)
        return scatter_shards(jnp.concatenate([hidden_sum, down_sum], axis=1))

    def end_attn_sums(pending, late):
        index, _, _, attn_pair, out_sum = pending
        attn_sum = reduce_end(attn_pair, late) if index > 0 else reduce_end(attn_pair)
        attn_sum = jnp.concatenate([attn_sum, out_sum], axis=2)
        return (scatter_shards(attn_sum), None) if index > 0 else sum_shards(attn_sum)

    pending = None
    small = [None] * layers
    shards_out = [None] * layers
    due = [()] * 5
    for index in reversed(range(layers)):
        vec, _ = vectors[index]
        hiddens, downs = gathered[index]
        (
            state_in, normed_chip, joined, out_whole, query, near, far, heads_out, lse, attended,
            branch_one, middle, normed_two_chip, act, slope, _,
        ) = kept[index]
        if index < layers - 1:
            d_branch_other = swap_core(d_branch_two)
        d_pre, part_own, part_send, d_bias_core, d_branch_chip = run_mlp_back(
            d_branch_two, d_branch_other, slope, hiddens, downs, due[0]
        )
        if pending is not None:
            shards_out[pending[0]] = (None, end_mlp_sums(pending, d_pre))
        d_down = low(left_product(act, d_branch_chip))
        d_hidden = low(left_product(normed_two_chip, d_pre))
        down_pair, hidden_pair = reduce_start(d_down, rows_down), reduce_start(d_hidden, rows_in)
        d_middle, d_one, d_att_own, d_att_send, sums_middle, _ = whole_call(
            middle_back_kernel, "middle_back",
            [rows_f32, rows_low, half_low, half_low, ((4, width), jnp.float32), rows_low],
            [grad, part_own, swap_core(part_send), middle, branch_one, vec, out_whole], place, due[1],
        )
        d_heads = (d_att_own, swap_core(d_att_send))
        d_query_far, d_far = attend_back(
            query, far, seg_q, seg_far_k, d_heads, heads_out, lse, None, due[2],
        )
        if pending is not None:
            shards_out[pending[0]] = (end_attn_sums(pending, d_query_far)[0], shards_out[pending[0]][1])
        d_near = swap_half(d_far)
        out_sum = reduce_end(reduce_start(low(left_product(attended, d_one)), rows_in))
        out_sum = low(
            wide(lax.dynamic_slice_in_dim(out_sum, core * half, half, 2))
            + wide(swap_core(lax.dynamic_slice_in_dim(out_sum, (1 - core) * half, half, 2)))
        )
        d_qkv = attend_back(
            query, near, seg_q, seg_near_k, d_heads, heads_out, lse, (d_query_far, d_near),
            due[3],
        )
        d_qkv_core = low(left_product(normed_chip, d_qkv))
        attn_pair = reduce_start(d_qkv_core, rows_in)
        part_own, part_send = whole_call(
            project_back_kernel, "project_back", [rows_f32, rows_low], [d_qkv, joined], None, due[4]
        )
        ends = [d_middle, part_own, swap_core(part_send), state_in, vec]
        sums_next = None
        if index == 0:
            sums_in, last_grad = whole_call(
                lambda *refs: enter_back_kernel(True, *refs), "enter_back",
                [((3, width), jnp.float32), rows_low], ends,
            )
        else:
            sums_in, grad, d_branch_two = whole_call(
                lambda *refs: enter_back_kernel(False, *refs), "enter_back",
                [((5, width), jnp.float32), rows_f32, rows_low],
                ends + [kept[index - 1][-1], vectors[index - 1][0]], None,
                (),
            )
            sums_next = sums_in[3:]
        pending = (index, down_pair, hidden_pair, attn_pair, out_sum)
        d_units = d_bias_core.reshape(shards, 1, hidden_cut)
        d_units = jnp.concatenate(
            [jnp.where(core == 0, d_units, 0.0), jnp.where(core == 1, d_units, 0.0)], axis=1
        )
        d_modulation = jnp.concatenate(
            [sums_in[:2], sums_middle[3:4], sums_middle[:2], sums_top[:1]], axis=0
        )
        small[index] = jnp.concatenate(
            [
                d_modulation.reshape(shards, -1),
                sums_in[2].reshape(shards, -1),
                sums_middle[2].reshape(shards, -1),
                sums_top[1].reshape(shards, -1),
                d_units.reshape(shards, -1),
            ],
            axis=1,
        )
        sums_top = sums_next

    attn_arrived = pending[3][1]
    attn_shard, shard_arrived = end_attn_sums(pending, None)
    shards_out[0] = (attn_shard, end_mlp_sums(pending, last_grad))
    tokens_grad = give_back(last_grad)

    vector = hold(jnp.stack(small), token(attn_arrived))
    vector = vector + swap_core(vector)
    vector = vector + swap_half(vector)
    parts = vector.transpose(1, 0, 2)
    arrived = [pick(parts, shard, 0)]
    for ahead in range(1, shards):
        arrived.append(from_shard(pick(parts, (shard + ahead) % shards, 0), ahead, shards))
    arrived = jnp.stack(arrived)
    other = swap_blk(arrived)
    totals = jnp.sum(arrived + other, axis=0)
    cond_rows = wide(conds).reshape(shards, 2, cond_width)
    cond_rows = jnp.stack([pick(cond_rows, (shard + shards - at) % shards, 0) for at in range(shards)])
    by_row = jnp.concatenate([arrived[:, :, :ada_part], other[:, :, :ada_part]], axis=0)
    cond_both = jnp.concatenate([pick(cond_rows, blk, 1), pick(cond_rows, 1 - blk, 1)], axis=0)
    grad_ada = jnp.einsum(
        "slm,sc->lmc", by_row, cond_both, precision=lax.Precision.HIGHEST
    )
    grad_ada_bias = totals[:, :ada_part]
    at = ada_part
    grad_gain_one = totals[:, at : at + part]
    grad_gain_two = totals[:, at + part : at + 2 * part]
    grad_bias_down = totals[:, at + 2 * part : at + 3 * part]
    grad_bias_hidden = totals[:, at + 3 * part :]

    def every_piece(piece, after):
        far, across = swap_blk(piece), swap_core(piece)
        cut = 4 * rows_in // 3
        last = jnp.concatenate([swap_blk(across[:cut]), swap_core(far[cut:])], axis=0)
        mine = jnp.stack([piece, far, across, last])
        other = swap_half(hold(mine, after) if after is not None else mine)
        return (
            jnp.stack([mine[0], other[0], mine[1], other[1]]),
            jnp.stack([mine[2], other[2], mine[3], other[3]]),
        )

    shapes = {
        "attn": [(layers, part, 3 * width), (layers, part, width)],
        "mlp": [(layers, part, hidden), (layers, 2, 4, rows_down, width)],
    }
    grads = None
    for index in reversed(range(layers)):
        piece = jnp.concatenate(shards_out[index], axis=0)
        if index > 0:
            pass
        grads = finish(
            place, index, ("attn", "mlp"), every_piece(piece, None), shapes, half, rows_in, shards, grads
        )
    grad_qkv, grad_out, grad_hidden, grad_down = grads
    grad_down = grad_down.reshape(layers, hidden_part, width)
    return (
        output,
        tokens_grad,
        grad_ada,
        grad_ada_bias,
        grad_gain_one,
        grad_qkv,
        grad_out,
        grad_gain_two,
        grad_hidden,
        grad_bias_hidden,
        grad_down,
        grad_bias_down,
    )


def pick_plan(mesh):
    def run(*arrays):
        tokens, first_gain, hidden_bias = arrays[0], arrays[7], arrays[12]
        fits = (
            mesh.shape["blk"] == 2
            and mesh.shape["uly"] == 4
            and tokens.shape[0] == 2
            and tokens.shape[1] % 64 == 0
            and tokens.shape[2] == HEADS * 64
            and HEADS % 4 == 0
            and first_gain.shape[1] % 64 == 0
            and hidden_bias.shape[1] % 256 == 0
        )
        return (local_paired if fits else local)(*arrays)

    return run


def solution(mesh):
    in_specs = (
        P("dp", ("blk", "uly"), None),
        P("dp", ("blk", "uly"), None),
        P("dp", ("blk", "uly")),
        P("dp", ("blk", "uly")),
        P("dp"),
        P(None, "dp", None),
        P(None, "dp"),
        P(None, "dp"),
        P(None, "dp", None),
        P(None, "dp", None),
        P(None, "dp"),
        P(None, "dp", None),
        P(None, "dp"),
        P(None, "dp", None),
        P(None, "dp"),
    )
    out_specs = (
        P("dp", ("blk", "uly"), None),
        P("dp", ("blk", "uly"), None),
        P(None, "dp", None),
        P(None, "dp"),
        P(None, "dp"),
        P(None, "dp", None),
        P(None, "dp", None),
        P(None, "dp"),
        P(None, "dp", None),
        P(None, "dp"),
        P(None, "dp", None),
        P(None, "dp"),
    )
    return jax.shard_map(pick_plan(mesh), mesh=mesh, in_specs=in_specs, out_specs=out_specs, check_vma=False)
```
